128 devices in a mesh: dp: 16 (over z_lo, y, core), seq: 8 (over x, z_hi).
Axes of the slice: x: 4, y: 4, z: 4 (z_hi: 2, z_lo: 2; z = z_hi * 2 + z_lo), core: 2. Of those that a mesh axis runs over, the one named last changes fastest.
Arguments:
- x_in: bfloat16 [32, 1024, 1024], P('dp', 'seq'), may hold values from -6 to 6
- scale_ids: int32 [32, 1024], P('dp', 'seq'), may hold values from 0 to 8, as said below
- pad_mask: int32 [32, 1024], P('dp', 'seq'), may hold values from 0 to 1, as said below
- loss_weights: int32 [32, 1024], P('dp', 'seq'), may hold values from 1 to 3
- targets: int32 [32, 1024], P('dp', 'seq'), may hold values from 0 to 4095
- labels: int32 [32], P('dp'), may hold values from 0 to 999
- cond_w: float32 [1024, 8192], P(None, 'dp'), may hold values from -0.1875 to 0.1875
- attn_w: float32 [1024, 4096], P(None, 'dp')
- mlp_w: float32 [2, 1024, 4096], P(None, None, 'dp'), may hold values from -0.1875 to 0.1875
- head_w: float32 [1024, 4096], P(None, 'dp')
- class_table: float32 [1000, 1024], P(None, 'dp'), may hold values from -6 to 6
- biases: float32 [20480], P('dp'), may hold values from -0.3 to 0.3
- first_cond: float32 [1024, 8192], P(None, 'dp'), may hold values from -1.1444092e-05 to 1.1444092e-05
- first_attn: float32 [1024, 4096], P(None, 'dp'), may hold values from -1.1444092e-05 to 1.1444092e-05
- first_mlp: float32 [2, 1024, 4096], P(None, None, 'dp'), may hold values from -1.1444092e-05 to 1.1444092e-05
- first_head: float32 [1024, 4096], P(None, 'dp'), may hold values from -1.1444092e-05 to 1.1444092e-05
- first_table: float32 [1000, 1024], P(None, 'dp'), may hold values from -1.1444092e-05 to 1.1444092e-05
- first_bias: float32 [20480], P('dp'), may hold values from -3.0517578e-05 to 3.0517578e-05
- second_cond: float32 [1024, 8192], P(None, 'dp'), may hold values from 3.818277e-12 to 1.5273107e-11
- second_attn: float32 [1024, 4096], P(None, 'dp'), may hold values from 3.818277e-12 to 1.5273107e-11
- second_mlp: float32 [2, 1024, 4096], P(None, None, 'dp'), may hold values from 3.818277e-12 to 1.5273107e-11
- second_head: float32 [1024, 4096], P(None, 'dp'), may hold values from 3.818277e-12 to 1.5273107e-11
- second_table: float32 [1000, 1024], P(None, 'dp'), may hold values from 3.818277e-12 to 1.5273107e-11
- second_bias: float32 [20480], P('dp'), may hold values from 3.436449e-11 to 1.3745796e-10
Outputs:
- updated_cond: float32 [1024, 8192], P(None, 'dp')
- updated_attn: float32 [1024, 4096], P(None, 'dp')
- updated_mlp: float32 [2, 1024, 4096], P(None, None, 'dp')
- updated_head: float32 [1024, 4096], P(None, 'dp')
- updated_table: float32 [1000, 1024], P(None, 'dp')
- updated_bias: float32 [20480], P('dp')
- moment_cond: float32 [1024, 8192], P(None, 'dp')
- moment_attn: float32 [1024, 4096], P(None, 'dp')
- moment_mlp: float32 [2, 1024, 4096], P(None, None, 'dp')
- moment_head: float32 [1024, 4096], P(None, 'dp')
- moment_table: float32 [1000, 1024], P(None, 'dp')
- moment_bias: float32 [20480], P('dp')
- square_cond: float32 [1024, 8192], P(None, 'dp')
- square_attn: float32 [1024, 4096], P(None, 'dp')
- square_mlp: float32 [2, 1024, 4096], P(None, None, 'dp')
- square_head: float32 [1024, 4096], P(None, 'dp')
- square_table: float32 [1000, 1024], P(None, 'dp')
- square_bias: float32 [20480], P('dp')
- copy_cond: bfloat16 [1024, 8192], P(None, 'dp')
- copy_attn: bfloat16 [1024, 4096], P(None, 'dp')
- copy_mlp: bfloat16 [2, 1024, 4096], P(None, None, 'dp')
- copy_head: bfloat16 [1024, 4096], P(None, 'dp')
- copy_table: bfloat16 [1000, 1024], P(None, 'dp')
- copy_bias: bfloat16 [20480], P('dp')
- grad_norm: float32 [], replicated
- loss_sum: float32 [], replicated
- true_count: float32 [], replicated
The draws below stay inside these ranges and needn't reach their ends.
Inputs may be any that keep to these rules, and one draw needn't show every extreme that they name: `scale_ids`: along each image the ids never fall; slot 0 of each image is real and has id 0. `pad_mask`: in each aligned block of 128 slots of an image the real slots come first, 64 of them or more; the last block of each image is full.
All inputs are finite; a program needn't handle non-finite values.
Results may differ from the reference program's by a relative error of at most 0.002.
The reference program's roundings to bfloat16 on the way count: a program that leaves them out, or rounds other values in their place, can miss the bound.
Values may be sent and summed in bfloat16 or wider, within the bound.
A program may use at most 320 MiB of HBM per device.

```python
import math
import jax
import jax.numpy as jnp
from jax import lax

D = 1024
FF = 4096
VOCAB = 4096
CLASSES = 1000
HEAD_DIM = 64
SEQ_SLOTS = 1024
STEP = 5
IMAGES = 32
N_SEQ = 8


def group_layout(key):
    fill_key, split_key, start_key, width_key, pick_key = jax.random.split(key, 5)
    slot_count = SEQ_SLOTS // N_SEQ
    filled = jax.random.randint(fill_key, (IMAGES, N_SEQ), slot_count // 2, slot_count + 1)
    filled = filled.at[:, N_SEQ - 1].set(slot_count)
    split_at = jax.random.randint(split_key, (IMAGES, N_SEQ), 1, slot_count)
    position = jnp.arange(slot_count)[None, None, :]
    group_index = jnp.arange(N_SEQ)[None, :, None]
    is_real = (position < filled[:, :, None]).astype(jnp.int32).reshape(IMAGES, SEQ_SLOTS)
    level = group_index + (position >= split_at[:, :, None]).astype(jnp.int32)
    span_start = jax.random.randint(start_key, (IMAGES,), 0, N_SEQ - 1)
    span_width = jax.random.randint(width_key, (IMAGES,), 1, N_SEQ)
    span_end = jnp.minimum(span_start + span_width, N_SEQ - 1)
    chosen = jax.random.randint(pick_key, (), 0, IMAGES)
    whole = jnp.arange(IMAGES) == chosen
    span_start = jnp.where(whole, 0, span_start)
    span_end = jnp.where(whole, N_SEQ, span_end)
    inside = (group_index >= span_start[:, None, None]) & (group_index < span_end[:, None, None])
    level = jnp.where(inside, span_start[:, None, None], level)
    scale_id = level.reshape(IMAGES, SEQ_SLOTS)
    return (scale_id.astype(jnp.int32), is_real)


def draw_scale_ids(key, part):
    shared = group_layout(key)
    return shared[0]


def draw_pad_mask(key, part):
    shared = group_layout(key)
    return shared[1]


def draw_attn_w(key, part):
    key = jax.random.fold_in(key, 3)
    noise = jax.random.normal(key, (D, 4 * D), jnp.float32)
    column = jnp.arange(4 * D)
    factor = jnp.where(column < 3 * D, D ** (-0.5), (SEQ_SLOTS / (3.0 * D)) ** 0.5)
    return noise * factor[None, :]


def draw_head_w(key, part):
    key = jax.random.fold_in(key, 4)
    noise = jax.random.normal(key, (D, VOCAB), jnp.float32)
    ramp = 3.0 ** (jnp.arange(VOCAB).astype(jnp.float32) / (VOCAB - 1))
    return noise * D ** (-0.5) * ramp[None, :]


def place_ends(drawn, rng, smallest, high):
    extent = drawn.shape
    index_at = [jax.random.randint(jax.random.fold_in(rng, axis), (), 0, extent[axis]) for axis in range(len(extent))]
    drawn = drawn.at[tuple(index_at)].set(smallest)
    longest = extent.index(max(extent))
    index_at[longest] = (index_at[longest] + 1) % extent[longest]
    return drawn.at[tuple(index_at)].set(high)


def block_levels(key, dims, cuts, smallest, largest):
    loudness, own = 1.0, jax.random.fold_in(key, 6)
    for dim, blocks in cuts:
        heights = jnp.exp(jax.random.uniform(jax.random.fold_in(own, dim), (blocks,), jnp.float32, smallest / len(cuts), largest / len(cuts)))
        loudness = loudness * jnp.repeat(heights, dims[dim] // blocks).reshape([-1 if axis == dim else 1 for axis in range(len(dims))])
    return loudness


def centred(own_key, extent, scale, limit, shards=(), kind=jnp.bfloat16):
    values = scale * jax.random.normal(own_key, extent, jnp.float32)
    if shards:
        values = values * block_levels(own_key, extent, shards, -0.22, 0.18)
    return jnp.clip(values, -limit, limit).astype(kind)


def setup_inputs(seed: int = 0) -> dict:
    seeds = jax.random.split(jax.random.key(seed), 25)
    return {
        "x_in": centred(seeds[0], (IMAGES, SEQ_SLOTS, D), 1.0, 6.0, ((0, 16), (1, 8))),
        "scale_ids": draw_scale_ids(jax.random.fold_in(seeds[24], 71), 0),
        "pad_mask": draw_pad_mask(jax.random.fold_in(seeds[24], 71), 0),
        "loss_weights": place_ends(jax.random.randint(seeds[3], (IMAGES, SEQ_SLOTS), 1, 4), jax.random.fold_in(seeds[3], 1), 1, 3).astype(jnp.int32),
        "targets": place_ends(jax.random.randint(seeds[4], (IMAGES, SEQ_SLOTS), 0, VOCAB), jax.random.fold_in(seeds[4], 1), 0, VOCAB - 1).astype(jnp.int32),
        "labels": place_ends(jax.random.randint(seeds[5], (IMAGES,), 0, CLASSES), jax.random.fold_in(seeds[5], 1), 0, CLASSES - 1).astype(jnp.int32),
        "cond_w": centred(seeds[6], (D, 8 * D), D ** -0.5, 0.1875, ((1, 16),), jnp.float32),
        "attn_w": draw_attn_w(jax.random.fold_in(seeds[24], 71), 0),
        "mlp_w": centred(seeds[8], (2, D, FF), D ** -0.5, 0.1875, ((2, 16),), jnp.float32),
        "head_w": draw_head_w(jax.random.fold_in(seeds[24], 71), 0),
        "class_table": centred(seeds[10], (CLASSES, D), 1.0, 6.0, ((1, 16),), jnp.float32),
        "biases": centred(seeds[11], (12 * D + FF + VOCAB,), 0.05, 0.3, ((0, 16),), jnp.float32),
        "first_cond": centred(seeds[12], (D, 8 * D), (0.01 / (12 * D * D + 2 * D * FF + D * VOCAB + CLASSES * D) ** 0.5), 1.1444091796875e-05, ((1, 16),), jnp.float32),
        "first_attn": centred(seeds[13], (D, 4 * D), (0.01 / (12 * D * D + 2 * D * FF + D * VOCAB + CLASSES * D) ** 0.5), 1.1444091796875e-05, ((1, 16),), jnp.float32),
        "first_mlp": centred(seeds[14], (2, D, FF), (0.01 / (12 * D * D + 2 * D * FF + D * VOCAB + CLASSES * D) ** 0.5), 1.1444091796875e-05, ((2, 16),), jnp.float32),
        "first_head": centred(seeds[15], (D, VOCAB), (0.01 / (12 * D * D + 2 * D * FF + D * VOCAB + CLASSES * D) ** 0.5), 1.1444091796875e-05, ((1, 16),), jnp.float32),
        "first_table": centred(seeds[16], (CLASSES, D), (0.01 / (12 * D * D + 2 * D * FF + D * VOCAB + CLASSES * D) ** 0.5), 1.1444091796875e-05, ((1, 16),), jnp.float32),
        "first_bias": centred(seeds[17], (12 * D + FF + VOCAB,), (0.03 / (12 * D * D + 2 * D * FF + D * VOCAB + CLASSES * D) ** 0.5), 3.0517578125e-05, ((0, 16),), jnp.float32),
        "second_cond": jnp.clip(jnp.exp(math.log(1.5273107431545974e-11) - 1.3862944 * jax.random.uniform(seeds[18], (D, 8 * D), jnp.float32) ** block_levels(seeds[18], (D, 8 * D), ((1, 16),), -0.2, 0.2)), 3.818276857886493e-12, 1.5273107431545974e-11),
        "second_attn": jnp.clip(jnp.exp(math.log(1.5273107431545974e-11) - 1.3862944 * jax.random.uniform(seeds[19], (D, 4 * D), jnp.float32) ** block_levels(seeds[19], (D, 4 * D), ((1, 16),), -0.2, 0.2)), 3.818276857886493e-12, 1.5273107431545974e-11),
        "second_mlp": jnp.clip(jnp.exp(math.log(1.5273107431545974e-11) - 1.3862944 * jax.random.uniform(seeds[20], (2, D, FF), jnp.float32) ** block_levels(seeds[20], (2, D, FF), ((2, 16),), -0.2, 0.2)), 3.818276857886493e-12, 1.5273107431545974e-11),
        "second_head": jnp.clip(jnp.exp(math.log(1.5273107431545974e-11) - 1.3862944 * jax.random.uniform(seeds[21], (D, VOCAB), jnp.float32) ** block_levels(seeds[21], (D, VOCAB), ((1, 16),), -0.2, 0.2)), 3.818276857886493e-12, 1.5273107431545974e-11),
        "second_table": jnp.clip(jnp.exp(math.log(1.5273107431545974e-11) - 1.3862944 * jax.random.uniform(seeds[22], (CLASSES, D), jnp.float32) ** block_levels(seeds[22], (CLASSES, D), ((1, 16),), -0.2, 0.2)), 3.818276857886493e-12, 1.5273107431545974e-11),
        "second_bias": jnp.clip(jnp.exp(math.log(1.3745796167974333e-10) - 1.3862944 * jax.random.uniform(seeds[23], (12 * D + FF + VOCAB,), jnp.float32) ** block_levels(seeds[23], (12 * D + FF + VOCAB,), ((0, 16),), -0.2, 0.2)), 3.4364490419935834e-11, 1.3745796167974333e-10),
    }


@jax.custom_vjp
def low(v):
    return lax.optimization_barrier(v.astype(jnp.bfloat16)).astype(jnp.float32)

@jax.custom_vjp
def low_back(v):
    return v

def low_keep(v):
    return (low(v), None)

def low_pass(kept, grad):
    return (grad,)

def back_keep(v):
    return (v, None)

def back_low(kept, grad):
    return (low(grad),)
low.defvjp(low_keep, low_pass)
low_back.defvjp(back_keep, back_low)
HIGH = lax.Precision.HIGHEST
NORM_EPS = 1e-06
CLIP = 0.01
LEARN = 0.02
DECAY = 0.1
BETA_ONE = 0.5
BETA_TWO = 0.5
ADAM_EPS = 1e-08
SCORE_SCALE = 0.125

def layer_norm(values):
    center = values - lax.optimization_barrier(jnp.mean(values, -1, keepdims=True))
    spread = lax.optimization_barrier(jnp.mean(center * center, -1, keepdims=True))
    return center * lax.rsqrt(spread + NORM_EPS)

def modulate(values, scale_row, shift_row):
    return layer_norm(values) * (1.0 + scale_row) + shift_row

def bias_parts(bias_all, model_width, hidden):
    offsets = [8 * model_width, 9 * model_width, 10 * model_width, 11 * model_width, 11 * model_width + hidden, 12 * model_width + hidden]
    return jnp.split(bias_all, offsets)

def image_loss(weights, image_row):
    attn_w, mlp_w, head_w, bias_q, bias_v, bias_proj, bias_fc1, bias_fc2, bias_head = weights
    tokens, scale_id, is_real, weight_tok, target, ada_row = image_row
    length, model_width = tokens.shape
    head_count = model_width // HEAD_DIM
    gate_attn, gate_mlp, scale_attn, scale_mlp, shift_attn, shift_mlp, scale_head, shift_head = jnp.split(ada_row, 8)
    normed = low(modulate(tokens, scale_attn, shift_attn))
    bias_qkv = jnp.concatenate([bias_q, jnp.zeros_like(bias_q), bias_v])
    qkv_all = low(low_back(jnp.dot(normed, attn_w[:, :3 * model_width], precision=HIGH) + bias_qkv))
    queries, key_rows, values = [section.reshape(length, head_count, HEAD_DIM) for section in jnp.split(qkv_all, 3, axis=1)]
    scores = low_back(jnp.einsum('qhd,khd->hqk', queries, key_rows, precision=HIGH) * SCORE_SCALE)
    visible = (is_real[None, :] > 0) & (scale_id[None, :] <= scale_id[:, None])
    prob_attn = low(jax.nn.softmax(jnp.where(visible[None], scores, -1e+30), axis=-1))
    mixed_out = jnp.einsum('hqk,khd->qhd', prob_attn, values, precision=HIGH).reshape(length, model_width)
    mixed_out = low(low_back(mixed_out))
    branch = low_back(jnp.dot(mixed_out, attn_w[:, 3 * model_width:], precision=HIGH) + bias_proj)
    after_attn = tokens + gate_attn * branch
    normed_two = low(modulate(after_attn, scale_mlp, shift_mlp))
    pre_act = low_back(jnp.dot(normed_two, mlp_w[0], precision=HIGH) + bias_fc1)
    activated = low(jax.nn.gelu(pre_act, approximate=True))
    mlp_out = low_back(jnp.dot(activated, mlp_w[1].T, precision=HIGH) + bias_fc2)
    after_mlp = after_attn + gate_mlp * mlp_out
    normed_head = low(modulate(after_mlp, scale_head, shift_head))
    logits = low_back(jnp.dot(normed_head, head_w, precision=HIGH) + bias_head)
    log_total = jax.nn.logsumexp(logits, axis=-1)
    picked = jnp.take_along_axis(logits, target[:, None], axis=1)[:, 0]
    return jnp.sum(weight_tok * (log_total - picked))

def total_loss(params, tokens_all, scale_ids, pad_mask, weight_tok, targets, labels):
    cond_w, attn_w, mlp_w, head_w, class_table, biases = [low(param) for param in params]
    model_width = tokens_all.shape[2]
    hidden = mlp_w.shape[2]
    bias_cond, bias_q, bias_v, bias_proj, bias_fc1, bias_fc2, bias_head = bias_parts(biases, model_width, hidden)
    condition = low(jax.nn.silu(class_table[labels]))
    ada_rows = jnp.dot(condition, cond_w, precision=HIGH) + bias_cond
    weights = (attn_w, mlp_w, head_w, bias_q, bias_v, bias_proj, bias_fc1, bias_fc2, bias_head)
    per_image = jax.checkpoint(image_loss)

    def step_image(carry, image_row):
        return (carry + per_image(weights, image_row), None)
    loss_total, _ = lax.scan(step_image, jnp.float32(0.0), (tokens_all, scale_ids, pad_mask, weight_tok, targets, ada_rows))
    return loss_total

def adamw(weight, first, second, grad, factor):
    clipped = grad * factor
    first_new = BETA_ONE * first + (1.0 - BETA_ONE) * clipped
    second_new = BETA_TWO * second + (1.0 - BETA_TWO) * clipped * clipped
    first_hat = first_new / (1.0 - BETA_ONE ** STEP)
    second_hat = second_new / (1.0 - BETA_TWO ** STEP)
    weight_new = weight - LEARN * (first_hat / (jnp.sqrt(second_hat) + ADAM_EPS) + DECAY * weight)
    return (weight_new, first_new, second_new)

def reference(x_in, scale_ids, pad_mask, loss_weights, targets, labels, cond_w, attn_w, mlp_w, head_w, class_table, biases, first_cond, first_attn, first_mlp, first_head, first_table, first_bias, second_cond, second_attn, second_mlp, second_head, second_table, second_bias):
    weight_tok = (loss_weights * pad_mask).astype(jnp.float32)
    true_count = jnp.sum(pad_mask).astype(jnp.float32)
    tokens_all = x_in.astype(jnp.float32)
    params = (cond_w, attn_w, mlp_w, head_w, class_table, biases)

    def mean_loss(param_set):
        loss_total = total_loss(param_set, tokens_all, scale_ids, pad_mask, weight_tok, targets, labels)
        return (loss_total / true_count, loss_total)
    (mean_value, loss_total), pull_back = jax.vjp(mean_loss, params)
    grads = pull_back((jnp.ones_like(mean_value), jnp.zeros_like(loss_total)))[0]
    grad_norm = jnp.sqrt(sum((jnp.sum(grad * grad) for grad in grads)))
    factor = jnp.minimum(1.0, CLIP / grad_norm)
    firsts = (first_cond, first_attn, first_mlp, first_head, first_table, first_bias)
    seconds = (second_cond, second_attn, second_mlp, second_head, second_table, second_bias)
    results = [adamw(param, first, second, grad, factor) for param, first, second, grad in zip(params, firsts, seconds, grads)]
    new_weights = [entry[0] for entry in results]
    new_first = [entry[1] for entry in results]
    new_second = [entry[2] for entry in results]
    copies = [weight.astype(jnp.bfloat16) for weight in new_weights]
    return tuple(new_weights + new_first + new_second + copies + [grad_norm, loss_total, true_count])
```

```python
import functools

import jax
import jax.numpy as jnp
from jax import lax
from jax.experimental import pallas as pl
from jax.experimental.pallas import tpu as pltpu
from jax.sharding import PartitionSpec as P

STEP = 5
HIGH = lax.Precision.HIGHEST
NORM_EPS = 1e-06
CLIP = 0.01
LEARN = 0.02
DECAY = 0.1
BETA_ONE = 0.5
BETA_TWO = 0.5
ADAM_EPS = 1e-08
SCORE_SCALE = 0.125
MESH = pl.DeviceIdType.MESH
F32 = jnp.float32
BF16 = jnp.bfloat16
ANY = pl.BlockSpec(memory_space=pl.ANY)
VM = pl.BlockSpec(memory_space=pltpu.VMEM)

ROWS_YZ = 576
HALF_YZ = 288
QUARTER = 112
PART_ROWS = (32, 56, 40)
PART_BASE = (0, 256, 704)
ORDERS = ("xyz", "yzx", "zxy")


def place():
    dp = lax.axis_index("dp")
    sq = lax.axis_index("seq")
    core = lax.rem(dp, 2)
    y = lax.rem(dp // 2, 4)
    z = lax.rem(sq, 2) * 2 + dp // 8
    return sq // 2, y, z, core


def at(x, y, z, core):
    x, y, z = lax.rem(x + 4, 4), lax.rem(y + 4, 4), lax.rem(z + 4, 4)
    return (lax.rem(z, 2) * 8 + y * 2 + core, x * 2 + z // 2)


def greet(devices):
    bar = pltpu.get_barrier_semaphore()
    for device in devices:
        pl.semaphore_signal(bar, inc=1, device_id=device, device_id_type=MESH)
    pl.semaphore_wait(bar, len(devices))


def remote(src, dst, send, recv, device):
    return pltpu.make_async_remote_copy(
        src_ref=src, dst_ref=dst, send_sem=send, recv_sem=recv, device_id=device, device_id_type=MESH
    )


def params(collective_id, vmem=None):
    return pltpu.CompilerParams(
        collective_id=collective_id, has_side_effects=True, vmem_limit_bytes=vmem
    )


def gather_kernel(s, w, wo, ss, rs, loc, os, orr):
    x, y, z, c = place()
    zl = lax.rem(z, 2)
    up, down = lax.rem(y + 1, 4), lax.rem(y + 3, 4)
    side = 1 - 2 * c
    yp, ym = at(x, y + 1, z, c), at(x, y - 1, z, c)
    zp, zm = at(x, y, z + 1, c), at(x, y, z - 1, c)
    xp, xm = at(x + 1, y, z, c), at(x - 1, y, z, c)
    zs = at(x, y, z + side, c)
    mate = at(x, y, z, 1 - c)
    greet([yp, ym, zp, zm, xp, xm, mate])

    def quarter(pos):
        return pl.ds(pl.multiple_of(ROWS_YZ + QUARTER * lax.rem(pos + 4, 4), 16), QUARTER)

    mine = quarter(x)
    full, first, second = pl.ds(0, ROWS_YZ), pl.ds(0, HALF_YZ), pl.ds(HALF_YZ, HALF_YZ)
    order = (0, 1, 2, 3)
    sent = []

    def go(j, k, src, dst, device):
        cp = remote(src, dst, ss.at[j, k], rs.at[j, k], device)
        cp.start()
        sent.append(cp)

    def got(j, k, ref):
        remote(ref, ref, ss.at[j, k], rs.at[j, k], mate).wait_recv()

    locals_ = []
    for j in order:
        go(j, 0, s.at[j, full], w.at[zl, y, j, full], yp)
        go(j, 1, s.at[j, full], w.at[zl, y, j, full], ym)
        go(j, 6, s.at[j, mine], w.at[zl, y, j, mine], zs)
        for i, rows in enumerate((full, mine)):
            cp = pltpu.make_async_copy(s.at[j, rows], w.at[zl, y, j, rows], loc.at[j, i])
            cp.start()
            locals_.append(cp)
    for cp in locals_:
        cp.wait()
    for j in order:
        got(j, 6, w.at[1 - zl, y, j, mine])
        go(j, 7, w.at[:, y, j, mine], w.at[:, y, j, mine], yp)
        go(j, 8, w.at[:, y, j, mine], w.at[:, y, j, mine], ym)
        got(j, 0, w.at[zl, down, j, full])
        got(j, 1, w.at[zl, up, j, full])
        go(j, 2, w.at[zl, down, j, first], w.at[zl, down, j, first], yp)
        go(j, 3, w.at[zl, up, j, second], w.at[zl, up, j, second], ym)
    for j in order:
        got(j, 7, w.at[:, down, j, mine])
        got(j, 8, w.at[:, up, j, mine])
        go(j, 9, w.at[0, down, j, mine], w.at[0, down, j, mine], yp)
        go(j, 10, w.at[1, up, j, mine], w.at[1, up, j, mine], ym)
        far = lax.rem(y + 2, 4)
        got(j, 2, w.at[zl, far, j, first])
        got(j, 3, w.at[zl, far, j, second])
        go(j, 4, w.at[zl, :, j, first], w.at[zl, :, j, first], zp)
        go(j, 5, w.at[zl, :, j, second], w.at[zl, :, j, second], zm)
    for j in order:
        far = lax.rem(y + 2, 4)
        got(j, 9, w.at[0, far, j, mine])
        got(j, 10, w.at[1, far, j, mine])
        go(j, 11, w.at[:, :, j, mine], w.at[:, :, j, mine], xp)
        go(j, 12, w.at[:, :, j, mine], w.at[:, :, j, mine], xm)
    for j in order:
        left, right = quarter(x - 1), quarter(x + 1)
        got(j, 11, w.at[:, :, j, left])
        got(j, 12, w.at[:, :, j, right])
        go(j, 13, w.at[0, :, j, left], w.at[0, :, j, left], xp)
        go(j, 14, w.at[1, :, j, right], w.at[1, :, j, right], xm)
    last = []
    for j in order:
        across = quarter(x + 2)
        got(j, 4, w.at[1 - zl, :, j, first])
        got(j, 5, w.at[1 - zl, :, j, second])
        got(j, 13, w.at[0, :, j, across])
        got(j, 14, w.at[1, :, j, across])
        if j == 0:
            for i in range(2):
                src = w.at[1, 2 + i, 0]
                dst = wo.at[2 * i + c]
                cp = remote(src, dst, os.at[i], orr.at[i], mate)
                cp.start()
                lc = pltpu.make_async_copy(src, dst, loc.at[i, 2])
                lc.start()
                last += [cp, lc]
    for cp in last:
        cp.wait()
    for cp in sent:
        cp.wait_send()


def gather_weights(shard):
    return pl.pallas_call(
        gather_kernel,
        out_shape=(
            jax.ShapeDtypeStruct((2, 4, 4, 1024, 256), BF16),
            jax.ShapeDtypeStruct((4, 1024, 256), BF16),
        ),
        in_specs=[ANY],
        out_specs=(ANY, ANY),
        scratch_shapes=[
            pltpu.SemaphoreType.DMA((4, 15)),
            pltpu.SemaphoreType.DMA((4, 15)),
            pltpu.SemaphoreType.DMA((4, 3)),
            pltpu.SemaphoreType.DMA((2,)),
            pltpu.SemaphoreType.DMA((2,)),
        ],
        compiler_params=params(0),
    )(shard)


def pair_kernel(n, *refs):
    ins, outs = refs[:n], refs[n : 2 * n]
    ss, rs, loc = refs[2 * n :]
    x, y, z, c = place()
    mate = at(x, y, z, 1 - c)
    greet([mate])
    cps = []
    for i in range(n):
        cps.append(remote(ins[i], outs[i].at[c], ss.at[i], rs.at[i], mate))
        cps.append(pltpu.make_async_copy(ins[i], outs[i].at[c], loc.at[i]))
    for cp in cps:
        cp.start()
    for cp in cps:
        cp.wait()


def pair_gather(cid, *arrays):
    n = len(arrays)
    return pl.pallas_call(
        functools.partial(pair_kernel, n),
        out_shape=tuple(jax.ShapeDtypeStruct((2,) + a.shape, a.dtype) for a in arrays),
        in_specs=[ANY] * n,
        out_specs=(ANY,) * n,
        scratch_shapes=[pltpu.SemaphoreType.DMA((n,))] * 3,
        compiler_params=params(cid),
    )(*arrays)


def swap_kernel(a, o, got, ss, rs):
    x, y, z, c = place()
    mate = at(x, y, z, 1 - c)
    greet([mate])
    cp = remote(a.at[1 - c], got, ss, rs, mate)
    cp.start()
    cp.wait()
    o[...] = a[c] + got[...]


def swap_add(cid, a):
    return pl.pallas_call(
        swap_kernel,
        out_shape=jax.ShapeDtypeStruct(a.shape[1:], a.dtype),
        in_specs=[VM],
        out_specs=VM,
        scratch_shapes=[
            pltpu.VMEM(a.shape[1:], a.dtype),
            pltpu.SemaphoreType.DMA,
            pltpu.SemaphoreType.DMA,
        ],
        compiler_params=params(cid, 32 * 2**20),
    )(a)


def group_peers():
    dp = lax.axis_index("dp")
    sq = lax.axis_index("seq")
    core = lax.rem(dp, 2)
    out = [(dp + 1 - 2 * core, sq)]
    for i in range(1, 8):
        for flip in range(2):
            out.append((dp + flip * (1 - 2 * core), lax.rem(sq + i, 8)))
    return out


def a2a_kernel(a, o, ss, rs, loc):
    dp = lax.axis_index("dp")
    sq = lax.axis_index("seq")
    peers = [(dp, lax.rem(sq + i, 8)) for i in range(1, 8)]
    greet(peers)
    own = pltpu.make_async_copy(a.at[sq], o.at[sq], loc)
    own.start()
    cps = []
    for i in range(1, 8):
        to = lax.rem(sq + i, 8)
        cp = remote(a.at[to], o.at[sq], ss.at[i], rs.at[i], (dp, to))
        cp.start()
        cps.append(cp)
    own.wait()
    for cp in cps:
        cp.wait()


def all_to_all(cid, a):
    return pl.pallas_call(
        a2a_kernel,
        out_shape=jax.ShapeDtypeStruct(a.shape, a.dtype),
        in_specs=[ANY],
        out_specs=ANY,
        scratch_shapes=[
            pltpu.SemaphoreType.DMA((8,)),
            pltpu.SemaphoreType.DMA((8,)),
            pltpu.SemaphoreType.DMA,
        ],
        compiler_params=params(cid),
    )(a)


def head_lanes(pair, core):
    return pl.ds(pl.multiple_of(((pair // 2 * 2 + core) * 2 + lax.rem(pair, 2)) * 128, 128), 128)


def to_tokens_kernel(a, o, ss, rs, loc):
    dp = lax.axis_index("dp")
    sq = lax.axis_index("seq")
    core = lax.rem(dp, 2)
    base = dp - core
    pair, owner = sq // 2, lax.rem(sq, 2)
    greet(group_peers())
    lanes = head_lanes(pair, core)

    def copy(i):
        to = lax.rem(sq + i, 8)
        return remote(
            a.at[to], o.at[:, lanes], ss.at[i], rs.at[pair, core], (base + owner, to)
        )

    for i in range(1, 8):
        copy(i).start()
    own = pltpu.make_async_copy(a.at[sq], o.at[:, lanes], loc)

    @pl.when(owner == core)
    def _():
        own.start()

    @pl.when(owner != core)
    def _():
        copy(0).start()

    for p in range(4):
        for q in range(2):
            view = o.at[:, pl.ds(((p // 2 * 2 + q) * 2 + p % 2) * 128, 128)]

            @pl.when(jnp.logical_or(sq != p * 2 + core, core != q))
            def _():
                remote(view, view, ss.at[0], rs.at[p, q], (base + owner, sq)).wait_recv()

    for i in range(1, 8):
        copy(i).wait_send()

    @pl.when(owner == core)
    def _():
        own.wait()

    @pl.when(owner != core)
    def _():
        copy(0).wait_send()


def to_tokens(cid, a):
    return pl.pallas_call(
        to_tokens_kernel,
        out_shape=jax.ShapeDtypeStruct((256, 1024), a.dtype),
        in_specs=[ANY],
        out_specs=ANY,
        scratch_shapes=[
            pltpu.SemaphoreType.DMA((8,)),
            pltpu.SemaphoreType.DMA((4, 2)),
            pltpu.SemaphoreType.DMA,
        ],
        compiler_params=params(cid),
    )(a)


def to_heads_kernel(a, o, ss, rs, loc):
    dp = lax.axis_index("dp")
    sq = lax.axis_index("seq")
    core = lax.rem(dp, 2)
    base = dp - core
    pair, owner = sq // 2, lax.rem(sq, 2)
    greet(group_peers())
    own = pltpu.make_async_copy(a.at[:, head_lanes(pair, core)], o.at[sq], loc)

    def each(fn):
        for p in range(4):
            for q in range(2):
                view = a.at[:, pl.ds(((p // 2 * 2 + q) * 2 + p % 2) * 128, 128)]
                to = (base + q, p * 2 + core)
                cp = remote(view, o.at[sq], ss.at[p, q], rs.at[sq], to)
                here = jnp.logical_and(sq == p * 2 + core, core == q)
                fn(cp, here)

    def start(cp, here):
        @pl.when(jnp.logical_not(here))
        def _():
            cp.start()

    def finish(cp, here):
        @pl.when(jnp.logical_not(here))
        def _():
            cp.wait_send()

    each(start)

    @pl.when(owner == core)
    def _():
        own.start()

    for i in range(8):
        view = o.at[i]

        @pl.when(jnp.logical_or(sq != i, owner != core))
        def _():
            remote(view, view, ss.at[0, 0], rs.at[i], (base, sq)).wait_recv()

    each(finish)

    @pl.when(owner == core)
    def _():
        own.wait()


def to_heads(cid, a):
    return pl.pallas_call(
        to_heads_kernel,
        out_shape=jax.ShapeDtypeStruct((8, 256, 128), a.dtype),
        in_specs=[ANY],
        out_specs=ANY,
        scratch_shapes=[
            pltpu.SemaphoreType.DMA((4, 2)),
            pltpu.SemaphoreType.DMA((8,)),
            pltpu.SemaphoreType.DMA,
        ],
        compiler_params=params(cid),
    )(a)


def cond_kernel(
    msg, slots, table, cond_w, msg_all, slots_all, cond_all, emb_out, ada,
    cond_own, ada_own, s1, r1, s2, r2, s3, r3, s4, r4,
):
    dp = lax.axis_index("dp")
    sq = lax.axis_index("seq")
    core = lax.rem(dp, 2)
    row = [(lax.rem(dp + i, 16), sq) for i in range(1, 16)]
    group = group_peers()
    greet(row + group[1:])
    first = []
    for i, to in enumerate(row):
        cp = remote(msg, msg_all.at[dp], s1.at[i], r1.at[i], to)
        cp.start()
        first.append(cp)
    msg_all[dp] = msg[...]
    for cp in first:
        cp.wait()
    seen = msg_all[...]
    count = jnp.sum(seen[:, 10, 2:3], axis=0, keepdims=True)
    slots[7:8, :] = jnp.broadcast_to(count, (1, 128))
    second = []
    for i, to in enumerate(group):
        cp = remote(slots, slots_all.at[sq * 2 + core], s2.at[i], r2.at[i], to)
        cp.start()
        second.append(cp)
    slots_all[sq * 2 + core] = slots[...]
    classes = table.shape[0]
    lane = lax.broadcasted_iota(jnp.int32, (32, classes), 1)
    labels = jnp.concatenate([seen[d, 10:11, i : i + 1] for d in range(16) for i in range(2)], axis=0)
    hit = jnp.where(lane == labels.astype(jnp.int32), 1.0, 0.0).astype(BF16)
    emb = jnp.dot(hit, table[...], preferred_element_type=F32)
    emb_out[...] = emb
    cond_own[...] = (emb / (1.0 + jnp.exp(-emb))).astype(BF16)
    cond_all[dp] = cond_own[...]
    third = []
    for i, to in enumerate(row):
        cp = remote(cond_own, cond_all.at[dp], s3.at[i], r3.at[i], to)
        cp.start()
        third.append(cp)
    for cp in third:
        cp.wait()
    acc = jnp.zeros((32, 512), F32)
    for d in range(16):
        acc += jnp.dot(cond_all[d], cond_w[pl.ds(64 * d, 64), :], preferred_element_type=F32)
    bias = []
    for i in range(4):
        at_row = dp * 4 + i
        bias.append(msg_all[at_row // 10, pl.ds(lax.rem(at_row, 10), 1), :])
    acc += jnp.concatenate(bias, axis=1)
    for d in range(16):
        ada_own[d] = acc[2 * d : 2 * d + 2]
    fourth = []
    for i in range(15):
        to = lax.rem(dp + 1 + i, 16)
        cp = remote(ada_own.at[to], ada.at[dp], s4.at[i], r4.at[i], (to, sq))
        cp.start()
        fourth.append(cp)
    ada[dp] = ada_own[dp]
    for cp in fourth:
        cp.wait()
    for cp in second:
        cp.wait()


def condition(msg, slots, table, cond_w):
    dma = pltpu.SemaphoreType.DMA
    return pl.pallas_call(
        cond_kernel,
        out_shape=(
            jax.ShapeDtypeStruct((16, 16, 128), F32),
            jax.ShapeDtypeStruct((16, 8, 128), F32),
            jax.ShapeDtypeStruct((16, 32, 64), BF16),
            jax.ShapeDtypeStruct((32, 64), F32),
            jax.ShapeDtypeStruct((16, 2, 512), F32),
        ),
        in_specs=[VM] * 4,
        out_specs=(VM,) * 5,
        scratch_shapes=[pltpu.VMEM((32, 64), BF16), pltpu.VMEM((16, 2, 512), F32)]
        + [dma((15,))] * 8,
        input_output_aliases={},
        compiler_params=params(1),
    )(msg, slots, table, cond_w)


def small_kernel(
    msg, cond_w, ada_all, bias_sum, dcond,
    got, mine, all_seq, part, back, s1, r1, s2, r2, s3, r3,
):
    dp = lax.axis_index("dp")
    sq = lax.axis_index("seq")
    row = [lax.rem(dp + i, 16) for i in range(1, 16)]
    line = [lax.rem(sq + i, 8) for i in range(1, 8)]
    greet([(d, sq) for d in row] + [(dp, s) for s in line])
    cps = []
    for i, d in enumerate(row):
        cp = remote(msg.at[d], got.at[dp], s1.at[i], r1.at[i], (d, sq))
        cp.start()
        cps.append(cp)
    got[dp] = msg[dp]
    for cp in cps:
        cp.wait()
    seen = got[...]
    for d in range(16):
        mine[d] = seen[d, :8, :]
    rest = jnp.sum(seen[:, 8:24, :], axis=0)
    mine[16] = rest[:8]
    mine[17] = rest[8:]
    cps = []
    for i, s in enumerate(line):
        cp = remote(mine, all_seq.at[sq], s2.at[i], r2.at[i], (dp, s))
        cp.start()
        cps.append(cp)
    all_seq[sq] = mine[...]
    for cp in cps:
        cp.wait()
    total = jnp.sum(all_seq[...], axis=0)
    bias_sum[0] = total[16]
    bias_sum[1] = total[17]
    rows = []
    for d in range(16):
        for i in range(2):
            rows.append(
                jnp.concatenate([total[d, 4 * i + k : 4 * i + k + 1, :] for k in range(4)], axis=1)
            )
    dada = jnp.concatenate(rows, axis=0)
    ada_all[...] = dada
    for d in range(16):
        part[d] = lax.dot_general(
            dada, cond_w[pl.ds(64 * d, 64), :].astype(F32), (((1,), (1,)), ((), ())),
            precision=HIGH, preferred_element_type=F32,
        )
    cps = []
    for i, d in enumerate(row):
        cp = remote(part.at[d], back.at[dp], s3.at[i], r3.at[i], (d, sq))
        cp.start()
        cps.append(cp)
    back[dp] = part[dp]
    for cp in cps:
        cp.wait()
    dcond[...] = jnp.sum(back[...], axis=0)


def small_reduce(msg, cond_w):
    dma = pltpu.SemaphoreType.DMA
    return pl.pallas_call(
        small_kernel,
        out_shape=(
            jax.ShapeDtypeStruct((32, 512), F32),
            jax.ShapeDtypeStruct((2, 8, 128), F32),
            jax.ShapeDtypeStruct((32, 64), F32),
        ),
        in_specs=[VM] * 2,
        out_specs=(VM,) * 3,
        scratch_shapes=[
            pltpu.VMEM((16, 24, 128), F32),
            pltpu.VMEM((18, 8, 128), F32),
            pltpu.VMEM((8, 18, 8, 128), F32),
            pltpu.VMEM((16, 32, 64), F32),
            pltpu.VMEM((16, 32, 64), F32),
        ]
        + [dma((15,))] * 6,
        compiler_params=params(2),
    )(msg, cond_w)


def pick(ref, x, y, z, extra=()):
    everything = slice(None)
    zl = everything if z is None else lax.rem(z, 2)
    zh = everything if z is None else z // 2
    return (
        zl,
        everything if y is None else y,
        everything if x is None else x,
        zh,
    )


def halves(order, phase, rows):
    axis = order[phase]
    later = order[phase + 1 :]
    if axis != "z" and "z" in later:
        return ("zl", slice(0, 1), slice(1, 2))
    if "y" in later:
        return ("y", slice(0, 2), slice(2, 4))
    if "x" in later:
        return ("x", slice(0, 2), slice(2, 4))
    cut = (rows // 16) * 8 if (rows // 16) * 16 == rows else (rows // 16) * 8 + 8
    return ("r", slice(0, cut), slice(cut, rows))


def cut_size(part, phase):
    order, rows = ORDERS[part], PART_ROWS[part]
    axis, later = order[phase], order[phase + 1 :]
    dims = {
        "zl": 2 if "z" in later else 1,
        "y": 4 if "y" in later else 1,
        "x": 4 if "x" in later else 1,
        "zh": 2 if "z" in later else 1,
        "r": rows,
    }
    return dims


def reduce_kernel(*refs):
    gs = refs[0:4]
    extra, out, norm = refs[4:7]
    pos = 7
    parts = [refs[pos + 3 * slot : pos + 3 * slot + 3] for slot in range(2)]
    pos += 6
    recv = {}
    for p in range(3):
        for ph in range(3):
            recv[p, ph] = refs[pos : pos + 4]
            pos += 4
    ss, rs, loc, gss, grs, oloc, tile, tiles, nss, nrs = refs[pos:]

    x, y, z, c = place()
    zl, zh = lax.rem(z, 2), z // 2
    here = {"x": x, "y": y, "z": z}

    def step(axis, by):
        q = dict(here)
        q[axis] = q[axis] + by
        return at(q["x"], q["y"], q["z"], c)

    mate = at(x, y, z, 1 - c)
    greet([step(a, b) for a in "xyz" for b in (1, 2, 3)] + [mate])

    def view(ref, p, ph, index, half=None):
        order = ORDERS[p]
        sel = {}
        for i, a in enumerate(order):
            if i < ph:
                sel[a] = here[a]
            elif i == ph:
                sel[a] = lax.rem(index + 4, 4)
            else:
                sel[a] = None
        idx = {
            "zl": slice(0, 2) if sel["z"] is None else pl.ds(lax.rem(sel["z"], 2), 1),
            "y": slice(0, 4) if sel["y"] is None else pl.ds(sel["y"], 1),
            "x": slice(0, 4) if sel["x"] is None else pl.ds(sel["x"], 1),
            "zh": slice(0, 2) if sel["z"] is None else pl.ds(sel["z"] // 2, 1),
            "r": slice(0, PART_ROWS[p]),
        }
        if half is not None:
            name, one, two = halves(order, ph, PART_ROWS[p])
            idx[name] = (one, two)[half]
        return ref.at[idx["zl"], idx["y"], idx["x"], idx["zh"], idx["r"]]

    def add(dst, srcs):
        dims = dst.shape[:4]
        total = dims[0] * dims[1] * dims[2] * dims[3]

        def body(i, carry):
            d = lax.rem(i, dims[3])
            i2 = i // dims[3]
            cc = lax.rem(i2, dims[2])
            i3 = i2 // dims[2]
            b = lax.rem(i3, dims[1])
            a = i3 // dims[1]
            acc = dst[a, b, cc, d]
            for s in srcs:
                acc = acc + s[a, b, cc, d]
            dst[a, b, cc, d] = acc
            return carry

        lax.fori_loop(0, total, body, 0)

    sent = []

    def job(j):
        slot = j % 2
        loads = []
        for p in range(3):
            r = PART_ROWS[p]
            for xi in range(4):
                for zi in range(2):
                    src = gs[j].at[:, :, pl.ds(PART_BASE[p] + (xi * 2 + zi) * r, r)]
                    cp = pltpu.make_async_copy(src, parts[slot][p].at[:, :, xi, zi], loc.at[slot, p, xi * 2 + zi])
                    cp.start()
                    loads.append(cp)
        yield
        for cp in loads:
            cp.wait()
        mine = []

        def go(p, ph, k, src, dst, device):
            cp = remote(src, dst, ss.at[j, p * 3 + ph, k], rs.at[j, p * 3 + ph, k], device)
            cp.start()
            mine.append(cp)

        def got(p, ph, k, ref):
            remote(ref, ref, ss.at[j, p * 3 + ph, k], rs.at[j, p * 3 + ph, k], mate).wait_recv()

        for ph in range(3):
            for p in range(3):
                a = ORDERS[p][ph]
                i = here[a]
                g = parts[slot][p]
                bufs = [b.at[j] for b in recv[p, ph]]
                go(p, ph, 0, view(g, p, ph, i + 2, 0), bufs[0], step(a, 1))
                go(p, ph, 1, view(g, p, ph, i + 2, 1), bufs[1], step(a, -1))
            yield
            for p in range(3):
                a = ORDERS[p][ph]
                i = here[a]
                g = parts[slot][p]
                bufs = [b.at[j] for b in recv[p, ph]]
                got(p, ph, 0, bufs[0])
                add(view(g, p, ph, i + 1, 0), [bufs[0]])
                got(p, ph, 1, bufs[1])
                add(view(g, p, ph, i - 1, 1), [bufs[1]])
                go(p, ph, 2, view(g, p, ph, i + 1), bufs[2], step(a, 1))
                go(p, ph, 3, view(g, p, ph, i - 1), bufs[3], step(a, -1))
            yield
            for p in range(3):
                a = ORDERS[p][ph]
                i = here[a]
                g = parts[slot][p]
                bufs = [b.at[j] for b in recv[p, ph]]
                got(p, ph, 2, bufs[2])
                got(p, ph, 3, bufs[3])
                add(view(g, p, ph, i), [bufs[2], bufs[3]])
        outs = []
        for p in range(3):
            r = PART_ROWS[p]
            piece = parts[slot][p].at[zl, y, x, zh]
            val = piece[...]
            sq = val * val
            acc = tile[...]
            for t in range(r // 8):
                for u in range(2):
                    acc = acc + sq[8 * t : 8 * t + 8, 128 * u : 128 * u + 128]
            tile[...] = acc
            rows = pl.ds(pl.multiple_of(PART_BASE[p] + (x * 2 + zh) * r, 8), r)
            cp = pltpu.make_async_copy(piece, out.at[j, rows], oloc.at[j, p])
            cp.start()
            outs.append(cp)
            cp = remote(piece, out.at[j, rows], gss.at[j, p, 0], grs.at[j, p, 0], step("z", 2))
            cp.start()
            mine.append(cp)
        yield
        for cp in outs:
            cp.wait()

        def rows_of(p, xi, zi, n):
            r = PART_ROWS[p]
            return pl.ds(pl.multiple_of(PART_BASE[p] + (lax.rem(xi + 4, 4) * 2 + zi) * r, 8), n * r)

        def ago(p, k, rows, device):
            cp = remote(out.at[j, rows], out.at[j, rows], gss.at[j, p, k], grs.at[j, p, k], device)
            cp.start()
            mine.append(cp)

        def agot(p, k, rows):
            ref = out.at[j, rows]
            remote(ref, ref, gss.at[j, p, k], grs.at[j, p, k], mate).wait_recv()

        for p in range(3):
            agot(p, 0, rows_of(p, x, 1 - zh, 1))
            ago(p, 1, rows_of(p, x, 0, 2), step("x", 1))
            ago(p, 2, rows_of(p, x, 0, 2), step("x", -1))
        yield
        for p in range(3):
            agot(p, 1, rows_of(p, x - 1, 0, 2))
            agot(p, 2, rows_of(p, x + 1, 0, 2))
            ago(p, 3, rows_of(p, x - 1, 0, 1), step("x", 1))
            ago(p, 4, rows_of(p, x + 1, 1, 1), step("x", -1))
        yield
        for p in range(3):
            agot(p, 3, rows_of(p, x + 2, 0, 1))
            agot(p, 4, rows_of(p, x + 2, 1, 1))
        for cp in mine:
            cp.wait_send()

    tile[...] = extra[...]
    jobs = [job(j) for j in range(4)]
    waiting = {0: [0, 2], 1: [1, 3]}
    active = []
    for slot in (0, 1):
        active.append([slot, waiting[slot].pop(0)])
    while active:
        for entry in list(active):
            try:
                next(jobs[entry[1]])
            except StopIteration:
                if waiting[entry[0]]:
                    entry[1] = waiting[entry[0]].pop(0)
                    next(jobs[entry[1]])
                else:
                    active.remove(entry)
    k = 0
    for a in ("x", "y", "z"):
        cps = []
        for by in (1, 2, 3):
            cp = remote(tile, tiles.at[k], nss.at[k], nrs.at[k], step(a, by))
            cp.start()
            cps.append((cp, k))
            k += 1
        for cp, _ in cps:
            cp.wait()
        acc = tile[...]
        for _, i in cps:
            acc = acc + tiles[i]
        tile[...] = acc
    cp = remote(tile, tiles.at[k], nss.at[k], nrs.at[k], mate)
    cp.start()
    cp.wait()
    norm[...] = tile[...] + tiles[k]


def reduce_grads(grads, extra):
    dma = pltpu.SemaphoreType.DMA
    scratch = []
    for slot in range(2):
        for p in range(3):
            scratch.append(pltpu.VMEM((2, 4, 4, 2, PART_ROWS[p], 256), F32))
    for p in range(3):
        for ph in range(3):
            dims = cut_size(p, ph)
            name, one, two = halves(ORDERS[p], ph, PART_ROWS[p])
            for k in range(4):
                d = dict(dims)
                if k < 2:
                    sl = (one, two)[k]
                    d[name] = sl.stop - sl.start
                scratch.append(pltpu.VMEM((4, d["zl"], d["y"], d["x"], d["zh"], d["r"], 256), F32))
    scratch += [
        dma((4, 9, 4)),
        dma((4, 9, 4)),
        dma((2, 3, 8)),
        dma((4, 3, 5)),
        dma((4, 3, 5)),
        dma((4, 3)),
        pltpu.VMEM((8, 128), F32),
        pltpu.VMEM((10, 8, 128), F32),
        dma((10,)),
        dma((10,)),
    ]
    return pl.pallas_call(
        reduce_kernel,
        out_shape=(
            jax.ShapeDtypeStruct((4, 1024, 256), F32),
            jax.ShapeDtypeStruct((8, 128), F32),
        ),
        in_specs=[ANY] * 4 + [VM],
        out_specs=(ANY, VM),
        scratch_shapes=scratch,
        compiler_params=params(3, 62 * 2**20),
    )(*grads, extra)


def layer_norm(values):
    center = values - jnp.mean(values, -1, keepdims=True)
    spread = jnp.mean(center * center, -1, keepdims=True)
    return center * lax.rsqrt(spread + NORM_EPS)


def modulate(values, scale_row, shift_row):
    return layer_norm(values) * (1.0 + scale_row) + shift_row


def modulate_back(values, scale_row, shift_row, grad_out):
    _, pull_back = jax.vjp(modulate, values, scale_row, shift_row)
    return pull_back(grad_out)


def columns(h, w):
    return jnp.einsum("td,jdk->jtk", h, w, preferred_element_type=F32)


def rows_back(g, w):
    return jnp.einsum("jtk,jdk->td", g, w, preferred_element_type=F32)


def weight_grad(h, g):
    return jnp.einsum("td,jtk->jdk", h, g, preferred_element_type=F32)


def adamw(weight, first, second, grad, factor):
    clipped = grad * factor
    first_new = BETA_ONE * first + (1.0 - BETA_ONE) * clipped
    second_new = BETA_TWO * second + (1.0 - BETA_TWO) * clipped * clipped
    first_hat = first_new / (1.0 - BETA_ONE**STEP)
    second_hat = second_new / (1.0 - BETA_TWO**STEP)
    weight_new = weight - LEARN * (first_hat / (jnp.sqrt(second_hat) + ADAM_EPS) + DECAY * weight)
    return (weight_new, first_new, second_new)


def local(
    x_in, scale_ids, pad_mask, loss_weights, targets, labels,
    cond_w, attn_w, mlp_w, head_w, class_table, biases,
    first_cond, first_attn, first_mlp, first_head, first_table, first_bias,
    second_cond, second_attn, second_mlp, second_head, second_table, second_bias,
):
    dp = lax.axis_index("dp")
    core = dp % 2
    wb_cond = cond_w.astype(BF16)
    shard = jnp.stack([attn_w, mlp_w[0], mlp_w[1], head_w]).astype(BF16)

    count_part = jnp.sum(pad_mask.astype(F32))
    row = jnp.concatenate([labels.astype(F32), count_part[None], jnp.zeros((125,), F32)])
    msg = jnp.concatenate(
        [biases.astype(BF16).astype(F32).reshape(10, 128), row[None], jnp.zeros((5, 128), F32)]
    )
    level = jnp.where(pad_mask > 0, scale_ids, 1000).astype(F32)
    weight_own = (loss_weights * pad_mask).astype(F32)
    slots = jnp.concatenate(
        [level * 16.0 + scale_ids.astype(F32), targets.astype(F32), weight_own, jnp.zeros((2, 128), F32)]
    )
    msg_all, slots_all, cond_all, embedded, ada = condition(
        msg, slots, class_table.astype(BF16), wb_cond
    )
    w, wo = gather_weights(shard)
    w = w.reshape(8, 4, 1024, 256)

    bias_all = msg_all[:, :10].reshape(20480)
    b_q, b_v, b_proj, b_fc1, b_fc2, b_head = jnp.split(
        bias_all[8192:], [1024, 2048, 3072, 7168, 8192]
    )

    def own_columns(b):
        return lax.dynamic_index_in_dim(b.reshape(-1, 2, 256), core, 1, keepdims=False)

    slots_all = slots_all.reshape(8, 2, 8, 128)
    true_count = jnp.sum(slots_all[:, 0, 7, 0])
    ada_rows = jnp.transpose(ada, (1, 0, 2)).reshape(2, 1, 8192)
    g_a, g_m, s_a, s_m, t_a, t_m, s_h, t_h = jnp.split(ada_rows, 8, axis=2)
    sq_index = lax.axis_index("seq")
    pair_slots = lax.dynamic_index_in_dim(slots_all, sq_index, 0, keepdims=False)
    target_pair = pair_slots[:, 2:4].reshape(512).astype(jnp.int32)
    weight_pair = pair_slots[:, 4:6].reshape(512)
    owner = sq_index % 2
    levels = lax.dynamic_index_in_dim(slots_all, owner, 1, keepdims=False)[:, 0:2]
    levels = jnp.transpose(levels, (1, 0, 2)).reshape(2, 1024)
    key_level = jnp.floor(levels / 16.0)
    query_level = levels - key_level * 16.0

    x = x_in.astype(F32)
    h1 = modulate(x, s_a, t_a).astype(BF16).reshape(256, 1024)
    (h1,) = pair_gather(4, h1)
    h1 = h1.reshape(512, 1024)
    bias_qkv = jnp.concatenate([own_columns(b_q), jnp.zeros((2, 256), F32), own_columns(b_v)])
    qkv = (columns(h1, w[:6, 0]) + bias_qkv[:, None, :]).astype(BF16)
    blocks = qkv.reshape(3, 2, 2, 256, 2, 128).transpose(1, 4, 2, 0, 3, 5).reshape(8, 3, 256, 128)
    heads = all_to_all(5, blocks)

    def by_head(block):
        return block.reshape(8, 2, 128, 2, 64).transpose(1, 3, 0, 2, 4).reshape(2, 2, 1024, 64)

    def from_head(block):
        return block.reshape(2, 2, 8, 128, 64).transpose(2, 0, 3, 1, 4).reshape(8, 256, 128)

    q, k, v = (by_head(heads[:, i]) for i in range(3))
    visible = (key_level[:, None, None, :] <= query_level[:, None, :, None])
    scores = jnp.einsum("ihqd,ihkd->ihqk", q, k, preferred_element_type=F32) * SCORE_SCALE
    probs = jax.nn.softmax(jnp.where(visible, scores, -1e30), axis=-1)
    probs_low = probs.astype(BF16)
    o = jnp.einsum("ihqk,ihkd->ihqd", probs_low, v, preferred_element_type=F32).astype(BF16)
    o = to_tokens(6, from_head(o))
    att = jnp.einsum("td,jdk->tjk", o, wo, preferred_element_type=F32).reshape(256, 1024) + b_proj
    att = att.reshape(2, 128, 1024)
    x1 = x + g_a * att
    h2 = modulate(x1, s_m, t_m).astype(BF16).reshape(256, 1024)
    (h2,) = pair_gather(7, h2)
    h2 = h2.reshape(512, 1024)
    f = columns(h2, w[:, 1]) + own_columns(b_fc1)[:, None, :]
    u = jax.nn.gelu(f, approximate=True).astype(BF16)
    mlp = swap_add(8, rows_back(u, w[:, 2]).reshape(2, 256, 1024)) + b_fc2
    mlp = mlp.reshape(2, 128, 1024)
    x2 = x1 + g_m * mlp
    h3 = modulate(x2, s_h, t_h).astype(BF16).reshape(256, 1024)
    (h3,) = pair_gather(9, h3)
    h3 = h3.reshape(512, 1024)
    logits = columns(h3, w[:, 3]) + own_columns(b_head)[:, None, :]
    top = jnp.max(logits, axis=(0, 2))
    mass = jnp.sum(jnp.exp(logits - top[None, :, None]), axis=(0, 2))
    column = (
        (2 * jnp.arange(8)[:, None] + core) * 256 + jnp.arange(256)[None, :]
    )
    target_hit = target_pair[None, :, None] == column[:, None, :]
    picked = jnp.sum(jnp.where(target_hit, logits, 0.0), axis=(0, 2))
    stats = jnp.stack([top, mass, picked]).reshape(3, 4, 128)
    (stats,) = pair_gather(10, stats)
    stats = stats.reshape(2, 3, 512)
    top_all = jnp.max(stats[:, 0], axis=0)
    mass_all = jnp.sum(stats[:, 1] * jnp.exp(stats[:, 0] - top_all[None]), axis=0)
    log_total = top_all + jnp.log(mass_all)
    picked_all = jnp.sum(stats[:, 2], axis=0)
    loss_part = 0.5 * jnp.sum(weight_pair * (log_total - picked_all))
    dlogits = (
        (weight_pair / true_count)[None, :, None]
        * (jnp.exp(logits - log_total[None, :, None]) - target_hit.astype(F32))
    ).astype(BF16)

    grad_head = weight_grad(h3, dlogits)
    db_head = jnp.sum(dlogits.astype(F32), axis=1)
    dh3 = swap_add(11, rows_back(dlogits, w[:, 3]).reshape(2, 256, 1024)).reshape(2, 128, 1024)
    dx2, ds_h, dt_h = modulate_back(x2, s_h, t_h, dh3)
    dg_m = jnp.sum(dx2 * mlp, axis=1, keepdims=True)
    dmlp = (g_m * dx2).astype(BF16).reshape(256, 1024)
    db_fc2 = jnp.sum(dmlp.astype(F32), axis=0)
    (dmlp,) = pair_gather(12, dmlp)
    dmlp = dmlp.reshape(512, 1024)
    grad_two = weight_grad(dmlp, u)
    du = columns(dmlp, w[:, 2])
    _, gelu_back = jax.vjp(functools.partial(jax.nn.gelu, approximate=True), f)
    df = gelu_back(du)[0].astype(BF16)
    grad_one = weight_grad(h2, df)
    db_fc1 = jnp.sum(df.astype(F32), axis=1)
    dh2 = swap_add(13, rows_back(df, w[:, 1]).reshape(2, 256, 1024)).reshape(2, 128, 1024)
    dx1, ds_m, dt_m = modulate_back(x1, s_m, t_m, dh2)
    dx1 = dx1 + dx2
    dg_a = jnp.sum(dx1 * att, axis=1, keepdims=True)
    datt = (g_a * dx1).astype(BF16).reshape(256, 1024)
    db_proj = jnp.sum(datt.astype(F32), axis=0)
    do = jnp.einsum(
        "tjk,jdk->td", datt.reshape(256, 4, 256), wo, preferred_element_type=F32
    ).astype(BF16)
    do_heads = by_head(to_heads(14, do))
    o_pair, datt_pair = pair_gather(15, o, datt)
    datt_own = lax.dynamic_index_in_dim(
        datt_pair.reshape(512, 2, 2, 256), core, 2, keepdims=False
    )
    grad_o = jnp.einsum(
        "td,tjk->jdk", o_pair.reshape(512, 1024), datt_own, preferred_element_type=F32
    )
    dprobs = jnp.einsum("ihqd,ihkd->ihqk", do_heads, v, preferred_element_type=F32)
    inner = jnp.sum(probs * dprobs, axis=-1, keepdims=True)
    dscores = (probs * (dprobs - inner)).astype(BF16)
    dq = jnp.einsum("ihqk,ihkd->ihqd", dscores, k, preferred_element_type=F32) * SCORE_SCALE
    dk = jnp.einsum("ihqk,ihqd->ihkd", dscores, q, preferred_element_type=F32) * SCORE_SCALE
    dv = jnp.einsum("ihqk,ihqd->ihkd", probs_low, do_heads, preferred_element_type=F32)
    dqkv = jnp.stack([from_head(t.astype(BF16)) for t in (dq, dk, dv)], axis=1)
    dqkv = all_to_all(16, dqkv)
    dqkv = dqkv.reshape(2, 2, 2, 3, 256, 128).transpose(3, 0, 2, 4, 1, 5).reshape(6, 512, 256)
    grad_qkv = weight_grad(h1, dqkv)
    db_qkv = jnp.sum(dqkv.astype(F32), axis=1)
    dh1 = swap_add(17, rows_back(dqkv, w[:6, 0]).reshape(2, 256, 1024)).reshape(2, 128, 1024)
    _, ds_a, dt_a = modulate_back(x, s_a, t_a, dh1)
    dada = jnp.concatenate([dg_a, dg_m, ds_a, ds_m, dt_a, dt_m, ds_h, dt_h], axis=2)[:, 0]

    def spread_columns(b):
        mine = jnp.arange(2)[None, :, None] == core
        return jnp.where(mine, b[:, None, :], 0.0).reshape(-1)

    bias_part = jnp.concatenate(
        [
            jnp.sum(dada, axis=0),
            spread_columns(db_qkv[0:2]),
            spread_columns(db_qkv[4:6]),
            db_proj,
            spread_columns(db_fc1),
            db_fc2,
            spread_columns(db_head),
        ]
    ).reshape(16, 10, 128)
    ada_msg = dada.reshape(2, 16, 512).transpose(1, 0, 2).reshape(16, 8, 128)
    tail = jnp.concatenate([jnp.full((16, 1, 128), loss_part), jnp.zeros((16, 5, 128), F32)], axis=1)
    dada_all, bias_sum, dcond = small_reduce(
        jnp.concatenate([ada_msg, bias_part, tail], axis=1), wb_cond
    )
    bias_sum = bias_sum.reshape(16, 128)
    loss_total = bias_sum[10, 0]
    grad_bias = bias_sum[:10].reshape(1280)
    cond_full = jnp.transpose(cond_all, (1, 0, 2)).reshape(32, 1024).astype(F32)
    grad_cond = lax.dot_general(
        cond_full, dada_all, (((0,), (0,)), ((), ())), precision=HIGH, preferred_element_type=F32
    )
    _, silu_back = jax.vjp(jax.nn.silu, embedded)
    demb = silu_back(dcond)[0]
    labels_all = msg_all[:, 10, 0:2].reshape(32).astype(jnp.int32)
    class_hit = (labels_all[:, None] == jnp.arange(class_table.shape[0])[None, :]).astype(F32)
    grad_table = lax.dot_general(
        class_hit, demb, (((0,), (0,)), ((), ())), precision=HIGH, preferred_element_type=F32
    )
    own_squares = (
        jnp.sum(grad_cond * grad_cond) + jnp.sum(grad_table * grad_table) + jnp.sum(grad_bias * grad_bias)
    ) / 8.0
    extra = jnp.zeros((8, 128), F32).at[0, 0].set(own_squares)
    grad_attn = jnp.concatenate([grad_qkv, grad_o])
    shape = (2, 4, 1024, 256)
    summed, squares = reduce_grads(
        [g.reshape(shape) for g in (grad_attn, grad_one, grad_two, grad_head)], extra
    )
    grad_norm = jnp.sqrt(jnp.sum(squares))
    factor = jnp.minimum(1.0, CLIP / grad_norm)
    grads = (grad_cond, summed[0], summed[1:3], summed[3], grad_table, grad_bias)
    weights = (cond_w, attn_w, mlp_w, head_w, class_table, biases)
    firsts = (first_cond, first_attn, first_mlp, first_head, first_table, first_bias)
    seconds = (second_cond, second_attn, second_mlp, second_head, second_table, second_bias)
    results = [
        adamw(weight, first, second, grad, factor)
        for weight, first, second, grad in zip(weights, firsts, seconds, grads)
    ]
    new_weights = [entry[0] for entry in results]
    new_first = [entry[1] for entry in results]
    new_second = [entry[2] for entry in results]
    copies = [weight.astype(BF16) for weight in new_weights]
    return tuple(new_weights + new_first + new_second + copies + [grad_norm, loss_total, true_count])


def solution(mesh):
    split = (P(None, "dp"), P(None, "dp"), P(None, None, "dp"), P(None, "dp"), P(None, "dp"), P("dp"))
    in_specs = (P("dp", "seq", None),) + (P("dp", "seq"),) * 4 + (P("dp"),) + split * 3
    out_specs = split * 4 + (P(), P(), P())
    return jax.shard_map(local, mesh=mesh, in_specs=in_specs, out_specs=out_specs, check_vma=False)
```

```python
import functools

import jax
import jax.numpy as jnp
from jax import lax
from jax.experimental import pallas as pl
from jax.experimental.pallas import tpu as pltpu
from jax.sharding import PartitionSpec as P

STEP = 5
HIGH = lax.Precision.HIGHEST
NORM_EPS = 1e-06
CLIP = 0.01
LEARN = 0.02
DECAY = 0.1
BETA_ONE = 0.5
BETA_TWO = 0.5
ADAM_EPS = 1e-08
SCORE_SCALE = 0.125
MESH = pl.DeviceIdType.MESH
F32 = jnp.float32
BF16 = jnp.bfloat16
ANY = pl.BlockSpec(memory_space=pl.ANY)
VM = pl.BlockSpec(memory_space=pltpu.VMEM)

ROWS_YZ = 576
HALF_YZ = 288
QUARTER = 112
PART_ROWS = (32, 56, 40)
PART_BASE = (0, 256, 704)
ORDERS = ("xyz", "yzx", "zxy")


def place():
    dp = lax.axis_index("dp")
    sq = lax.axis_index("seq")
    core = lax.rem(dp, 2)
    y = lax.rem(dp // 2, 4)
    z = lax.rem(sq, 2) * 2 + dp // 8
    return sq // 2, y, z, core


def at(x, y, z, core):
    x, y, z = lax.rem(x + 4, 4), lax.rem(y + 4, 4), lax.rem(z + 4, 4)
    return (lax.rem(z, 2) * 8 + y * 2 + core, x * 2 + z // 2)


def greet(devices):
    bar = pltpu.get_barrier_semaphore()
    for device in devices:
        pl.semaphore_signal(bar, inc=1, device_id=device, device_id_type=MESH)
    pl.semaphore_wait(bar, len(devices))


def remote(src, dst, send, recv, device):
    return pltpu.make_async_remote_copy(
        src_ref=src, dst_ref=dst, send_sem=send, recv_sem=recv, device_id=device, device_id_type=MESH
    )


def params(collective_id, vmem=None):
    return pltpu.CompilerParams(
        collective_id=collective_id, has_side_effects=True, vmem_limit_bytes=vmem
    )


def pair_kernel(n, *refs):
    ins, outs = refs[:n], refs[n : 2 * n]
    ss, rs = refs[2 * n :]
    x, y, z, c = place()
    mate = at(x, y, z, 1 - c)
    greet([mate])
    cps = []
    for i in range(n):
        cps.append(remote(ins[i], outs[i].at[c], ss.at[i], rs.at[i], mate))
    for cp in cps:
        cp.start()
    for i in range(n):
        outs[i][c] = ins[i][...]
    for cp in cps:
        cp.wait()


def pair_gather(cid, *arrays):
    n = len(arrays)
    return pl.pallas_call(
        functools.partial(pair_kernel, n),
        out_shape=tuple(jax.ShapeDtypeStruct((2,) + a.shape, a.dtype) for a in arrays),
        in_specs=[VM] * n,
        out_specs=(VM,) * n,
        scratch_shapes=[pltpu.SemaphoreType.DMA((n,))] * 2,
        compiler_params=params(cid, 32 * 2**20),
    )(*arrays)


def swap_kernel(a, o, got, ss, rs):
    x, y, z, c = place()
    mate = at(x, y, z, 1 - c)
    greet([mate])
    cp = remote(a.at[1 - c], got, ss, rs, mate)
    cp.start()
    cp.wait()
    o[...] = a[c] + got[...]


def swap_add(cid, a):
    return pl.pallas_call(
        swap_kernel,
        out_shape=jax.ShapeDtypeStruct(a.shape[1:], a.dtype),
        in_specs=[VM],
        out_specs=VM,
        scratch_shapes=[
            pltpu.VMEM(a.shape[1:], a.dtype),
            pltpu.SemaphoreType.DMA,
            pltpu.SemaphoreType.DMA,
        ],
        compiler_params=params(cid, 32 * 2**20),
    )(a)


def group_peers():
    dp = lax.axis_index("dp")
    sq = lax.axis_index("seq")
    core = lax.rem(dp, 2)
    out = [(dp + 1 - 2 * core, sq)]
    for i in range(1, 8):
        for flip in range(2):
            out.append((dp + flip * (1 - 2 * core), lax.rem(sq + i, 8)))
    return out


def a2a_kernel(a, o, ss, rs, loc):
    dp = lax.axis_index("dp")
    sq = lax.axis_index("seq")
    peers = [(dp, lax.rem(sq + i, 8)) for i in range(1, 8)]
    greet(peers)
    own = pltpu.make_async_copy(a.at[sq], o.at[sq], loc)
    own.start()
    cps = []
    for i in range(1, 8):
        to = lax.rem(sq + i, 8)
        cp = remote(a.at[to], o.at[sq], ss.at[i], rs.at[i], (dp, to))
        cp.start()
        cps.append(cp)
    own.wait()
    for cp in cps:
        cp.wait()


def all_to_all(cid, a):
    return pl.pallas_call(
        a2a_kernel,
        out_shape=jax.ShapeDtypeStruct(a.shape, a.dtype),
        in_specs=[ANY],
        out_specs=ANY,
        scratch_shapes=[
            pltpu.SemaphoreType.DMA((8,)),
            pltpu.SemaphoreType.DMA((8,)),
            pltpu.SemaphoreType.DMA,
        ],
        compiler_params=params(cid),
    )(a)


def head_lanes(pair, core):
    return pl.ds(pl.multiple_of(((pair // 2 * 2 + core) * 2 + lax.rem(pair, 2)) * 128, 128), 128)


def to_tokens_kernel(a, o, ss, rs, loc):
    dp = lax.axis_index("dp")
    sq = lax.axis_index("seq")
    core = lax.rem(dp, 2)
    base = dp - core
    pair, owner = sq // 2, lax.rem(sq, 2)
    greet(group_peers())
    lanes = head_lanes(pair, core)

    def copy(i):
        to = lax.rem(sq + i, 8)
        return remote(
            a.at[to], o.at[:, lanes], ss.at[i], rs.at[pair, core], (base + owner, to)
        )

    for i in range(1, 8):
        copy(i).start()
    own = pltpu.make_async_copy(a.at[sq], o.at[:, lanes], loc)

    @pl.when(owner == core)
    def _():
        own.start()

    @pl.when(owner != core)
    def _():
        copy(0).start()

    for p in range(4):
        for q in range(2):
            view = o.at[:, pl.ds(((p // 2 * 2 + q) * 2 + p % 2) * 128, 128)]

            @pl.when(jnp.logical_or(sq != p * 2 + core, core != q))
            def _():
                remote(view, view, ss.at[0], rs.at[p, q], (base + owner, sq)).wait_recv()

    for i in range(1, 8):
        copy(i).wait_send()

    @pl.when(owner == core)
    def _():
        own.wait()

    @pl.when(owner != core)
    def _():
        copy(0).wait_send()


def to_tokens(cid, a):
    return pl.pallas_call(
        to_tokens_kernel,
        out_shape=jax.ShapeDtypeStruct((256, 1024), a.dtype),
        in_specs=[ANY],
        out_specs=ANY,
        scratch_shapes=[
            pltpu.SemaphoreType.DMA((8,)),
            pltpu.SemaphoreType.DMA((4, 2)),
            pltpu.SemaphoreType.DMA,
        ],
        compiler_params=params(cid),
    )(a)


def to_heads_kernel(a, o, ss, rs, loc):
    dp = lax.axis_index("dp")
    sq = lax.axis_index("seq")
    core = lax.rem(dp, 2)
    base = dp - core
    pair, owner = sq // 2, lax.rem(sq, 2)
    greet(group_peers())
    own = pltpu.make_async_copy(a.at[:, head_lanes(pair, core)], o.at[sq], loc)

    def each(fn):
        for p in range(4):
            for q in range(2):
                view = a.at[:, pl.ds(((p // 2 * 2 + q) * 2 + p % 2) * 128, 128)]
                to = (base + q, p * 2 + core)
                cp = remote(view, o.at[sq], ss.at[p, q], rs.at[sq], to)
                here = jnp.logical_and(sq == p * 2 + core, core == q)
                fn(cp, here)

    def start(cp, here):
        @pl.when(jnp.logical_not(here))
        def _():
            cp.start()

    def finish(cp, here):
        @pl.when(jnp.logical_not(here))
        def _():
            cp.wait_send()

    each(start)

    @pl.when(owner == core)
    def _():
        own.start()

    for i in range(8):
        view = o.at[i]

        @pl.when(jnp.logical_or(sq != i, owner != core))
        def _():
            remote(view, view, ss.at[0, 0], rs.at[i], (base, sq)).wait_recv()

    each(finish)

    @pl.when(owner == core)
    def _():
        own.wait()


def to_heads(cid, a):
    return pl.pallas_call(
        to_heads_kernel,
        out_shape=jax.ShapeDtypeStruct((8, 256, 128), a.dtype),
        in_specs=[ANY],
        out_specs=ANY,
        scratch_shapes=[
            pltpu.SemaphoreType.DMA((4, 2)),
            pltpu.SemaphoreType.DMA((8,)),
            pltpu.SemaphoreType.DMA,
        ],
        compiler_params=params(cid),
    )(a)


NT = (((1,), (1,)), ((), ()))


def normalize(v):
    center = v - jnp.mean(v, -1, keepdims=True)
    spread = jnp.mean(center * center, -1, keepdims=True)
    return center * lax.rsqrt(spread + NORM_EPS)


def ada_row(ada, k, img):
    return jnp.concatenate([ada[2 * k, img : img + 1, :], ada[2 * k + 1, img : img + 1, :]], axis=1)


def column_of(row):
    return jnp.transpose(jnp.broadcast_to(row, (128, 128)))


def forward_kernel(
    msg, slots, table, cond_w, x_in, s,
    msg_all, slots_all, cond_all, emb_out, ada, loss_out,
    w_o, wo_o, h1_o, h2_o, h3_o, hb_o, ot_o, att_o, x1_o, mlp_o, x2_o, f_o, u_o, dl_o,
    w, wo, h1, h2, h3, src, hb, oh, ot, att, x1, mlp, x2, acc, got_acc, f, u, dl,
    cond_own, ada_own, bias, qcol, tcol, wcol, stats,
    gs, gr, gl, os, orr, s1, r1, s2, r2, s3, r3, s4, r4, ps, pr, as_, ar, al, ts, tr, tl, outs_sem,
):
    x, y, z, c = place()
    dp = lax.axis_index("dp")
    sq = lax.axis_index("seq")
    zl = lax.rem(z, 2)
    up, down, far = lax.rem(y + 1, 4), lax.rem(y + 3, 4), lax.rem(y + 2, 4)
    yp, ym = at(x, y + 1, z, c), at(x, y - 1, z, c)
    zp, zm = at(x, y, z + 1, c), at(x, y, z - 1, c)
    xp, xm = at(x + 1, y, z, c), at(x - 1, y, z, c)
    zs = at(x, y, z + 1 - 2 * c, c)
    mate = at(x, y, z, 1 - c)
    base = dp - c
    row = [(lax.rem(dp + i, 16), sq) for i in range(1, 16)]
    group = group_peers()
    greet(row + group[1:] + [at(x, y, z + 2 * zl - 1, c)])

    pending = []

    def keep(k, src_ref, dst_ref):
        cp = pltpu.make_async_copy(src_ref, dst_ref, outs_sem.at[k])
        cp.start()
        pending.append(cp)
        return cp

    def quarter(pos):
        return pl.ds(pl.multiple_of(ROWS_YZ + QUARTER * lax.rem(pos + 4, 4), 16), QUARTER)

    mine = quarter(x)
    full, first, second = pl.ds(0, ROWS_YZ), pl.ds(0, HALF_YZ), pl.ds(HALF_YZ, HALF_YZ)
    sent = []

    def go(j, k, a, b, device):
        cp = remote(a, b, gs.at[j, k], gr.at[j, k], device)
        cp.start()
        sent.append(cp)

    def got(j, k, ref):
        remote(ref, ref, gs.at[j, k], gr.at[j, k], mate).wait_recv()

    def stage(kind, j):
        if kind == "A":
            go(j, 0, s.at[j, full], w.at[zl, y, j, full], yp)
            go(j, 1, s.at[j, full], w.at[zl, y, j, full], ym)
            go(j, 6, s.at[j, mine], w.at[zl, y, j, mine], zs)
            for i, rows in enumerate((full, mine)):
                pltpu.make_async_copy(s.at[j, rows], w.at[zl, y, j, rows], gl.at[j, i]).start()
        if kind == "B":
            for i, rows in enumerate((full, mine)):
                pltpu.make_async_copy(s.at[j, rows], w.at[zl, y, j, rows], gl.at[j, i]).wait()
            got(j, 6, w.at[1 - zl, y, j, mine])
            go(j, 7, w.at[:, y, j, mine], w.at[:, y, j, mine], yp)
            go(j, 8, w.at[:, y, j, mine], w.at[:, y, j, mine], ym)
            got(j, 0, w.at[zl, down, j, full])
            got(j, 1, w.at[zl, up, j, full])
            go(j, 2, w.at[zl, down, j, first], w.at[zl, down, j, first], yp)
            go(j, 3, w.at[zl, up, j, second], w.at[zl, up, j, second], ym)
        if kind == "C":
            got(j, 7, w.at[:, down, j, mine])
            got(j, 8, w.at[:, up, j, mine])
            go(j, 9, w.at[0, down, j, mine], w.at[0, down, j, mine], yp)
            go(j, 10, w.at[1, up, j, mine], w.at[1, up, j, mine], ym)
            got(j, 2, w.at[zl, far, j, first])
            got(j, 3, w.at[zl, far, j, second])
            go(j, 4, w.at[zl, :, j, first], w.at[zl, :, j, first], zp)
            go(j, 5, w.at[zl, :, j, second], w.at[zl, :, j, second], zm)
        if kind == "D":
            got(j, 9, w.at[0, far, j, mine])
            got(j, 10, w.at[1, far, j, mine])
            go(j, 11, w.at[:, :, j, mine], w.at[:, :, j, mine], xp)
            go(j, 12, w.at[:, :, j, mine], w.at[:, :, j, mine], xm)
        if kind == "E":
            left, right = quarter(x - 1), quarter(x + 1)
            got(j, 11, w.at[:, :, j, left])
            got(j, 12, w.at[:, :, j, right])
            go(j, 13, w.at[0, :, j, left], w.at[0, :, j, left], xp)
            go(j, 14, w.at[1, :, j, right], w.at[1, :, j, right], xm)
        if kind == "F":
            across = quarter(x + 2)
            got(j, 4, w.at[1 - zl, :, j, first])
            got(j, 5, w.at[1 - zl, :, j, second])
            got(j, 13, w.at[0, :, j, across])
            got(j, 14, w.at[1, :, j, across])
            keep(j, w.at[:, :, j], w_o.at[:, :, j])
            if j == 0:
                for i in range(2):
                    remote(w.at[1, 2 + i, 0], wo.at[2 * i + c], os.at[i], orr.at[i], mate).start()
                    pltpu.make_async_copy(w.at[1, 2 + i, 0], wo.at[2 * i + c], gl.at[i, 2]).start()

    wave = [
        "A0 A1", "B0 A2", "C0 B1 A3", "D0 C1 B2", "E0 D1 C2 B3", "F0 E1 D2 C3", "E2 D3", "E3", "F1", "F2", "F3"
    ]

    def pump(n=1):
        for _ in range(n):
            if wave:
                for item in wave.pop(0).split():
                    stage(item[0], int(item[1]))

    pump()
    firsts = []
    for i, to in enumerate(row):
        cp = remote(msg, msg_all.at[dp], s1.at[i], r1.at[i], to)
        cp.start()
        firsts.append(cp)
    msg_all[dp] = msg[...]
    for cp in firsts:
        cp.wait()
    seen = msg_all[...]
    count = jnp.sum(seen[:, 10, 2:3], axis=0, keepdims=True)
    slots[8:9, :] = jnp.broadcast_to(count, (1, 128))
    for d in range(16):
        bias[pl.ds(10 * d, 10), :] = seen[d, 0:10, :]
    seconds = []
    for i, to in enumerate(group):
        cp = remote(slots, slots_all.at[sq * 2 + c], s2.at[i], r2.at[i], to)
        cp.start()
        seconds.append(cp)
    slots_all[sq * 2 + c] = slots[...]
    classes = table.shape[0]
    lane = lax.broadcasted_iota(jnp.int32, (32, classes), 1)
    labels = jnp.concatenate([seen[d, 10:11, i : i + 1] for d in range(16) for i in range(2)], axis=0)
    hit = jnp.where(lane == labels.astype(jnp.int32), 1.0, 0.0).astype(BF16)
    emb = jnp.dot(hit, table[...], preferred_element_type=F32)
    emb_out[...] = emb
    cond_own[...] = (emb / (1.0 + jnp.exp(-emb))).astype(BF16)
    cond_all[dp] = cond_own[...]
    thirds = []
    for i, to in enumerate(row):
        cp = remote(cond_own, cond_all.at[dp], s3.at[i], r3.at[i], to)
        cp.start()
        thirds.append(cp)
    pump()
    for cp in thirds:
        cp.wait()
    total = jnp.zeros((32, 512), F32)
    for d in range(16):
        total += jnp.dot(cond_all[d], cond_w[pl.ds(64 * d, 64), :], preferred_element_type=F32)
    total += jnp.concatenate([bias[pl.ds(dp * 4 + i, 1), :] for i in range(4)], axis=1)
    for d in range(16):
        ada_own[d] = total[2 * d : 2 * d + 2]
    fourths = []
    for i in range(15):
        to = lax.rem(dp + 1 + i, 16)
        cp = remote(ada_own.at[to], ada.at[dp], s4.at[i], r4.at[i], (to, sq))
        cp.start()
        fourths.append(cp)
    ada[dp] = ada_own[dp]
    pump()
    for cp in fourths:
        cp.wait()
    for cp in seconds:
        cp.wait()

    owner = lax.rem(sq, 2)
    for img in range(2):
        for g in range(8):
            qcol[img, g] = column_of(slots_all[g * 2 + owner, pl.ds(2 + img, 1), :])
        for q in range(2):
            at_rows = pl.ds((q * 2 + img) * 128, 128)
            tcol[at_rows, :] = column_of(slots_all[sq * 2 + q, pl.ds(4 + img, 1), :])
            wcol[at_rows, :] = column_of(slots_all[sq * 2 + q, pl.ds(6 + img, 1), :])
    true_count = jnp.sum(
        jnp.concatenate([slots_all[2 * g, 8:9, 0:1] for g in range(8)], axis=0), axis=0, keepdims=True
    )

    def blocks(fn):
        for img in range(2):
            def body(i, carry, img=img):
                fn(img, pl.ds(pl.multiple_of(img * 128 + i * 32, 32), 32))
                return carry
            lax.fori_loop(0, 4, body, 0)

    def exchange(k, ref):
        cp = remote(ref.at[c], ref.at[c], ps.at[k], pr.at[k], mate)
        cp.start()
        return cp

    def modulated(img, v, scale, shift):
        return (normalize(v) * (1.0 + ada_row(ada, scale, img)) + ada_row(ada, shift, img)).astype(BF16)

    def do_h1(img, rows):
        h1[c, rows, :] = modulated(img, x_in[rows, :].astype(F32), 2, 4)

    blocks(do_h1)
    cp = exchange(0, h1)
    pump()
    cp.wait()
    keep(4, h1, h1_o)
    pump(2)

    def bias_row(start):
        return jnp.concatenate([bias[pl.ds(start, 1), :], bias[pl.ds(start + 1, 1), :]], axis=1)

    tokens = h1[...].reshape(512, 1024)
    for j in range(6):
        t, jj = j // 2, j % 2
        val = jnp.dot(tokens, w[j // 4, j % 4, 0], preferred_element_type=F32)
        if t != 1:
            val = val + bias_row(64 + (0 if t == 0 else 8) + (2 * jj + c) * 2)
        val = val.astype(BF16)
        for half in range(2):
            for ip in range(2):
                src[(jj * 2 + half) * 2 + ip, t] = val[
                    ip * 256 : ip * 256 + 256, half * 128 : half * 128 + 128
                ].reshape(2, 128, 128)
    cps = []
    for i in range(1, 8):
        to = lax.rem(sq + i, 8)
        cp = remote(src.at[to], hb.at[sq], as_.at[i], ar.at[i], (dp, to))
        cp.start()
        cps.append(cp)
    hb[sq] = src[sq]
    pump(2)
    for cp in cps:
        cp.wait()
    keep(5, hb, hb_o)

    low_lanes = lax.broadcasted_iota(jnp.int32, (256, 128), 1) < 64

    def attend_block(i, carry):
        img, qb = i // 4, lax.rem(i, 4)
        q = jnp.concatenate([hb[2 * qb, 0, img], hb[2 * qb + 1, 0, img]], axis=0)
        k = jnp.concatenate([hb[g, 1, img] for g in range(8)], axis=0)
        v = jnp.concatenate([hb[g, 2, img] for g in range(8)], axis=0)
        key = jnp.concatenate([slots_all[g * 2 + owner, pl.ds(img, 1), :] for g in range(8)], axis=1)
        query = jnp.concatenate([qcol[img, 2 * qb], qcol[img, 2 * qb + 1]], axis=0)[:, 0:1]
        seen_by = key <= query
        heads = []
        for h in range(2):
            mask = low_lanes if h == 0 else jnp.logical_not(low_lanes)
            qh = jnp.where(mask, q, jnp.zeros_like(q))
            sc = lax.dot_general(qh, k, NT, preferred_element_type=F32) * SCORE_SCALE
            sc = jnp.where(seen_by, sc, -1e30)
            e = jnp.exp(sc - jnp.max(sc, axis=-1, keepdims=True))
            p = (e / jnp.sum(e, axis=-1, keepdims=True)).astype(BF16)
            heads.append(jnp.dot(p, v, preferred_element_type=F32))
        o = jnp.where(low_lanes, heads[0], heads[1]).astype(BF16)
        oh[2 * qb, img] = o[:128]
        oh[2 * qb + 1, img] = o[128:]
        return carry

    lax.fori_loop(0, 8, attend_block, 0)
    pair = sq // 2
    lanes = head_lanes(pair, c)

    def o_copy(i, img):
        to = lax.rem(sq + i, 8)
        return remote(
            oh.at[to, img], ot.at[pl.ds(img * 128, 128), lanes], ts.at[i, img], tr.at[pair, c, img],
            (base + owner, to),
        )

    for img in range(2):
        for i in range(1, 8):
            o_copy(i, img).start()

        @pl.when(owner == c)
        def _():
            ot[pl.ds(img * 128, 128), lanes] = oh[sq, img]

        @pl.when(owner != c)
        def _():
            o_copy(0, img).start()

    pump()
    for img in range(2):
        for p in range(4):
            for q in range(2):
                view = ot.at[pl.ds(img * 128, 128), pl.ds(((p // 2 * 2 + q) * 2 + p % 2) * 128, 128)]

                @pl.when(jnp.logical_or(sq != p * 2 + c, c != q))
                def _():
                    remote(view, view, ts.at[0, img], tr.at[p, q, img], mate).wait_recv()

    keep(6, ot, ot_o)
    for i in range(2):
        remote(w.at[1, 2 + i, 0], wo.at[2 * i + c], os.at[i], orr.at[i], mate).wait()
        pltpu.make_async_copy(w.at[1, 2 + i, 0], wo.at[2 * i + c], gl.at[i, 2]).wait()
    keep(7, wo, wo_o)
    for k in range(4):
        cols = pl.ds(256 * k, 256)
        att[:, cols] = jnp.dot(ot[...], wo[k], preferred_element_type=F32) + bias_row(80 + 2 * k)
    keep(8, att, att_o)

    def do_h2(img, rows):
        v = x_in[rows, :].astype(F32) + ada_row(ada, 0, img) * att[rows, :]
        x1[rows, :] = v
        h2[c, rows, :] = modulated(img, v, 3, 5)

    blocks(do_h2)
    cp = exchange(1, h2)
    keep(9, x1, x1_o)
    pump(20)
    cp.wait()
    keep(10, h2, h2_o)

    def chunk(ref, j, kind):
        return ref[j // 4, lax.rem(j, 4), kind]

    def do_f(j, carry):
        val = jnp.dot(h2[...].reshape(512, 1024), chunk(w, j, 1), preferred_element_type=F32)
        val = val + bias_row(88 + (2 * j + c) * 2)
        f[j] = val
        act = jax.nn.gelu(val, approximate=True).astype(BF16)
        u[j] = act
        part = lax.dot_general(act, chunk(w, j, 2), NT, preferred_element_type=F32).reshape(2, 256, 1024)

        @pl.when(j == 0)
        def _():
            acc[...] = part

        @pl.when(j > 0)
        def _():
            acc[...] += part

        return carry

    lax.fori_loop(0, 8, do_f, 0)
    f_copy = keep(11, f, f_o)
    keep(12, u, u_o)
    cp = remote(acc.at[1 - c], got_acc, ps.at[2], pr.at[2], mate)
    cp.start()
    b_two = jnp.concatenate([bias[pl.ds(120 + i, 1), :] for i in range(8)], axis=1)
    cp.wait()

    def do_h3(img, rows):
        m = acc[c, rows, :] + got_acc[rows, :] + b_two
        mlp[rows, :] = m
        v = x1[rows, :] + ada_row(ada, 1, img) * m
        x2[rows, :] = v
        h3[c, rows, :] = modulated(img, v, 6, 7)

    blocks(do_h3)
    cp = exchange(3, h3)
    keep(13, mlp, mlp_o)
    keep(14, x2, x2_o)
    f_copy.wait()
    pending[:] = [p for p in pending if p is not f_copy]
    cp.wait()
    keep(15, h3, h3_o)

    def do_logits(j, top):
        val = jnp.dot(h3[...].reshape(512, 1024), chunk(w, j, 3), preferred_element_type=F32)
        val = val + bias_row(128 + (2 * j + c) * 2)
        f[j] = val
        return jnp.maximum(top, jnp.max(val, axis=-1, keepdims=True))

    top = lax.fori_loop(0, 8, do_logits, jnp.full((512, 1), -jnp.inf, F32))
    inner = lax.broadcasted_iota(jnp.int32, (512, 256), 1)

    def target_hit(j):
        return inner == (tcol[:, 0:1].astype(jnp.int32) - (2 * j + c) * 256)

    def do_mass(j, carry):
        mass, picked = carry
        val = f[j]
        mass = mass + jnp.sum(jnp.exp(val - top), axis=-1, keepdims=True)
        picked = picked + jnp.sum(jnp.where(target_hit(j), val, 0.0), axis=-1, keepdims=True)
        return mass, picked

    zero = jnp.zeros((512, 1), F32)
    mass, picked = lax.fori_loop(0, 8, do_mass, (zero, zero))
    lane = lax.broadcasted_iota(jnp.int32, (512, 128), 1)
    stats[c] = jnp.where(lane == 0, top, jnp.where(lane == 1, mass, picked))
    cp = exchange(4, stats)
    cp.wait()
    both = [stats[0], stats[1]]
    top_all = jnp.maximum(both[0][:, 0:1], both[1][:, 0:1])
    mass_all = sum(b[:, 1:2] * jnp.exp(b[:, 0:1] - top_all) for b in both)
    log_total = top_all + jnp.log(mass_all)
    weight = wcol[:, 0:1]
    losses = weight * (log_total - (both[0][:, 2:3] + both[1][:, 2:3]))
    loss_out[...] = jnp.broadcast_to(0.5 * jnp.sum(losses, axis=0, keepdims=True), (8, 128))
    share = weight / true_count

    def do_dlogits(j, carry):
        grad = share * (jnp.exp(f[j] - log_total) - jnp.where(target_hit(j), 1.0, 0.0))
        dl[j] = grad.astype(BF16)
        return carry

    lax.fori_loop(0, 8, do_dlogits, 0)
    keep(16, dl, dl_o)
    for img in range(2):
        for i in range(1, 8):
            o_copy(i, img).wait_send()

        @pl.when(owner != c)
        def _():
            o_copy(0, img).wait_send()

    for cp in sent:
        cp.wait_send()
    for cp in pending:
        cp.wait()


def forward_pass(msg, slots, table, cond_w, x_rows, shard):
    dma = pltpu.SemaphoreType.DMA
    sd = jax.ShapeDtypeStruct
    kept = [
        sd((2, 4, 4, 1024, 256), BF16), sd((4, 1024, 256), BF16),
        sd((2, 256, 1024), BF16), sd((2, 256, 1024), BF16), sd((2, 256, 1024), BF16),
        sd((8, 3, 2, 128, 128), BF16), sd((256, 1024), BF16),
        sd((256, 1024), F32), sd((256, 1024), F32), sd((256, 1024), F32), sd((256, 1024), F32),
        sd((8, 512, 256), F32), sd((8, 512, 256), BF16), sd((8, 512, 256), BF16),
    ]
    vm = pltpu.VMEM
    return pl.pallas_call(
        forward_kernel,
        out_shape=[
            sd((16, 16, 128), F32), sd((16, 16, 128), F32), sd((16, 32, 64), BF16),
            sd((32, 64), F32), sd((16, 2, 512), F32), sd((8, 128), F32),
        ] + kept,
        in_specs=[VM] * 5 + [ANY],
        out_specs=[VM] * 6 + [ANY] * len(kept),
        scratch_shapes=[
            vm((2, 4, 4, 1024, 256), BF16), vm((4, 1024, 256), BF16),
            vm((2, 256, 1024), BF16), vm((2, 256, 1024), BF16), vm((2, 256, 1024), BF16),
            vm((8, 3, 2, 128, 128), BF16), vm((8, 3, 2, 128, 128), BF16), vm((8, 2, 128, 128), BF16),
            vm((256, 1024), BF16),
            vm((256, 1024), F32), vm((256, 1024), F32), vm((256, 1024), F32), vm((256, 1024), F32),
            vm((2, 256, 1024), F32), vm((256, 1024), F32),
            vm((8, 512, 256), F32), vm((8, 512, 256), BF16), vm((8, 512, 256), BF16),
            vm((32, 64), BF16), vm((16, 2, 512), F32), vm((160, 128), F32),
            vm((2, 8, 128, 128), F32), vm((512, 128), F32), vm((512, 128), F32), vm((2, 512, 128), F32),
            dma((4, 15)), dma((4, 15)), dma((4, 3)), dma((2,)), dma((2,)),
            dma((15,)), dma((15,)), dma((15,)), dma((15,)), dma((15,)), dma((15,)), dma((15,)), dma((15,)),
            dma((5,)), dma((5,)), dma((8,)), dma((8,)), dma,
            dma((8, 2)), dma((4, 2, 2)), dma, dma((17,)),
        ],
        compiler_params=params(0, 63 * 2**20),
    )(msg, slots, table, cond_w, x_rows, shard)


def small_kernel(
    msg, cond_w, ada_all, bias_sum, dcond,
    got, mine, all_seq, part, back, s1, r1, s2, r2, s3, r3,
):
    dp = lax.axis_index("dp")
    sq = lax.axis_index("seq")
    row = [lax.rem(dp + i, 16) for i in range(1, 16)]
    line = [lax.rem(sq + i, 8) for i in range(1, 8)]
    greet([(d, sq) for d in row] + [(dp, s) for s in line])
    cps = []
    for i, d in enumerate(row):
        cp = remote(msg.at[d], got.at[dp], s1.at[i], r1.at[i], (d, sq))
        cp.start()
        cps.append(cp)
    got[dp] = msg[dp]
    for cp in cps:
        cp.wait()
    seen = got[...]
    for d in range(16):
        mine[d] = seen[d, :8, :]
    rest = jnp.sum(seen[:, 8:24, :], axis=0)
    mine[16] = rest[:8]
    mine[17] = rest[8:]
    cps = []
    for i, s in enumerate(line):
        cp = remote(mine, all_seq.at[sq], s2.at[i], r2.at[i], (dp, s))
        cp.start()
        cps.append(cp)
    all_seq[sq] = mine[...]
    for cp in cps:
        cp.wait()
    total = jnp.sum(all_seq[...], axis=0)
    bias_sum[0] = total[16]
    bias_sum[1] = total[17]
    rows = []
    for d in range(16):
        for i in range(2):
            rows.append(
                jnp.concatenate([total[d, 4 * i + k : 4 * i + k + 1, :] for k in range(4)], axis=1)
            )
    dada = jnp.concatenate(rows, axis=0)
    ada_all[...] = dada
    for d in range(16):
        part[d] = lax.dot_general(
            dada, cond_w[pl.ds(64 * d, 64), :].astype(F32), (((1,), (1,)), ((), ())),
            precision=HIGH, preferred_element_type=F32,
        )
    cps = []
    for i, d in enumerate(row):
        cp = remote(part.at[d], back.at[dp], s3.at[i], r3.at[i], (d, sq))
        cp.start()
        cps.append(cp)
    back[dp] = part[dp]
    for cp in cps:
        cp.wait()
    dcond[...] = jnp.sum(back[...], axis=0)


def small_reduce(msg, cond_w):
    dma = pltpu.SemaphoreType.DMA
    return pl.pallas_call(
        small_kernel,
        out_shape=(
            jax.ShapeDtypeStruct((32, 512), F32),
            jax.ShapeDtypeStruct((2, 8, 128), F32),
            jax.ShapeDtypeStruct((32, 64), F32),
        ),
        in_specs=[VM] * 2,
        out_specs=(VM,) * 3,
        scratch_shapes=[
            pltpu.VMEM((16, 24, 128), F32),
            pltpu.VMEM((18, 8, 128), F32),
            pltpu.VMEM((8, 18, 8, 128), F32),
            pltpu.VMEM((16, 32, 64), F32),
            pltpu.VMEM((16, 32, 64), F32),
        ]
        + [dma((15,))] * 6,
        compiler_params=params(2),
    )(msg, cond_w)


def pick(ref, x, y, z, extra=()):
    everything = slice(None)
    zl = everything if z is None else lax.rem(z, 2)
    zh = everything if z is None else z // 2
    return (
        zl,
        everything if y is None else y,
        everything if x is None else x,
        zh,
    )


def halves(order, phase, rows):
    axis = order[phase]
    later = order[phase + 1 :]
    if axis != "z" and "z" in later:
        return ("zl", slice(0, 1), slice(1, 2))
    if "y" in later:
        return ("y", slice(0, 2), slice(2, 4))
    if "x" in later:
        return ("x", slice(0, 2), slice(2, 4))
    cut = (rows // 16) * 8 if (rows // 16) * 16 == rows else (rows // 16) * 8 + 8
    return ("r", slice(0, cut), slice(cut, rows))


def cut_size(part, phase):
    order, rows = ORDERS[part], PART_ROWS[part]
    axis, later = order[phase], order[phase + 1 :]
    dims = {
        "zl": 2 if "z" in later else 1,
        "y": 4 if "y" in later else 1,
        "x": 4 if "x" in later else 1,
        "zh": 2 if "z" in later else 1,
        "r": rows,
    }
    return dims


def reduce_kernel(*refs):
    gs = refs[0:4]
    extra, out, norm = refs[4:7]
    pos = 7
    parts = [refs[pos + 3 * slot : pos + 3 * slot + 3] for slot in range(2)]
    pos += 6
    recv = {}
    for p in range(3):
        for ph in range(3):
            recv[p, ph] = refs[pos : pos + 4]
            pos += 4
    ss, rs, loc, gss, grs, oloc, tile, tiles, nss, nrs = refs[pos:]

    x, y, z, c = place()
    zl, zh = lax.rem(z, 2), z // 2
    here = {"x": x, "y": y, "z": z}

    def step(axis, by):
        q = dict(here)
        q[axis] = q[axis] + by
        return at(q["x"], q["y"], q["z"], c)

    mate = at(x, y, z, 1 - c)
    greet([step(a, b) for a in "xyz" for b in (1, 2, 3)] + [mate])

    def view(ref, p, ph, index, half=None):
        order = ORDERS[p]
        sel = {}
        for i, a in enumerate(order):
            if i < ph:
                sel[a] = here[a]
            elif i == ph:
                sel[a] = lax.rem(index + 4, 4)
            else:
                sel[a] = None
        idx = {
            "zl": slice(0, 2) if sel["z"] is None else pl.ds(lax.rem(sel["z"], 2), 1),
            "y": slice(0, 4) if sel["y"] is None else pl.ds(sel["y"], 1),
            "x": slice(0, 4) if sel["x"] is None else pl.ds(sel["x"], 1),
            "zh": slice(0, 2) if sel["z"] is None else pl.ds(sel["z"] // 2, 1),
            "r": slice(0, PART_ROWS[p]),
        }
        if half is not None:
            name, one, two = halves(order, ph, PART_ROWS[p])
            idx[name] = (one, two)[half]
        return ref.at[idx["zl"], idx["y"], idx["x"], idx["zh"], idx["r"]]

    def add(dst, srcs):
        dims = dst.shape[:4]
        total = dims[0] * dims[1] * dims[2] * dims[3]

        def body(i, carry):
            d = lax.rem(i, dims[3])
            i2 = i // dims[3]
            cc = lax.rem(i2, dims[2])
            i3 = i2 // dims[2]
            b = lax.rem(i3, dims[1])
            a = i3 // dims[1]
            acc = dst[a, b, cc, d]
            for s in srcs:
                acc = acc + s[a, b, cc, d]
            dst[a, b, cc, d] = acc
            return carry

        lax.fori_loop(0, total, body, 0)

    sent = []

    def job(j):
        slot = j % 2
        loads = []
        for p in range(3):
            r = PART_ROWS[p]
            for xi in range(4):
                for zi in range(2):
                    src = gs[j].at[:, :, pl.ds(PART_BASE[p] + (xi * 2 + zi) * r, r)]
                    cp = pltpu.make_async_copy(src, parts[slot][p].at[:, :, xi, zi], loc.at[slot, p, xi * 2 + zi])
                    cp.start()
                    loads.append(cp)
        yield
        for cp in loads:
            cp.wait()
        mine = []

        def go(p, ph, k, src, dst, device):
            cp = remote(src, dst, ss.at[j, p * 3 + ph, k], rs.at[j, p * 3 + ph, k], device)
            cp.start()
            mine.append(cp)

        def got(p, ph, k, ref):
            remote(ref, ref, ss.at[j, p * 3 + ph, k], rs.at[j, p * 3 + ph, k], mate).wait_recv()

        for ph in range(3):
            for p in range(3):
                a = ORDERS[p][ph]
                i = here[a]
                g = parts[slot][p]
                bufs = [b.at[j] for b in recv[p, ph]]
                go(p, ph, 0, view(g, p, ph, i + 2, 0), bufs[0], step(a, 1))
                go(p, ph, 1, view(g, p, ph, i + 2, 1), bufs[1], step(a, -1))
            yield
            for p in range(3):
                a = ORDERS[p][ph]
                i = here[a]
                g = parts[slot][p]
                bufs = [b.at[j] for b in recv[p, ph]]
                got(p, ph, 0, bufs[0])
                add(view(g, p, ph, i + 1, 0), [bufs[0]])
                got(p, ph, 1, bufs[1])
                add(view(g, p, ph, i - 1, 1), [bufs[1]])
                go(p, ph, 2, view(g, p, ph, i + 1), bufs[2], step(a, 1))
                go(p, ph, 3, view(g, p, ph, i - 1), bufs[3], step(a, -1))
            yield
            for p in range(3):
                a = ORDERS[p][ph]
                i = here[a]
                g = parts[slot][p]
                bufs = [b.at[j] for b in recv[p, ph]]
                got(p, ph, 2, bufs[2])
                got(p, ph, 3, bufs[3])
                add(view(g, p, ph, i), [bufs[2], bufs[3]])
        outs = []
        for p in range(3):
            r = PART_ROWS[p]
            piece = parts[slot][p].at[zl, y, x, zh]
            val = piece[...]
            sq = val * val
            acc = tile[...]
            for t in range(r // 8):
                for u in range(2):
                    acc = acc + sq[8 * t : 8 * t + 8, 128 * u : 128 * u + 128]
            tile[...] = acc
            rows = pl.ds(pl.multiple_of(PART_BASE[p] + (x * 2 + zh) * r, 8), r)
            cp = pltpu.make_async_copy(piece, out.at[j, rows], oloc.at[j, p])
            cp.start()
            outs.append(cp)
            cp = remote(piece, out.at[j, rows], gss.at[j, p, 0], grs.at[j, p, 0], step("z", 2))
            cp.start()
            mine.append(cp)
        yield
        for cp in outs:
            cp.wait()

        def rows_of(p, xi, zi, n):
            r = PART_ROWS[p]
            return pl.ds(pl.multiple_of(PART_BASE[p] + (lax.rem(xi + 4, 4) * 2 + zi) * r, 8), n * r)

        def ago(p, k, rows, device):
            cp = remote(out.at[j, rows], out.at[j, rows], gss.at[j, p, k], grs.at[j, p, k], device)
            cp.start()
            mine.append(cp)

        def agot(p, k, rows):
            ref = out.at[j, rows]
            remote(ref, ref, gss.at[j, p, k], grs.at[j, p, k], mate).wait_recv()

        for p in range(3):
            agot(p, 0, rows_of(p, x, 1 - zh, 1))
            ago(p, 1, rows_of(p, x, 0, 2), step("x", 1))
            ago(p, 2, rows_of(p, x, 0, 2), step("x", -1))
        yield
        for p in range(3):
            agot(p, 1, rows_of(p, x - 1, 0, 2))
            agot(p, 2, rows_of(p, x + 1, 0, 2))
            ago(p, 3, rows_of(p, x - 1, 0, 1), step("x", 1))
            ago(p, 4, rows_of(p, x + 1, 1, 1), step("x", -1))
        yield
        for p in range(3):
            agot(p, 3, rows_of(p, x + 2, 0, 1))
            agot(p, 4, rows_of(p, x + 2, 1, 1))
        for cp in mine:
            cp.wait_send()

    tile[...] = extra[...]
    jobs = [job(j) for j in range(4)]
    waiting = {0: [0, 2], 1: [1, 3]}
    active = []
    for slot in (0, 1):
        active.append([slot, waiting[slot].pop(0)])
    while active:
        for entry in list(active):
            try:
                next(jobs[entry[1]])
            except StopIteration:
                if waiting[entry[0]]:
                    entry[1] = waiting[entry[0]].pop(0)
                    next(jobs[entry[1]])
                else:
                    active.remove(entry)
    k = 0
    for a in ("x", "y", "z"):
        cps = []
        for by in (1, 2, 3):
            cp = remote(tile, tiles.at[k], nss.at[k], nrs.at[k], step(a, by))
            cp.start()
            cps.append((cp, k))
            k += 1
        for cp, _ in cps:
            cp.wait()
        acc = tile[...]
        for _, i in cps:
            acc = acc + tiles[i]
        tile[...] = acc
    cp = remote(tile, tiles.at[k], nss.at[k], nrs.at[k], mate)
    cp.start()
    cp.wait()
    norm[...] = tile[...] + tiles[k]


def reduce_grads(grads, extra):
    dma = pltpu.SemaphoreType.DMA
    scratch = []
    for slot in range(2):
        for p in range(3):
            scratch.append(pltpu.VMEM((2, 4, 4, 2, PART_ROWS[p], 256), F32))
    for p in range(3):
        for ph in range(3):
            dims = cut_size(p, ph)
            name, one, two = halves(ORDERS[p], ph, PART_ROWS[p])
            for k in range(4):
                d = dict(dims)
                if k < 2:
                    sl = (one, two)[k]
                    d[name] = sl.stop - sl.start
                scratch.append(pltpu.VMEM((4, d["zl"], d["y"], d["x"], d["zh"], d["r"], 256), F32))
    scratch += [
        dma((4, 9, 4)),
        dma((4, 9, 4)),
        dma((2, 3, 8)),
        dma((4, 3, 5)),
        dma((4, 3, 5)),
        dma((4, 3)),
        pltpu.VMEM((8, 128), F32),
        pltpu.VMEM((10, 8, 128), F32),
        dma((10,)),
        dma((10,)),
    ]
    return pl.pallas_call(
        reduce_kernel,
        out_shape=(
            jax.ShapeDtypeStruct((4, 1024, 256), F32),
            jax.ShapeDtypeStruct((8, 128), F32),
        ),
        in_specs=[ANY] * 4 + [VM],
        out_specs=(ANY, VM),
        scratch_shapes=scratch,
        compiler_params=params(3, 62 * 2**20),
    )(*grads, extra)


def layer_norm(values):
    center = values - jnp.mean(values, -1, keepdims=True)
    spread = jnp.mean(center * center, -1, keepdims=True)
    return center * lax.rsqrt(spread + NORM_EPS)


def modulate(values, scale_row, shift_row):
    return layer_norm(values) * (1.0 + scale_row) + shift_row


def modulate_back(values, scale_row, shift_row, grad_out):
    _, pull_back = jax.vjp(modulate, values, scale_row, shift_row)
    return pull_back(grad_out)


def columns(h, w):
    return jnp.einsum("td,jdk->jtk", h, w, preferred_element_type=F32)


def rows_back(g, w):
    return jnp.einsum("jtk,jdk->td", g, w, preferred_element_type=F32)


def weight_grad(h, g):
    return jnp.einsum("td,jtk->jdk", h, g, preferred_element_type=F32)


def adamw(weight, first, second, grad, factor):
    clipped = grad * factor
    first_new = BETA_ONE * first + (1.0 - BETA_ONE) * clipped
    second_new = BETA_TWO * second + (1.0 - BETA_TWO) * clipped * clipped
    first_hat = first_new / (1.0 - BETA_ONE**STEP)
    second_hat = second_new / (1.0 - BETA_TWO**STEP)
    weight_new = weight - LEARN * (first_hat / (jnp.sqrt(second_hat) + ADAM_EPS) + DECAY * weight)
    return (weight_new, first_new, second_new)


def local(
    x_in, scale_ids, pad_mask, loss_weights, targets, labels,
    cond_w, attn_w, mlp_w, head_w, class_table, biases,
    first_cond, first_attn, first_mlp, first_head, first_table, first_bias,
    second_cond, second_attn, second_mlp, second_head, second_table, second_bias,
):
    dp = lax.axis_index("dp")
    core = dp % 2
    wb_cond = cond_w.astype(BF16)
    shard = jnp.stack([attn_w, mlp_w[0], mlp_w[1], head_w]).astype(BF16)

    count_part = jnp.sum(pad_mask.astype(F32))
    row = jnp.concatenate([labels.astype(F32), count_part[None], jnp.zeros((125,), F32)])
    rounded = lax.reduce_precision(biases, 8, 7).reshape(10, 128)
    msg = jnp.concatenate([rounded, row[None], jnp.zeros((5, 128), F32)])
    level = jnp.where(pad_mask > 0, scale_ids, 1000).astype(F32)
    weight_own = (loss_weights * pad_mask).astype(F32)
    slots = jnp.concatenate(
        [level, scale_ids.astype(F32), targets.astype(F32), weight_own, jnp.zeros((8, 128), F32)]
    )
    (
        msg_all, slots_all, cond_all, embedded, ada, loss_tile,
        w, wo, h1, h2, h3, heads, o, att, x1, mlp, x2, f, u, dlogits,
    ) = forward_pass(msg, slots, class_table.astype(BF16), wb_cond, x_in.reshape(256, 1024), shard)
    w = w.reshape(8, 4, 1024, 256)
    h1, h2, h3 = (h.reshape(512, 1024) for h in (h1, h2, h3))
    att, x1, mlp, x2 = (a.reshape(2, 128, 1024) for a in (att, x1, mlp, x2))
    x = x_in.astype(F32)
    loss_part = loss_tile[0, 0]
    slots_all = slots_all.reshape(8, 2, 16, 128)
    true_count = jnp.sum(slots_all[:, 0, 8, 0])
    ada_rows = jnp.transpose(ada, (1, 0, 2)).reshape(2, 1, 8192)
    g_a, g_m, s_a, s_m, t_a, t_m, s_h, t_h = jnp.split(ada_rows, 8, axis=2)
    sq_index = lax.axis_index("seq")
    levels = lax.dynamic_index_in_dim(slots_all, sq_index % 2, 1, keepdims=False)
    key_level = jnp.transpose(levels[:, 0:2], (1, 0, 2)).reshape(2, 1024)
    query_level = jnp.transpose(levels[:, 2:4], (1, 0, 2)).reshape(2, 1024)

    def by_head(block):
        return block.reshape(8, 2, 128, 2, 64).transpose(1, 3, 0, 2, 4).reshape(2, 2, 1024, 64)

    def from_head(block):
        return block.reshape(2, 2, 8, 128, 64).transpose(2, 0, 3, 1, 4).reshape(8, 256, 128)

    q, k, v = (by_head(heads[:, i].reshape(8, 256, 128)) for i in range(3))
    visible = (key_level[:, None, None, :] <= query_level[:, None, :, None])
    scores = jnp.einsum("ihqd,ihkd->ihqk", q, k, preferred_element_type=F32) * SCORE_SCALE
    probs = jax.nn.softmax(jnp.where(visible, scores, -1e30), axis=-1)
    probs_low = probs.astype(BF16)

    grad_head = weight_grad(h3, dlogits)
    db_head = jnp.sum(dlogits.astype(F32), axis=1)
    dh3 = swap_add(11, rows_back(dlogits, w[:, 3]).reshape(2, 256, 1024)).reshape(2, 128, 1024)
    dx2, ds_h, dt_h = modulate_back(x2, s_h, t_h, dh3)
    dg_m = jnp.sum(dx2 * mlp, axis=1, keepdims=True)
    dmlp = (g_m * dx2).astype(BF16).reshape(256, 1024)
    db_fc2 = jnp.sum(dmlp.astype(F32), axis=0)
    (dmlp,) = pair_gather(12, dmlp)
    dmlp = dmlp.reshape(512, 1024)
    grad_two = weight_grad(dmlp, u)
    du = columns(dmlp, w[:, 2])
    _, gelu_back = jax.vjp(functools.partial(jax.nn.gelu, approximate=True), f)
    df = gelu_back(du)[0].astype(BF16)
    grad_one = weight_grad(h2, df)
    db_fc1 = jnp.sum(df.astype(F32), axis=1)
    dh2 = swap_add(13, rows_back(df, w[:, 1]).reshape(2, 256, 1024)).reshape(2, 128, 1024)
    dx1, ds_m, dt_m = modulate_back(x1, s_m, t_m, dh2)
    dx1 = dx1 + dx2
    dg_a = jnp.sum(dx1 * att, axis=1, keepdims=True)
    datt = (g_a * dx1).astype(BF16).reshape(256, 1024)
    db_proj = jnp.sum(datt.astype(F32), axis=0)
    do = jnp.einsum(
        "tjk,jdk->td", datt.reshape(256, 4, 256), wo, preferred_element_type=F32
    ).astype(BF16)
    do_heads = by_head(to_heads(14, do))
    o_pair, datt_pair = pair_gather(15, o, datt)
    datt_own = lax.dynamic_index_in_dim(
        datt_pair.reshape(512, 2, 2, 256), core, 2, keepdims=False
    )
    grad_o = jnp.einsum(
        "td,tjk->jdk", o_pair.reshape(512, 1024), datt_own, preferred_element_type=F32
    )
    dprobs = jnp.einsum("ihqd,ihkd->ihqk", do_heads, v, preferred_element_type=F32)
    inner = jnp.sum(probs * dprobs, axis=-1, keepdims=True)
    dscores = (probs * (dprobs - inner)).astype(BF16)
    dq = jnp.einsum("ihqk,ihkd->ihqd", dscores, k, preferred_element_type=F32) * SCORE_SCALE
    dk = jnp.einsum("ihqk,ihqd->ihkd", dscores, q, preferred_element_type=F32) * SCORE_SCALE
    dv = jnp.einsum("ihqk,ihqd->ihkd", probs_low, do_heads, preferred_element_type=F32)
    dqkv = jnp.stack([from_head(t.astype(BF16)) for t in (dq, dk, dv)], axis=1)
    dqkv = all_to_all(16, dqkv)
    dqkv = dqkv.reshape(2, 2, 2, 3, 256, 128).transpose(3, 0, 2, 4, 1, 5).reshape(6, 512, 256)
    grad_qkv = weight_grad(h1, dqkv)
    db_qkv = jnp.sum(dqkv.astype(F32), axis=1)
    dh1 = swap_add(17, rows_back(dqkv, w[:6, 0]).reshape(2, 256, 1024)).reshape(2, 128, 1024)
    _, ds_a, dt_a = modulate_back(x, s_a, t_a, dh1)
    dada = jnp.concatenate([dg_a, dg_m, ds_a, ds_m, dt_a, dt_m, ds_h, dt_h], axis=2)[:, 0]

    def spread_columns(b):
        mine = jnp.arange(2)[None, :, None] == core
        return jnp.where(mine, b[:, None, :], 0.0).reshape(-1)

    bias_part = jnp.concatenate(
        [
            jnp.sum(dada, axis=0),
            spread_columns(db_qkv[0:2]),
            spread_columns(db_qkv[4:6]),
            db_proj,
            spread_columns(db_fc1),
            db_fc2,
            spread_columns(db_head),
        ]
    ).reshape(16, 10, 128)
    ada_msg = dada.reshape(2, 16, 512).transpose(1, 0, 2).reshape(16, 8, 128)
    tail = jnp.concatenate([jnp.full((16, 1, 128), loss_part), jnp.zeros((16, 5, 128), F32)], axis=1)
    dada_all, bias_sum, dcond = small_reduce(
        jnp.concatenate([ada_msg, bias_part, tail], axis=1), wb_cond
    )
    bias_sum = bias_sum.reshape(16, 128)
    loss_total = bias_sum[10, 0]
    grad_bias = bias_sum[:10].reshape(1280)
    cond_full = jnp.transpose(cond_all, (1, 0, 2)).reshape(32, 1024).astype(F32)
    grad_cond = lax.dot_general(
        cond_full, dada_all, (((0,), (0,)), ((), ())), precision=HIGH, preferred_element_type=F32
    )
    _, silu_back = jax.vjp(jax.nn.silu, embedded)
    demb = silu_back(dcond)[0]
    labels_all = msg_all[:, 10, 0:2].reshape(32).astype(jnp.int32)
    class_hit = (labels_all[:, None] == jnp.arange(class_table.shape[0])[None, :]).astype(F32)
    grad_table = lax.dot_general(
        class_hit, demb, (((0,), (0,)), ((), ())), precision=HIGH, preferred_element_type=F32
    )
    own_squares = (
        jnp.sum(grad_cond * grad_cond) + jnp.sum(grad_table * grad_table) + jnp.sum(grad_bias * grad_bias)
    ) / 8.0
    extra = jnp.zeros((8, 128), F32).at[0, 0].set(own_squares)
    grad_attn = jnp.concatenate([grad_qkv, grad_o])
    shape = (2, 4, 1024, 256)
    summed, squares = reduce_grads(
        [g.reshape(shape) for g in (grad_attn, grad_one, grad_two, grad_head)], extra
    )
    grad_norm = jnp.sqrt(jnp.sum(squares))
    factor = jnp.minimum(1.0, CLIP / grad_norm)
    grads = (grad_cond, summed[0], summed[1:3], summed[3], grad_table, grad_bias)
    weights = (cond_w, attn_w, mlp_w, head_w, class_table, biases)
    firsts = (first_cond, first_attn, first_mlp, first_head, first_table, first_bias)
    seconds = (second_cond, second_attn, second_mlp, second_head, second_table, second_bias)
    results = [
        adamw(weight, first, second, grad, factor)
        for weight, first, second, grad in zip(weights, firsts, seconds, grads)
    ]
    new_weights = [entry[0] for entry in results]
    new_first = [entry[1] for entry in results]
    new_second = [entry[2] for entry in results]
    copies = [weight.astype(BF16) for weight in new_weights]
    return tuple(new_weights + new_first + new_second + copies + [grad_norm, loss_total, true_count])


def solution(mesh):
    split = (P(None, "dp"), P(None, "dp"), P(None, None, "dp"), P(None, "dp"), P(None, "dp"), P("dp"))
    in_specs = (P("dp", "seq", None),) + (P("dp", "seq"),) * 4 + (P("dp"),) + split * 3
    out_specs = split * 4 + (P(), P(), P())
    return jax.shard_map(local, mesh=mesh, in_specs=in_specs, out_specs=out_specs, check_vma=False)
```

```python
import functools

import jax
import jax.numpy as jnp
from jax import lax
from jax.experimental import pallas as pl
from jax.experimental.pallas import tpu as pltpu
from jax.sharding import PartitionSpec as P

STEP = 5
HIGH = lax.Precision.HIGHEST
NORM_EPS = 1e-06
CLIP = 0.01
LEARN = 0.02
DECAY = 0.1
BETA_ONE = 0.5
BETA_TWO = 0.5
ADAM_EPS = 1e-08
SCORE_SCALE = 0.125
MESH = pl.DeviceIdType.MESH
F32 = jnp.float32
BF16 = jnp.bfloat16
ANY = pl.BlockSpec(memory_space=pl.ANY)
VM = pl.BlockSpec(memory_space=pltpu.VMEM)

ROWS_YZ = 320
HALF_YZ = 160
QUARTER = 48


def place():
    dp = lax.axis_index("dp")
    sq = lax.axis_index("seq")
    core = lax.rem(dp, 2)
    y = lax.rem(dp // 2, 4)
    z = lax.rem(sq, 2) * 2 + dp // 8
    return sq // 2, y, z, core


def at(x, y, z, core):
    x, y, z = lax.rem(x + 4, 4), lax.rem(y + 4, 4), lax.rem(z + 4, 4)
    return (lax.rem(z, 2) * 8 + y * 2 + core, x * 2 + z // 2)


def greet(devices):
    bar = pltpu.get_barrier_semaphore()
    for device in devices:
        pl.semaphore_signal(bar, inc=1, device_id=device, device_id_type=MESH)
    pl.semaphore_wait(bar, len(devices))


def remote(src, dst, send, recv, device):
    return pltpu.make_async_remote_copy(
        src_ref=src, dst_ref=dst, send_sem=send, recv_sem=recv, device_id=device, device_id_type=MESH
    )


def params(collective_id, vmem=None):
    return pltpu.CompilerParams(
        collective_id=collective_id, has_side_effects=True, vmem_limit_bytes=vmem
    )


def group_peers():
    dp = lax.axis_index("dp")
    sq = lax.axis_index("seq")
    core = lax.rem(dp, 2)
    out = [(dp + 1 - 2 * core, sq)]
    for i in range(1, 8):
        for flip in range(2):
            out.append((dp + flip * (1 - 2 * core), lax.rem(sq + i, 8)))
    return out


def head_lanes(pair, core):
    return pl.ds(pl.multiple_of(((pair // 2 * 2 + core) * 2 + lax.rem(pair, 2)) * 128, 128), 128)


NT = (((1,), (1,)), ((), ()))


def normalize(v):
    center = v - jnp.mean(v, -1, keepdims=True)
    spread = jnp.mean(center * center, -1, keepdims=True)
    return center * lax.rsqrt(spread + NORM_EPS)


def ada_row(ada, k, img):
    return jnp.concatenate([ada[2 * k, img : img + 1, :], ada[2 * k + 1, img : img + 1, :]], axis=1)


def column_of(row):
    return jnp.transpose(jnp.broadcast_to(row, (128, 128)))


def forward_kernel(
    msg, slots, table, cond_w, x_in, s,
    msg_all, slots_all, cond_all, emb_out, ada, loss_out,
    w_o, wo_o, h1_o, h2_o, h3_o, hb_o, ot_o, att_o, x1_o, mlp_o, x2_o, f_o, u_o, dl_o,
    w, wo, h1, h2, h3, src, hb, oh, ot, att, x1, mlp, x2, acc, got_acc, f, u, dl,
    cond_own, ada_own, bias, qcol, tcol, wcol, stats,
    gs, gr, gl, os, orr, s1, r1, s2, r2, s3, r3, s4, r4, ps, pr, as_, ar, al, ts, tr, tl, outs_sem,
):
    x, y, z, c = place()
    dp = lax.axis_index("dp")
    sq = lax.axis_index("seq")
    zl = lax.rem(z, 2)
    up, down, far = lax.rem(y + 1, 4), lax.rem(y + 3, 4), lax.rem(y + 2, 4)
    yp, ym = at(x, y + 1, z, c), at(x, y - 1, z, c)
    zp, zm = at(x, y, z + 1, c), at(x, y, z - 1, c)
    xp, xm = at(x + 1, y, z, c), at(x - 1, y, z, c)
    zs = at(x, y, z + 1 - 2 * c, c)
    mate = at(x, y, z, 1 - c)
    base = dp - c
    row = [(lax.rem(dp + i, 16), sq) for i in range(1, 16)]
    group = group_peers()
    greet(row + group[1:] + [at(x, y, z + 2 * zl - 1, c)])

    pending = []

    def keep(k, src_ref, dst_ref):
        cp = pltpu.make_async_copy(src_ref, dst_ref, outs_sem.at[k])
        cp.start()
        pending.append(cp)
        return cp

    def rows_at(j, start, count):
        return pl.ds(512 * (j % 2) + start, count)

    def quarter(j, pos):
        start = 512 * (j % 2) + ROWS_YZ + QUARTER * lax.rem(pos + 4, 4)
        return pl.ds(pl.multiple_of(start, 16), QUARTER)

    sent = []

    def go(j, k, a, b, device):
        cp = remote(a, b, gs.at[j, k], gr.at[j, k], device)
        cp.start()
        sent.append(cp)

    def got(j, k, ref):
        remote(ref, ref, gs.at[j, k], gr.at[j, k], mate).wait_recv()

    def stage(kind, j):
        m = j // 2
        full, first = rows_at(j, 0, ROWS_YZ), rows_at(j, 0, HALF_YZ)
        second, mine = rows_at(j, HALF_YZ, HALF_YZ), quarter(j, x)
        own = []
        if kind in "AB":
            for i, rows in enumerate((full, mine)):
                own.append(pltpu.make_async_copy(s.at[m, rows], w.at[zl, y, m, rows], gl.at[j, i]))
        if kind == "A":
            go(j, 0, s.at[m, full], w.at[zl, y, m, full], yp)
            go(j, 1, s.at[m, full], w.at[zl, y, m, full], ym)
            go(j, 6, s.at[m, mine], w.at[zl, y, m, mine], zs)
            for cp in own:
                cp.start()
        if kind == "B":
            for cp in own:
                cp.wait()
            got(j, 6, w.at[1 - zl, y, m, mine])
            go(j, 7, w.at[:, y, m, mine], w.at[:, y, m, mine], yp)
            go(j, 8, w.at[:, y, m, mine], w.at[:, y, m, mine], ym)
            got(j, 0, w.at[zl, down, m, full])
            got(j, 1, w.at[zl, up, m, full])
            go(j, 2, w.at[zl, down, m, first], w.at[zl, down, m, first], yp)
            go(j, 3, w.at[zl, up, m, second], w.at[zl, up, m, second], ym)
        if kind == "C":
            got(j, 7, w.at[:, down, m, mine])
            got(j, 8, w.at[:, up, m, mine])
            go(j, 9, w.at[0, down, m, mine], w.at[0, down, m, mine], yp)
            go(j, 10, w.at[1, up, m, mine], w.at[1, up, m, mine], ym)
            got(j, 2, w.at[zl, far, m, first])
            got(j, 3, w.at[zl, far, m, second])
            go(j, 4, w.at[zl, :, m, first], w.at[zl, :, m, first], zp)
            go(j, 5, w.at[zl, :, m, second], w.at[zl, :, m, second], zm)
        if kind == "D":
            got(j, 9, w.at[0, far, m, mine])
            got(j, 10, w.at[1, far, m, mine])
            go(j, 11, w.at[:, :, m, mine], w.at[:, :, m, mine], xp)
            go(j, 12, w.at[:, :, m, mine], w.at[:, :, m, mine], xm)
        if kind == "E":
            left, right = quarter(j, x - 1), quarter(j, x + 1)
            got(j, 11, w.at[:, :, m, left])
            got(j, 12, w.at[:, :, m, right])
            go(j, 13, w.at[0, :, m, left], w.at[0, :, m, left], xp)
            go(j, 14, w.at[1, :, m, right], w.at[1, :, m, right], xm)
        if kind == "F":
            across = quarter(j, x + 2)
            got(j, 4, w.at[1 - zl, :, m, first])
            got(j, 5, w.at[1 - zl, :, m, second])
            got(j, 13, w.at[0, :, m, across])
            got(j, 14, w.at[1, :, m, across])
            if j % 2:
                keep(m, w.at[:, :, m], w_o.at[:, :, m])
            if j == 1:
                for i in range(2):
                    remote(w.at[1, 2 + i, 0], wo.at[2 * i + c], os.at[i], orr.at[i], mate).start()
                    pltpu.make_async_copy(w.at[1, 2 + i, 0], wo.at[2 * i + c], gl.at[i, 2]).start()

    wave = [
        ["A0"], ["A1"], ["B0", "A2"], ["B1", "C0", "A3"],
        ["C1", "D0", "B2", "A4"], ["D1", "E0", "C2", "B3", "A5"], ["E1", "F0", "D2", "C3", "B4"], ["F1"],
        ["E2", "D3", "C4", "B5", "A6"],
        ["F2", "E3", "D4", "C5", "B6", "A7"], ["F3", "E4", "D5", "C6", "B7"], ["F4", "E5", "D6", "C7"],
        ["F5", "E6", "D7"], ["F6", "E7"], ["F7"],
    ]

    def pump(n=1):
        for _ in range(n):
            if wave:
                for item in wave.pop(0):
                    stage(item[0], int(item[1]))

    firsts = []
    for i, to in enumerate(row):
        cp = remote(msg, msg_all.at[dp], s1.at[i], r1.at[i], to)
        cp.start()
        firsts.append(cp)
    msg_all[dp] = msg[...]
    pump()
    for cp in firsts:
        cp.wait()
    seen = msg_all[...]
    count = jnp.sum(seen[:, 10, 2:3], axis=0, keepdims=True)
    slots[8:9, :] = jnp.broadcast_to(count, (1, 128))
    for d in range(16):
        bias[pl.ds(10 * d, 10), :] = seen[d, 0:10, :]
    seconds = []
    for i, to in enumerate(group):
        cp = remote(slots, slots_all.at[sq * 2 + c], s2.at[i], r2.at[i], to)
        cp.start()
        seconds.append(cp)
    slots_all[sq * 2 + c] = slots[...]
    classes = table.shape[1]
    lane = lax.broadcasted_iota(jnp.int32, (32, classes), 1)
    labels = jnp.concatenate([seen[d, 10:11, i : i + 1] for d in range(16) for i in range(2)], axis=0)
    hit = jnp.where(lane == labels.astype(jnp.int32), 1.0, 0.0).astype(BF16)
    emb = lax.dot_general(hit, table[...], NT, preferred_element_type=F32)
    emb_out[...] = emb
    cond_own[...] = (emb / (1.0 + jnp.exp(-emb))).astype(BF16)
    cond_all[dp] = cond_own[...]
    thirds = []
    for i, to in enumerate(row):
        cp = remote(cond_own, cond_all.at[dp], s3.at[i], r3.at[i], to)
        cp.start()
        thirds.append(cp)
    pump()
    for cp in thirds:
        cp.wait()
    total = jnp.zeros((32, 512), F32)
    for d in range(16):
        total += jnp.dot(cond_all[d], cond_w[pl.ds(64 * d, 64), :], preferred_element_type=F32)
    total += jnp.concatenate([bias[pl.ds(dp * 4 + i, 1), :] for i in range(4)], axis=1)
    for d in range(16):
        ada_own[d] = total[2 * d : 2 * d + 2]
    fourths = []
    for i in range(15):
        to = lax.rem(dp + 1 + i, 16)
        cp = remote(ada_own.at[to], ada.at[dp], s4.at[i], r4.at[i], (to, sq))
        cp.start()
        fourths.append(cp)
    ada[dp] = ada_own[dp]
    pump()
    for cp in fourths:
        cp.wait()
    for cp in seconds:
        cp.wait()

    owner = lax.rem(sq, 2)
    for img in range(2):
        for g in range(8):
            qcol[img, g] = column_of(slots_all[g * 2 + owner, pl.ds(2 + img, 1), :])
        for q in range(2):
            at_rows = pl.ds((q * 2 + img) * 128, 128)
            tcol[at_rows, :] = column_of(slots_all[sq * 2 + q, pl.ds(4 + img, 1), :])
            wcol[at_rows, :] = column_of(slots_all[sq * 2 + q, pl.ds(6 + img, 1), :])
    true_count = jnp.sum(
        jnp.concatenate([slots_all[2 * g, 8:9, 0:1] for g in range(8)], axis=0), axis=0, keepdims=True
    )

    def blocks(fn):
        for img in range(2):
            def body(i, carry, img=img):
                fn(img, pl.ds(pl.multiple_of(img * 128 + i * 32, 32), 32))
                return carry
            lax.fori_loop(0, 4, body, 0)

    def exchange(k, ref):
        cp = remote(ref.at[c], ref.at[c], ps.at[k], pr.at[k], mate)
        cp.start()
        return cp

    def modulated(img, v, scale, shift):
        return (normalize(v) * (1.0 + ada_row(ada, scale, img)) + ada_row(ada, shift, img)).astype(BF16)

    def do_h1(img, rows):
        h1[c, rows, :] = modulated(img, x_in[rows, :].astype(F32), 2, 4)

    blocks(do_h1)
    cp = exchange(0, h1)
    pump()
    cp.wait()
    keep(4, h1, h1_o)
    pump(4)

    def bias_row(start):
        return jnp.concatenate([bias[pl.ds(start, 1), :], bias[pl.ds(start + 1, 1), :]], axis=1)

    tokens = h1[...].reshape(512, 1024)
    for j in range(6):
        t, jj = j // 2, j % 2
        val = jnp.dot(tokens, w[j // 4, j % 4, 0], preferred_element_type=F32)
        if t != 1:
            val = val + bias_row(64 + (0 if t == 0 else 8) + (2 * jj + c) * 2)
        val = val.astype(BF16)
        for half in range(2):
            for ip in range(2):
                src[(jj * 2 + half) * 2 + ip, t] = val[
                    ip * 256 : ip * 256 + 256, half * 128 : half * 128 + 128
                ].reshape(2, 128, 128)
    cps = []
    for i in range(1, 8):
        to = lax.rem(sq + i, 8)
        cp = remote(src.at[to], hb.at[sq], as_.at[i], ar.at[i], (dp, to))
        cp.start()
        cps.append(cp)
    hb[sq] = src[sq]
    pump()
    for cp in cps:
        cp.wait()
    keep(5, hb, hb_o)

    low_lanes = lax.broadcasted_iota(jnp.int32, (256, 128), 1) < 64

    def attend_block(i, carry):
        img, qb = i // 4, lax.rem(i, 4)
        q = jnp.concatenate([hb[2 * qb, 0, img], hb[2 * qb + 1, 0, img]], axis=0)
        k = jnp.concatenate([hb[g, 1, img] for g in range(8)], axis=0)
        v = jnp.concatenate([hb[g, 2, img] for g in range(8)], axis=0)
        key = jnp.concatenate([slots_all[g * 2 + owner, pl.ds(img, 1), :] for g in range(8)], axis=1)
        query = jnp.concatenate([qcol[img, 2 * qb], qcol[img, 2 * qb + 1]], axis=0)[:, 0:1]
        seen_by = key <= query
        heads = []
        for h in range(2):
            mask = low_lanes if h == 0 else jnp.logical_not(low_lanes)
            qh = jnp.where(mask, q, jnp.zeros_like(q))
            sc = lax.dot_general(qh, k, NT, preferred_element_type=F32) * SCORE_SCALE
            sc = jnp.where(seen_by, sc, -1e30)
            e = jnp.exp(sc - jnp.max(sc, axis=-1, keepdims=True))
            p = (e / jnp.sum(e, axis=-1, keepdims=True)).astype(BF16)
            heads.append(jnp.dot(p, v, preferred_element_type=F32))
        o = jnp.where(low_lanes, heads[0], heads[1]).astype(BF16)
        oh[2 * qb, img] = o[:128]
        oh[2 * qb + 1, img] = o[128:]
        return carry

    for i in range(0, 8, 2):
        lax.fori_loop(i, i + 2, attend_block, 0)
        if i < 6:
            pump()
    pair = sq // 2
    lanes = head_lanes(pair, c)

    def o_copy(i, img):
        to = lax.rem(sq + i, 8)
        return remote(
            oh.at[to, img], ot.at[pl.ds(img * 128, 128), lanes], ts.at[i, img], tr.at[pair, c, img],
            (base + owner, to),
        )

    for img in range(2):
        for i in range(1, 8):
            o_copy(i, img).start()

        @pl.when(owner == c)
        def _():
            ot[pl.ds(img * 128, 128), lanes] = oh[sq, img]

        @pl.when(owner != c)
        def _():
            o_copy(0, img).start()

    pump()
    for img in range(2):
        for p in range(4):
            for q in range(2):
                view = ot.at[pl.ds(img * 128, 128), pl.ds(((p // 2 * 2 + q) * 2 + p % 2) * 128, 128)]

                @pl.when(jnp.logical_or(sq != p * 2 + c, c != q))
                def _():
                    remote(view, view, ts.at[0, img], tr.at[p, q, img], mate).wait_recv()

    keep(6, ot, ot_o)
    for i in range(2):
        remote(w.at[1, 2 + i, 0], wo.at[2 * i + c], os.at[i], orr.at[i], mate).wait()
        pltpu.make_async_copy(w.at[1, 2 + i, 0], wo.at[2 * i + c], gl.at[i, 2]).wait()
    keep(7, wo, wo_o)
    for k in range(4):
        cols = pl.ds(256 * k, 256)
        att[:, cols] = jnp.dot(ot[...], wo[k], preferred_element_type=F32) + bias_row(80 + 2 * k)
    keep(8, att, att_o)

    def do_h2(img, rows):
        v = x_in[rows, :].astype(F32) + ada_row(ada, 0, img) * att[rows, :]
        x1[rows, :] = v
        h2[c, rows, :] = modulated(img, v, 3, 5)

    blocks(do_h2)
    cp = exchange(1, h2)
    keep(9, x1, x1_o)
    cp.wait()
    keep(10, h2, h2_o)
    pump()

    def chunk(ref, j, kind):
        return ref[j // 4, lax.rem(j, 4), kind]

    def do_f(j, carry):
        val = jnp.dot(h2[...].reshape(512, 1024), chunk(w, j, 1), preferred_element_type=F32)
        val = val + bias_row(88 + (2 * j + c) * 2)
        f[j] = val
        act = jax.nn.gelu(val, approximate=True).astype(BF16)
        u[j] = act
        part = lax.dot_general(act, chunk(w, j, 2), NT, preferred_element_type=F32).reshape(2, 256, 1024)

        @pl.when(j == 0)
        def _():
            acc[...] = part

        @pl.when(j > 0)
        def _():
            acc[...] += part

        return carry

    lax.fori_loop(0, 8, do_f, 0)
    f_copy = keep(11, f, f_o)
    keep(12, u, u_o)
    cp = remote(acc.at[1 - c], got_acc, ps.at[2], pr.at[2], mate)
    cp.start()
    pump()
    b_two = jnp.concatenate([bias[pl.ds(120 + i, 1), :] for i in range(8)], axis=1)
    cp.wait()

    def do_h3(img, rows):
        m = acc[c, rows, :] + got_acc[rows, :] + b_two
        mlp[rows, :] = m
        v = x1[rows, :] + ada_row(ada, 1, img) * m
        x2[rows, :] = v
        h3[c, rows, :] = modulated(img, v, 6, 7)

    blocks(do_h3)
    cp = exchange(3, h3)
    keep(13, mlp, mlp_o)
    keep(14, x2, x2_o)
    f_copy.wait()
    pending[:] = [p for p in pending if p is not f_copy]
    cp.wait()
    keep(15, h3, h3_o)

    def do_logits(j, top):
        val = jnp.dot(h3[...].reshape(512, 1024), chunk(w, j, 3), preferred_element_type=F32)
        val = val + bias_row(128 + (2 * j + c) * 2)
        f[j] = val
        return jnp.maximum(top, jnp.max(val, axis=-1, keepdims=True))

    top = lax.fori_loop(0, 8, do_logits, jnp.full((512, 1), -jnp.inf, F32))
    inner = lax.broadcasted_iota(jnp.int32, (512, 256), 1)

    def target_hit(j):
        return inner == (tcol[:, 0:1].astype(jnp.int32) - (2 * j + c) * 256)

    def do_mass(j, carry):
        mass, picked = carry
        val = f[j]
        mass = mass + jnp.sum(jnp.exp(val - top), axis=-1, keepdims=True)
        picked = picked + jnp.sum(jnp.where(target_hit(j), val, 0.0), axis=-1, keepdims=True)
        return mass, picked

    zero = jnp.zeros((512, 1), F32)
    mass, picked = lax.fori_loop(0, 8, do_mass, (zero, zero))
    lane = lax.broadcasted_iota(jnp.int32, (512, 128), 1)
    stats[c] = jnp.where(lane == 0, top, jnp.where(lane == 1, mass, picked))
    cp = exchange(4, stats)
    cp.wait()
    both = [stats[0], stats[1]]
    top_all = jnp.maximum(both[0][:, 0:1], both[1][:, 0:1])
    mass_all = sum(b[:, 1:2] * jnp.exp(b[:, 0:1] - top_all) for b in both)
    log_total = top_all + jnp.log(mass_all)
    weight = wcol[:, 0:1]
    losses = weight * (log_total - (both[0][:, 2:3] + both[1][:, 2:3]))
    loss_out[...] = jnp.broadcast_to(0.5 * jnp.sum(losses, axis=0, keepdims=True), (8, 128))
    share = weight / true_count

    def do_dlogits(j, carry):
        grad = share * (jnp.exp(f[j] - log_total) - jnp.where(target_hit(j), 1.0, 0.0))
        dl[j] = grad.astype(BF16)
        return carry

    lax.fori_loop(0, 8, do_dlogits, 0)
    keep(16, dl, dl_o)
    for img in range(2):
        for i in range(1, 8):
            o_copy(i, img).wait_send()

        @pl.when(owner != c)
        def _():
            o_copy(0, img).wait_send()

    for cp in sent:
        cp.wait_send()
    for cp in pending:
        cp.wait()


def forward_pass(msg, slots, table, cond_w, x_rows, shard):
    dma = pltpu.SemaphoreType.DMA
    sd = jax.ShapeDtypeStruct
    kept = [
        sd((2, 4, 4, 1024, 256), BF16), sd((4, 1024, 256), BF16),
        sd((2, 256, 1024), BF16), sd((2, 256, 1024), BF16), sd((2, 256, 1024), BF16),
        sd((8, 3, 2, 128, 128), BF16), sd((256, 1024), BF16),
        sd((256, 1024), F32), sd((256, 1024), F32), sd((256, 1024), F32), sd((256, 1024), F32),
        sd((8, 512, 256), F32), sd((8, 512, 256), BF16), sd((8, 512, 256), BF16),
    ]
    vm = pltpu.VMEM
    return pl.pallas_call(
        forward_kernel,
        out_shape=[
            sd((16, 16, 128), F32), sd((16, 16, 128), F32), sd((16, 32, 64), BF16),
            sd((32, 64), F32), sd((16, 2, 512), F32), sd((8, 128), F32),
        ] + kept,
        in_specs=[VM] * 5 + [ANY],
        out_specs=[VM] * 6 + [ANY] * len(kept),
        scratch_shapes=[
            vm((2, 4, 4, 1024, 256), BF16), vm((4, 1024, 256), BF16),
            vm((2, 256, 1024), BF16), vm((2, 256, 1024), BF16), vm((2, 256, 1024), BF16),
            vm((8, 3, 2, 128, 128), BF16), vm((8, 3, 2, 128, 128), BF16), vm((8, 2, 128, 128), BF16),
            vm((256, 1024), BF16),
            vm((256, 1024), F32), vm((256, 1024), F32), vm((256, 1024), F32), vm((256, 1024), F32),
            vm((2, 256, 1024), F32), vm((256, 1024), F32),
            vm((8, 512, 256), F32), vm((8, 512, 256), BF16), vm((8, 512, 256), BF16),
            vm((32, 64), BF16), vm((16, 2, 512), F32), vm((160, 128), F32),
            vm((2, 8, 128, 128), F32), vm((512, 128), F32), vm((512, 128), F32), vm((2, 512, 128), F32),
            dma((8, 15)), dma((8, 15)), dma((8, 3)), dma((2,)), dma((2,)),
            dma((15,)), dma((15,)), dma((15,)), dma((15,)), dma((15,)), dma((15,)), dma((15,)), dma((15,)),
            dma((5,)), dma((5,)), dma((8,)), dma((8,)), dma,
            dma((8, 2)), dma((4, 2, 2)), dma, dma((17,)),
        ],
        compiler_params=params(0, 63 * 2**20),
    )(msg, slots, table, cond_w, x_rows, shard)


PART_ROWS = (16, 24, 24)
PART_BASE = (0, 128, 320)
ORDERS = ("xyz", "yzx", "zxy")
SLOTS = 3
JOBS = 8


def block_cut(order, phase, rows):
    axis, later = order[phase], order[phase + 1 :]
    if axis != "z" and "z" in later:
        return ("zl", slice(0, 1), slice(1, 2))
    if "y" in later:
        return ("y", slice(0, 2), slice(2, 4))
    if "x" in later:
        return ("x", slice(0, 2), slice(2, 4))
    cut = (rows // 8 + 1) // 2 * 8
    return ("r", slice(0, cut), slice(cut, rows))


def block_dims(part, phase):
    later = ORDERS[part][phase + 1 :]
    return {
        "zl": 2 if "z" in later else 1,
        "y": 4 if "y" in later else 1,
        "x": 4 if "x" in later else 1,
        "zh": 2 if "z" in later else 1,
        "r": PART_ROWS[part],
    }


def recv_shapes():
    shapes = []
    for p in range(3):
        for ph in range(3):
            name, one, two = block_cut(ORDERS[p], ph, PART_ROWS[p])
            for k in range(4 if ph < 2 else 3):
                d = dict(block_dims(p, ph))
                if ph < 2 and k < 2:
                    cut = (one, two)[k]
                    d[name] = cut.stop - cut.start
                shapes.append((SLOTS, d["zl"], d["y"], d["x"], d["zh"], d["r"], 256))
    return shapes


def backward_kernel(*refs):
    names = [
        "msg_all", "slots_all", "cond_all", "emb", "ada", "loss", "cond_w", "x_in", "w_i", "wo_i",
        "h1_i", "h2_i", "h3_i", "hb_i", "ot_i", "att_i", "x1_i", "mlp_i", "x2_i", "f_i", "u_i", "dl_i",
        "out", "norm", "bias_sum", "gtable", "gcond", "wb", "dl", "u", "fb", "hh", "hT", "oT", "dm",
        "otp", "da", "acc", "got", "xa", "xb", "dx", "hb", "doh", "dov", "dkv", "dsrc", "dr", "dq6",
        "kcol", "dmod", "biasp", "smsg", "sgot", "smine", "sall", "spart", "sback", "gst", "gcs",
        "tile", "tiles",
    ]
    names += ["g%d" % i for i in range(3 * SLOTS)] + ["st0", "st1", "st2"]
    n = len(names)
    r = dict(zip(names, refs[:n]))
    rest = list(refs[n:])
    recv = {}
    for p in range(3):
        for ph in range(3):
            count = 4 if ph < 2 else 3
            recv[p, ph] = rest[:count]
            rest = rest[count:]
    (
        ls, fs, ps, pr, hs, hr, hl, as_, ar, js, jr, gss, grs, ol, credit,
        s1, r1, s2, r2, s3, r3, ns, nr, gl,
    ) = rest
    msg_all, slots_all, ada, biasp, dmod = r["msg_all"], r["slots_all"], r["ada"], r["biasp"], r["dmod"]
    dl, u, hT, oT, acc, got = r["dl"], r["u"], r["hT"], r["oT"], r["acc"], r["got"]
    dx, xa, xb, wb, hh = r["dx"], r["xa"], r["xb"], r["wb"], r["hh"]
    dm, otp, da, tile = r["dm"], r["otp"], r["da"], r["tile"]
    parts = [[r["g%d" % (s * 3 + p)] for p in range(3)] for s in range(SLOTS)]
    stage_out = [r["st0"], r["st1"], r["st2"]]
    out = r["out"]

    x, y, z, c = place()
    dp = lax.axis_index("dp")
    sq = lax.axis_index("seq")
    zl, zh = lax.rem(z, 2), z // 2
    base = dp - c
    owner = lax.rem(sq, 2)
    pair = sq // 2
    mate = at(x, y, z, 1 - c)
    row = [lax.rem(dp + i, 16) for i in range(1, 16)]
    line = [lax.rem(sq + i, 8) for i in range(1, 8)]
    greet([(d, sq) for d in row] + group_peers()[1:] + [at(x, y, z + 2 * zl - 1, c)])
    here = {"x": x, "y": y, "z": z}

    def step(axis, by):
        q = dict(here)
        q[axis] = q[axis] + by
        return at(q["x"], q["y"], q["z"], c)

    def load(k, src, dst):
        cp = pltpu.make_async_copy(src, dst, ls.at[k])
        cp.start()
        return cp

    loads = {
        "h3": load(0, r["h3_i"], hh),
        "dl": load(1, r["dl_i"], dl),
        "w3": load(2, r["w_i"].at[:, :, 3], wb),
        "x2": load(3, r["x2_i"], xa),
        "mlp": load(4, r["mlp_i"], xb),
        "u": load(5, r["u_i"], u),
        "hb": load(6, r["hb_i"], r["hb"]),
        "ot": load(8, r["ot_i"], otp.at[c]),
    }

    def view(ref, p, ph, index, half=None):
        order = ORDERS[p]
        sel = {}
        for i, a in enumerate(order):
            sel[a] = here[a] if i < ph else (lax.rem(index + 4, 4) if i == ph else None)
        idx = {
            "zl": slice(0, 2) if sel["z"] is None else pl.ds(lax.rem(sel["z"], 2), 1),
            "y": slice(0, 4) if sel["y"] is None else pl.ds(sel["y"], 1),
            "x": slice(0, 4) if sel["x"] is None else pl.ds(sel["x"], 1),
            "zh": slice(0, 2) if sel["z"] is None else pl.ds(sel["z"] // 2, 1),
            "r": slice(0, PART_ROWS[p]),
        }
        if half is not None:
            name, one, two = block_cut(order, ph, PART_ROWS[p])
            idx[name] = (one, two)[half]
        return ref.at[idx["zl"], idx["y"], idx["x"], idx["zh"], idx["r"]]

    def add(dst, srcs):
        d0, d1, d2, d3 = dst.shape[:4]

        def body(i, carry):
            a, b = i // d1, lax.rem(i, d1)
            for cc in range(d2):
                for d in range(d3):
                    val = dst[a, b, cc, d]
                    for s in srcs:
                        val = val + s[a, b, cc, d]
                    dst[a, b, cc, d] = val
            return carry

        if d0 * d1 == 1:
            body(0, 0)
        else:
            lax.fori_loop(0, d0 * d1, body, 0)

    neighbours = [step(a, b) for a in "xyz" for b in (1, -1)]
    unsent = []

    def phases(j, slot, again, reused):
        mine = []
        if again:
            pl.semaphore_wait(credit.at[slot], 6)

        def go(p, ph, k, src, dst, device):
            cp = remote(src, dst, js.at[j, p * 3 + ph, k], jr.at[j, p * 3 + ph, k], device)
            cp.start()
            mine.append(cp)

        def arrived(p, ph, k, ref):
            remote(ref, ref, js.at[j, p * 3 + ph, k], jr.at[j, p * 3 + ph, k], mate).wait_recv()

        for ph in range(3):
            info = []
            for p in range(3):
                a = ORDERS[p][ph]
                info.append((p, a, here[a], parts[slot][p], [b.at[slot] for b in recv[p, ph]]))
            if ph == 2:
                for p, a, i, g, bufs in info:
                    for k, by in enumerate((1, -1, 2)):
                        go(p, ph, k, view(g, p, ph, i + by), bufs[k], step(a, by))
                yield
                for p, a, i, g, bufs in info:
                    for k in range(3):
                        arrived(p, ph, k, bufs[k])
                    add(view(g, p, ph, i), bufs)
                break
            for p, a, i, g, bufs in info:
                go(p, ph, 0, view(g, p, ph, i + 2, 0), bufs[0], step(a, 1))
                go(p, ph, 1, view(g, p, ph, i + 2, 1), bufs[1], step(a, -1))
            yield
            for p, a, i, g, bufs in info:
                arrived(p, ph, 0, bufs[0])
                add(view(g, p, ph, i + 1, 0), [bufs[0]])
                go(p, ph, 2, view(g, p, ph, i + 1), bufs[2], step(a, 1))
                arrived(p, ph, 1, bufs[1])
                add(view(g, p, ph, i - 1, 1), [bufs[1]])
                go(p, ph, 3, view(g, p, ph, i - 1), bufs[3], step(a, -1))
            yield
            for p, a, i, g, bufs in info:
                arrived(p, ph, 2, bufs[2])
                arrived(p, ph, 3, bufs[3])
                add(view(g, p, ph, i), [bufs[2], bufs[3]])
        for p in range(3):
            val = parts[slot][p][zl, y, x, zh]
            stage_out[p][j] = val
            square = val * val
            total = tile[...]
            for t in range(PART_ROWS[p] // 8):
                for k in range(2):
                    total = total + square[8 * t : 8 * t + 8, 128 * k : 128 * k + 128]
            tile[...] = total
        for cp in mine:
            cp.wait_send()
        if reused():
            for device in neighbours:
                pl.semaphore_signal(credit.at[slot], inc=1, device_id=device, device_id_type=MESH)

    def tail(j):
        kind, half = JOB_KIND[j // 2], j % 2
        o = out.at[kind]

        def rows_of(p, xi, zi, count):
            n_rows = PART_ROWS[p]
            start = half * 512 + PART_BASE[p] + (lax.rem(xi + 4, 4) * 2 + zi) * n_rows
            return pl.ds(pl.multiple_of(start, 8), count * n_rows)

        def go(p, k, src, rows, device):
            cp = remote(src, o.at[rows], gss.at[j, p, k], grs.at[j, p, k], device)
            cp.start()
            unsent.append(cp)

        def arrived(p, k, rows):
            remote(o.at[rows], o.at[rows], gss.at[j, p, k], grs.at[j, p, k], mate).wait_recv()

        own = []
        for p in range(3):
            rows = rows_of(p, x, zh, 1)
            cp = pltpu.make_async_copy(stage_out[p].at[j], o.at[rows], ol.at[j, p])
            cp.start()
            own.append(cp)
            go(p, 0, stage_out[p].at[j], rows, step("z", 2))
        yield
        for p in range(3):
            own[p].wait()
            arrived(p, 0, rows_of(p, x, 1 - zh, 1))
            both = rows_of(p, x, 0, 2)
            go(p, 1, o.at[both], both, step("x", 1))
            go(p, 2, o.at[both], both, step("x", -1))
        yield
        for p in range(3):
            arrived(p, 1, rows_of(p, x - 1, 0, 2))
            arrived(p, 2, rows_of(p, x + 1, 0, 2))
            left, right = rows_of(p, x - 1, 0, 1), rows_of(p, x + 1, 1, 1)
            go(p, 3, o.at[left], left, step("x", 1))
            go(p, 4, o.at[right], right, step("x", -1))
        yield
        for p in range(3):
            arrived(p, 3, rows_of(p, x + 2, 0, 1))
            arrived(p, 4, rows_of(p, x + 2, 1, 1))

    JOB_KIND = (3, 2, 1, 0)

    def transpose_into(dst, src):
        def body(i, carry):
            cols = pl.ds(pl.multiple_of(i * 128, 128), 128)
            dst[cols, :] = jnp.transpose(src[:, :, cols].reshape(512, 128))
            return carry
        lax.fori_loop(0, 8, body, 0)

    def store_part(slot, a, b, val):
        for p in range(3):
            n_rows = PART_ROWS[p]
            for xi in range(4):
                for zi in range(2):
                    start = PART_BASE[p] + (xi * 2 + zi) * n_rows
                    parts[slot][p][a, b, xi, zi] = val[start : start + n_rows]

    prepared = set()

    def fill(j, slot):
        kind, half = JOB_KIND[j // 2], j % 2
        if kind not in prepared:
            prepared.add(kind)
            if kind == 3:
                transpose_into(hT, hh)
            if kind == 2:
                transpose_into(hT, dm)
            if kind == 1:
                loads["h2"].wait()
                transpose_into(hT, hh)
                loads["h1"] = load(0, r["h1_i"], hh)
            if kind == 0:
                loads["h1"].wait()
                transpose_into(hT, hh)
                transpose_into(oT, otp)
        rows = pl.ds(half * 512, 512)
        right = {3: dl, 2: u, 1: dl}

        def body(i, carry):
            g = right[kind][i] if kind else r["dq6"][i]
            store_part(slot, i // 4, lax.rem(i, 4), jnp.dot(hT[rows, :], g, preferred_element_type=F32))
            return carry

        lax.fori_loop(0, 8 if kind else 6, body, 0)
        if kind == 0:
            for jj in range(2):
                cols = pl.ds(pl.multiple_of((2 * jj + c) * 256, 256), 256)
                g = da[:, :, cols].reshape(512, 256)
                store_part(slot, 1, 2 + jj, jnp.dot(oT[rows, :], g, preferred_element_type=F32))

    queue = list(range(JOBS))
    running = []
    tails = []
    free = list(range(SLOTS))
    ready = {3}
    used = set()

    steps_done = {}

    def launch():
        if not (queue and free and JOB_KIND[queue[0] // 2] in ready):
            return
        if running and steps_done[running[-1][1]] < 1:
            return
        j = queue.pop(0)
        slot = free.pop(0)
        fill(j, slot)
        gen = phases(j, slot, slot in used, lambda: len(queue) > len(free))
        used.add(slot)
        next(gen)
        steps_done[j] = 0
        running.append((gen, j, slot))

    def service(count=1):
        for _ in range(count):
            old = list(tails)
            for entry in list(running):
                gen, j, slot = entry
                try:
                    next(gen)
                    steps_done[j] += 1
                except StopIteration:
                    running[:] = [e for e in running if e is not entry]
                    free.append(slot)
                    t = tail(j)
                    next(t)
                    tails.append(t)
            launch()
            for gen in old:
                try:
                    next(gen)
                except StopIteration:
                    tails.remove(gen)

    tile[...] = jnp.zeros((8, 128), F32)
    biasp[...] = jnp.zeros((160, 128), F32)
    dmod[...] = jnp.zeros((2, 8, 1024), F32)
    loads["h3"].wait()
    loads["dl"].wait()
    launch()
    loads["h2"] = load(0, r["h2_i"], hh)

    def store_bias(start, val):
        for i in range(val.shape[1] // 128):
            biasp[pl.ds(start + i, 1), :] = val[:, 128 * i : 128 * i + 128]

    def blocks(fn):
        for img in range(2):
            def body(i, carry, img=img):
                fn(img, pl.ds(pl.multiple_of(img * 128 + i * 32, 32), 32))
                return carry
            lax.fori_loop(0, 4, body, 0)

    def exchange(k, ref):
        cp = remote(ref.at[c], ref.at[c], ps.at[k], pr.at[k], mate)
        cp.start()
        return cp

    def swap(k):
        cp = remote(acc.at[1 - c], got, ps.at[k], pr.at[k], mate)
        cp.start()
        return cp

    def back_rows(grad, count):
        def body(i, carry):
            for half in range(2):
                part = lax.dot_general(
                    grad[i, 256 * half : 256 * half + 256, :], wb[i // 4, lax.rem(i, 4)], NT,
                    preferred_element_type=F32,
                )

                @pl.when(i == 0)
                def _():
                    acc[half] = part

                @pl.when(i > 0)
                def _():
                    acc[half] += part

            return carry
        lax.fori_loop(0, count, body, 0)

    def norm_back(img, v, scale, shift, dy):
        center = v - jnp.mean(v, -1, keepdims=True)
        inv = lax.rsqrt(jnp.mean(center * center, -1, keepdims=True) + NORM_EPS)
        unit = center * inv
        dmod[img, scale : scale + 1, :] += jnp.sum(dy * unit, axis=0, keepdims=True)
        dmod[img, shift : shift + 1, :] += jnp.sum(dy, axis=0, keepdims=True)
        dn = dy * (1.0 + ada_row(ada, scale, img))
        return inv * (
            dn - jnp.mean(dn, -1, keepdims=True) - unit * jnp.mean(dn * unit, -1, keepdims=True)
        )

    loads["w3"].wait()
    back_rows(dl, 8)
    cp = swap(0)
    w_next = load(2, r["w_i"].at[:, :, 2], wb)

    def head_bias(i, carry):
        store_bias(128 + (2 * i + c) * 2, jnp.sum(dl[i].astype(F32), axis=0, keepdims=True))
        return carry

    lax.fori_loop(0, 8, head_bias, 0)
    service()
    loads["x2"].wait()
    loads["mlp"].wait()
    cp.wait()
    fc2_rows = jnp.zeros((1, 1024), F32)

    def do_x2(img, rows):
        grad = norm_back(img, xa[rows, :], 6, 7, acc[c, rows, :] + got[rows, :])
        dx[rows, :] = grad
        dmod[img, 1:2, :] += jnp.sum(grad * xb[rows, :], axis=0, keepdims=True)
        low = (ada_row(ada, 1, img) * grad).astype(BF16)
        dm[c, rows, :] = low
        r["gst"][0, 0:1, :] += jnp.sum(low.astype(F32), axis=0, keepdims=True)

    r["gst"][0, 0:1, :] = fc2_rows
    blocks(do_x2)
    cp = exchange(1, dm)
    store_bias(120, r["gst"][0, 0:1, :])
    loads["x1"] = load(3, r["x1_i"], xa)
    loads["att"] = load(4, r["att_i"], xb)
    cp.wait()
    loads["u"].wait()
    ready.add(2)
    service()
    w_next.wait()

    fb = r["fb"]

    def f_load(i):
        return pltpu.make_async_copy(r["f_i"].at[i], fb.at[lax.rem(i, 2)], fs.at[lax.rem(i, 2)])

    f_load(0).start()

    def do_df(i, carry):
        @pl.when(i < 7)
        def _():
            f_load(i + 1).start()

        du = jnp.dot(dm[...].reshape(512, 1024), wb[i // 4, lax.rem(i, 4)], preferred_element_type=F32)
        f_load(i).wait()
        v = fb[lax.rem(i, 2)]
        k0 = 0.7978845608028654
        th = jnp.tanh(k0 * (v + 0.044715 * (v * v * v)))
        slope = 0.5 * (1.0 + th) + 0.5 * v * (1.0 - th * th) * (k0 * (1.0 + 3.0 * 0.044715 * (v * v)))
        df = (slope * du).astype(BF16)
        dl[i] = df
        store_bias(88 + (2 * i + c) * 2, jnp.sum(df.astype(F32), axis=0, keepdims=True))
        return carry

    while 1 in queue:
        service()
    lax.fori_loop(0, 8, do_df, 0)
    ready.add(1)
    w_next = load(2, r["w_i"].at[:, :, 1], wb)
    service()
    w_next.wait()
    back_rows(dl, 8)
    cp = swap(2)
    w_next = load(2, r["wo_i"], wb.at[0])
    loads["x1"].wait()
    loads["att"].wait()
    loads["ot"].wait()
    ot_swap = exchange(3, otp)
    service()
    cp.wait()

    def do_x1(img, rows):
        grad = norm_back(img, xa[rows, :], 3, 5, acc[c, rows, :] + got[rows, :]) + dx[rows, :]
        dmod[img, 0:1, :] += jnp.sum(grad * xb[rows, :], axis=0, keepdims=True)
        low = (ada_row(ada, 0, img) * grad).astype(BF16)
        da[c, rows, :] = low
        r["gst"][0, 0:1, :] += jnp.sum(low.astype(F32), axis=0, keepdims=True)

    r["gst"][0, 0:1, :] = fc2_rows
    blocks(do_x1)
    da_swap = exchange(4, da)
    store_bias(80, r["gst"][0, 0:1, :])
    w_next.wait()
    dov, doh, hb = r["dov"], r["doh"], r["hb"]
    for img in range(2):
        rows = pl.ds(128 * img, 128)
        low = jnp.zeros((128, 1024), F32)
        for k in range(4):
            low += lax.dot_general(
                da[c, rows, 256 * k : 256 * k + 256], wb[0, k], NT, preferred_element_type=F32
            )
        dov[img] = low.astype(BF16)
    w_next = load(2, r["w_i"].at[:, :, 0], wb)

    def do_sends(fn):
        for p in range(4):
            for q in range(2):
                src = dov.at[:, :, pl.ds(((p // 2 * 2 + q) * 2 + p % 2) * 128, 128)]
                cp = remote(src, doh.at[sq], hs.at[p, q], hr.at[sq], (base + q, p * 2 + c))

                @pl.when(jnp.logical_not(jnp.logical_and(sq == p * 2 + c, c == q)))
                def _():
                    fn(cp)

    do_sends(lambda cp: cp.start())

    @pl.when(owner == c)
    def _():
        doh[sq] = dov[:, :, head_lanes(pair, c)]

    kcol = r["kcol"]
    for img in range(2):
        for g in range(8):
            kcol[img, g] = column_of(slots_all[g * 2 + owner, pl.ds(img, 1), :])
    service()
    for i in range(8):
        landed = doh.at[i]

        @pl.when(jnp.logical_or(sq != i, owner != c))
        def _():
            remote(landed, landed, hs.at[0, 0], hr.at[i], mate).wait_recv()

    loads["hb"].wait()
    dkv, dsrc, dr, dq6 = r["dkv"], r["dsrc"], r["dr"], r["dq6"]
    low_lanes = lax.broadcasted_iota(jnp.int32, (256, 128), 1) < 64
    low_rows = lax.broadcasted_iota(jnp.int32, (128, 256), 0) < 64

    for img in range(2):
        dkv[...] = jnp.zeros((2, 1024, 128), F32)

        def attend_block(qb, carry, img=img):
            q = jnp.concatenate([hb[2 * qb, 0, img], hb[2 * qb + 1, 0, img]], axis=0)
            k = jnp.concatenate([hb[g, 1, img] for g in range(8)], axis=0)
            v = jnp.concatenate([hb[g, 2, img] for g in range(8)], axis=0)
            do = jnp.concatenate([doh[2 * qb, img], doh[2 * qb + 1, img]], axis=0)
            kT = jnp.transpose(k)
            key = jnp.concatenate([kcol[img, g] for g in range(8)], axis=0)[:, 0:1]
            query = jnp.concatenate(
                [slots_all[(2 * qb + i) * 2 + owner, 2 + img : 3 + img, :] for i in range(2)], axis=1
            )
            seen_by = key <= query
            heads = []
            for h in range(2):
                mask = low_lanes if h == 0 else jnp.logical_not(low_lanes)
                qh = jnp.where(mask, q, jnp.zeros_like(q))
                doh_h = jnp.where(mask, do, jnp.zeros_like(do))
                sc = lax.dot_general(k, qh, NT, preferred_element_type=F32) * SCORE_SCALE
                sc = jnp.where(seen_by, sc, -1e30)
                e = jnp.exp(sc - jnp.max(sc, axis=0, keepdims=True))
                p = e / jnp.sum(e, axis=0, keepdims=True)
                dpr = lax.dot_general(v, doh_h, NT, preferred_element_type=F32)
                inner = jnp.sum(p * dpr, axis=0, keepdims=True)
                ds = (p * (dpr - inner)).astype(BF16)
                dkv[0] += jnp.dot(ds, qh, preferred_element_type=F32)
                dkv[1] += jnp.dot(p.astype(BF16), doh_h, preferred_element_type=F32)
                heads.append(jnp.dot(kT, ds, preferred_element_type=F32))
            dq = jnp.transpose(jnp.where(low_rows, heads[0], heads[1]) * SCORE_SCALE).astype(BF16)
            dsrc[2 * qb, 0, img] = dq[:128]
            dsrc[2 * qb + 1, 0, img] = dq[128:]
            return carry

        lax.fori_loop(0, 4, attend_block, 0)
        for g in range(8):
            dsrc[g, 1, img] = (dkv[0, 128 * g : 128 * g + 128] * SCORE_SCALE).astype(BF16)
            dsrc[g, 2, img] = dkv[1, 128 * g : 128 * g + 128].astype(BF16)
        if img == 0:
            service()
    sends = []
    for i, to in enumerate(line):
        cp = remote(dsrc.at[to], dr.at[sq], as_.at[i], ar.at[i], (dp, to))
        cp.start()
        sends.append(cp)
    dr[sq] = dsrc[sq]
    service(2)
    for cp in sends:
        cp.wait()
    for t in range(3):
        for jj in range(2):
            for half in range(2):
                for ip in range(2):
                    dq6[t * 2 + jj, ip * 256 : ip * 256 + 256, half * 128 : half * 128 + 128] = dr[
                        (jj * 2 + half) * 2 + ip, t
                    ].reshape(256, 128)
    for jj in range(2):
        for start, t in ((64, 0), (72, 2)):
            store_bias(
                start + (2 * jj + c) * 2,
                jnp.sum(dq6[t * 2 + jj].astype(F32), axis=0, keepdims=True),
            )
    w_next.wait()
    back_rows(dq6, 6)
    cp = swap(5)
    ot_swap.wait()
    da_swap.wait()
    ready.add(0)
    service()
    cp.wait()

    def do_x0(img, rows):
        norm_back(img, r["x_in"][rows, :].astype(F32), 2, 4, acc[c, rows, :] + got[rows, :])

    blocks(do_x0)
    do_sends(lambda cp: cp.wait_send())

    smsg, sgot, smine = r["smsg"], r["sgot"], r["smine"]
    sall, spart, sback = r["sall"], r["spart"], r["sback"]
    for k in range(8):
        both = dmod[0, k : k + 1, :] + dmod[1, k : k + 1, :]
        for i in range(8):
            biasp[8 * k + i : 8 * k + i + 1, :] = both[:, 128 * i : 128 * i + 128]
    for d in range(16):
        for img in range(2):
            for i in range(4):
                lo = (d % 2) * 512 + i * 128
                smsg[d, img * 4 + i : img * 4 + i + 1, :] = dmod[img, d // 2 : d // 2 + 1, lo : lo + 128]
        smsg[d, 8:18, :] = biasp[10 * d : 10 * d + 10, :]
        smsg[d, 18:24, :] = jnp.broadcast_to(r["loss"][0:1, :], (6, 128))
    cps = []
    for i, d in enumerate(row):
        cp = remote(smsg.at[d], sgot.at[dp], s1.at[i], r1.at[i], (d, sq))
        cp.start()
        cps.append(cp)
    sgot[dp] = smsg[dp]
    service()
    for cp in cps:
        cp.wait()
    for d in range(16):
        smine[d] = sgot[d, 0:8, :]
    for i in range(2):
        smine[16 + i] = sum(sgot[d, 8 + 8 * i : 16 + 8 * i, :] for d in range(16))
    cps = []
    for i, s in enumerate(line):
        cp = remote(smine, sall.at[sq], s2.at[i], r2.at[i], (dp, s))
        cp.start()
        cps.append(cp)
    sall[sq] = smine[...]
    service()
    for cp in cps:
        cp.wait()
    for k in range(18):
        smine[k] = sum(sall[s, k] for s in range(8))
    r["bias_sum"][0] = smine[16]
    r["bias_sum"][1] = smine[17]
    dada = jnp.concatenate(
        [
            jnp.concatenate([smine[d, 4 * i + k : 4 * i + k + 1, :] for k in range(4)], axis=1)
            for d in range(16)
            for i in range(2)
        ],
        axis=0,
    )

    def dcond_part(d, carry):
        rows = pl.ds(pl.multiple_of(64 * d, 64), 64)
        spart[d] = lax.dot_general(
            dada, r["cond_w"][rows, :].astype(F32), NT, precision=HIGH, preferred_element_type=F32
        )
        return carry

    lax.fori_loop(0, 16, dcond_part, 0)
    cps = []
    for i, d in enumerate(row):
        cp = remote(spart.at[d], sback.at[dp], s3.at[i], r3.at[i], (d, sq))
        cp.start()
        cps.append(cp)
    sback[dp] = spart[dp]
    service()
    squares = jnp.zeros((8, 128), F32)

    def fold(val):
        total = jnp.zeros((8, 128), F32)
        for i in range(val.shape[0] // 8):
            for k in range(val.shape[1] // 128):
                total = total + val[8 * i : 8 * i + 8, 128 * k : 128 * k + 128]
        return total

    gcs = r["gcs"]

    def gcond_copy(d):
        slot = lax.rem(d, 2)
        rows = pl.ds(pl.multiple_of(64 * d, 64), 64)
        return pltpu.make_async_copy(gcs.at[slot], r["gcond"].at[rows], gl.at[slot])

    def gcond_part(d, total):
        @pl.when(d > 1)
        def _():
            gcond_copy(d - 2).wait()

        val = lax.dot_general(
            r["cond_all"][d].astype(F32), dada, (((0,), (0,)), ((), ())),
            precision=HIGH, preferred_element_type=F32,
        )
        gcs[lax.rem(d, 2)] = val
        gcond_copy(d).start()
        return total + fold(val * val)

    squares = squares + lax.fori_loop(0, 16, gcond_part, squares)
    gcond_copy(14).wait()
    gcond_copy(15).wait()
    for cp in cps:
        cp.wait()
    dcond = sum(sback[d] for d in range(16))
    emb = r["emb"][...]
    sig = 1.0 / (1.0 + jnp.exp(-emb))
    demb = dcond * (sig * (1.0 + emb * (1.0 - sig)))
    labels = jnp.concatenate(
        [msg_all[d, 10:11, i : i + 1] for d in range(16) for i in range(2)], axis=0
    ).astype(jnp.int32)
    hit = jnp.where(lax.broadcasted_iota(jnp.int32, (32, 1000), 1) == labels, 1.0, 0.0)
    gtable = jnp.dot(jnp.transpose(demb), hit, precision=HIGH, preferred_element_type=F32)
    r["gtable"][...] = gtable
    table_squares = jnp.sum(jnp.sum(gtable * gtable, axis=1, keepdims=True), axis=0, keepdims=True)
    bias_rows = jnp.concatenate([smine[16], smine[17][0:2]], axis=0)
    bias_squares = jnp.sum(jnp.sum(bias_rows * bias_rows, axis=1, keepdims=True), axis=0, keepdims=True)
    spot = jnp.logical_and(
        lax.broadcasted_iota(jnp.int32, (8, 128), 0) == 0, lax.broadcasted_iota(jnp.int32, (8, 128), 1) == 0
    )
    squares = squares + jnp.where(spot, table_squares + bias_squares, 0.0)
    while queue or running:
        service()
    tile[...] += squares * 0.125
    tiles = r["tiles"]
    cps = []
    for i, d in enumerate(row):
        cp = remote(tile, tiles.at[i], ns.at[i], nr.at[i], (d, sq))
        cp.start()
        cps.append(cp)
    for cp in cps:
        cp.wait()
    tile[...] += sum(tiles[i] for i in range(15))
    cps = []
    for i, d in enumerate(line):
        cp = remote(tile, tiles.at[15 + i], ns.at[15 + i], nr.at[15 + i], (dp, d))
        cp.start()
        cps.append(cp)
    service()
    for cp in cps:
        cp.wait()
    r["norm"][...] = tile[...] + sum(tiles[15 + i] for i in range(7))
    while tails:
        service()
    for cp in unsent:
        cp.wait_send()


def backward_pass(small, kept):
    dma = pltpu.SemaphoreType.DMA
    sd = jax.ShapeDtypeStruct
    vm = pltpu.VMEM
    scratch = [
        vm((2, 4, 1024, 256), BF16),
        vm((8, 512, 256), BF16), vm((8, 512, 256), BF16), vm((2, 512, 256), F32),
        vm((2, 256, 1024), BF16), vm((1024, 512), BF16), vm((1024, 512), BF16),
        vm((2, 256, 1024), BF16), vm((2, 256, 1024), BF16), vm((2, 256, 1024), BF16),
        vm((2, 256, 1024), F32), vm((256, 1024), F32), vm((256, 1024), F32), vm((256, 1024), F32),
        vm((256, 1024), F32),
        vm((8, 3, 2, 128, 128), BF16), vm((8, 2, 128, 128), BF16), vm((2, 128, 1024), BF16),
        vm((2, 1024, 128), F32), vm((8, 3, 2, 128, 128), BF16), vm((8, 3, 2, 128, 128), BF16),
        vm((6, 512, 256), BF16), vm((2, 8, 128, 128), F32), vm((2, 8, 1024), F32), vm((160, 128), F32),
        vm((16, 24, 128), F32), vm((16, 24, 128), F32), vm((18, 8, 128), F32), vm((8, 18, 8, 128), F32),
        vm((16, 32, 64), F32), vm((16, 32, 64), F32), vm((1, 8, 1024), F32),
        vm((2, 64, 512), F32),
        vm((8, 128), F32), vm((22, 8, 128), F32),
    ]
    for _ in range(SLOTS):
        for p in range(3):
            scratch.append(vm((2, 4, 4, 2, PART_ROWS[p], 256), F32))
    for p in range(3):
        scratch.append(vm((JOBS, PART_ROWS[p], 256), F32))
    scratch += [vm(shape, F32) for shape in recv_shapes()]
    scratch += [
        dma((9,)), dma((2,)), dma((6,)), dma((6,)), dma((4, 2)), dma((8,)), dma, dma((7,)), dma((7,)),
        dma((JOBS, 9, 4)), dma((JOBS, 9, 4)), dma((JOBS, 3, 5)), dma((JOBS, 3, 5)), dma((JOBS, 3)),
        pltpu.SemaphoreType.REGULAR((SLOTS,)),
        dma((15,)), dma((15,)), dma((7,)), dma((7,)), dma((15,)), dma((15,)), dma((22,)), dma((22,)),
        dma((2,)),
    ]
    return pl.pallas_call(
        backward_kernel,
        out_shape=[
            sd((4, 1024, 256), F32), sd((8, 128), F32), sd((2, 8, 128), F32),
            sd((64, 1000), F32), sd((1024, 512), F32),
        ],
        in_specs=[VM] * len(small) + [ANY] * len(kept),
        out_specs=[ANY, VM, VM, VM, ANY],
        scratch_shapes=scratch,
        compiler_params=params(1, 64 * 2**20 - 2**17),
    )(*small, *kept)


def adamw(weight, first, second, grad, factor):
    clipped = grad * factor
    first_new = BETA_ONE * first + (1.0 - BETA_ONE) * clipped
    second_new = BETA_TWO * second + (1.0 - BETA_TWO) * clipped * clipped
    first_hat = first_new / (1.0 - BETA_ONE**STEP)
    second_hat = second_new / (1.0 - BETA_TWO**STEP)
    weight_new = weight - LEARN * (first_hat / (jnp.sqrt(second_hat) + ADAM_EPS) + DECAY * weight)
    return (weight_new, first_new, second_new)


def local(
    x_in, scale_ids, pad_mask, loss_weights, targets, labels,
    cond_w, attn_w, mlp_w, head_w, class_table, biases,
    first_cond, first_attn, first_mlp, first_head, first_table, first_bias,
    second_cond, second_attn, second_mlp, second_head, second_table, second_bias,
):
    wb_cond = cond_w.astype(BF16)
    shard = jnp.stack([attn_w, mlp_w[0], mlp_w[1], head_w]).astype(BF16)

    x_rows = x_in.reshape(256, 1024)
    count_part = jnp.sum(pad_mask.astype(F32))
    row = jnp.concatenate([labels.astype(F32), count_part[None], jnp.zeros((125,), F32)])
    rounded = lax.reduce_precision(biases, 8, 7).reshape(10, 128)
    msg = jnp.concatenate([rounded, row[None], jnp.zeros((5, 128), F32)])
    level = jnp.where(pad_mask > 0, scale_ids, 1000).astype(F32)
    weight_own = (loss_weights * pad_mask).astype(F32)
    slots = jnp.concatenate(
        [level, scale_ids.astype(F32), targets.astype(F32), weight_own, jnp.zeros((8, 128), F32)]
    )
    (
        msg_all, slots_all, cond_all, embedded, ada, loss_tile,
        w, wo, h1, h2, h3, heads, o, att, x1, mlp, x2, f, u, dlogits,
    ) = forward_pass(msg, slots, class_table.T.astype(BF16), wb_cond, x_rows, shard)
    true_count = jnp.sum(slots_all.reshape(8, 2, 16, 128)[:, 0, 8, 0])
    summed, squares, bias_sum, grad_table, grad_cond = backward_pass(
        (msg_all, slots_all, cond_all, embedded, ada, loss_tile, wb_cond, x_rows),
        (w, wo, h1, h2, h3, heads, o, att, x1, mlp, x2, f, u, dlogits),
    )
    bias_sum = bias_sum.reshape(16, 128)
    loss_total = bias_sum[10, 0]
    grad_bias = bias_sum[:10].reshape(1280)
    grad_norm = jnp.sqrt(jnp.sum(squares))
    factor = jnp.minimum(1.0, CLIP / grad_norm)
    grads = (grad_cond, summed[0], summed[1:3], summed[3], grad_table, grad_bias)
    weights = (cond_w, attn_w, mlp_w, head_w, class_table.T, biases)
    firsts = (first_cond, first_attn, first_mlp, first_head, first_table.T, first_bias)
    seconds = (second_cond, second_attn, second_mlp, second_head, second_table.T, second_bias)
    results = [
        adamw(weight, first, second, grad, factor)
        for weight, first, second, grad in zip(weights, firsts, seconds, grads)
    ]
    new_weights = [entry[0] for entry in results]
    new_first = [entry[1] for entry in results]
    new_second = [entry[2] for entry in results]
    copies = [weight.astype(BF16) for weight in new_weights]
    for group in (new_weights, new_first, new_second, copies):
        group[4] = group[4].T
    return tuple(new_weights + new_first + new_second + copies + [grad_norm, loss_total, true_count])


def solution(mesh):
    split = (P(None, "dp"), P(None, "dp"), P(None, None, "dp"), P(None, "dp"), P(None, "dp"), P("dp"))
    in_specs = (P("dp", "seq", None),) + (P("dp", "seq"),) * 4 + (P("dp"),) + split * 3
    out_specs = split * 4 + (P(), P(), P())
    return jax.shard_map(local, mesh=mesh, in_specs=in_specs, out_specs=out_specs, check_vma=False)
```

```python
import functools

import jax
import jax.numpy as jnp
from jax import lax
from jax.experimental import pallas as pl
from jax.experimental.pallas import tpu as pltpu
from jax.sharding import PartitionSpec as P

STEP = 5
HIGH = lax.Precision.HIGHEST
NORM_EPS = 1e-06
CLIP = 0.01
LEARN = 0.02
DECAY = 0.1
BETA_ONE = 0.5
BETA_TWO = 0.5
ADAM_EPS = 1e-08
SCORE_SCALE = 0.125
MESH = pl.DeviceIdType.MESH
F32 = jnp.float32
BF16 = jnp.bfloat16
ANY = pl.BlockSpec(memory_space=pl.ANY)
VM = pl.BlockSpec(memory_space=pltpu.VMEM)

ROWS_YZ = 320
HALF_YZ = 160
QUARTER = 48


def place():
    dp = lax.axis_index("dp")
    sq = lax.axis_index("seq")
    core = lax.rem(dp, 2)
    y = lax.rem(dp // 2, 4)
    z = lax.rem(sq, 2) * 2 + dp // 8
    return sq // 2, y, z, core


def at(x, y, z, core):
    x, y, z = lax.rem(x + 4, 4), lax.rem(y + 4, 4), lax.rem(z + 4, 4)
    return (lax.rem(z, 2) * 8 + y * 2 + core, x * 2 + z // 2)


def greet(devices):
    bar = pltpu.get_barrier_semaphore()
    for device in devices:
        pl.semaphore_signal(bar, inc=1, device_id=device, device_id_type=MESH)
    pl.semaphore_wait(bar, len(devices))


def remote(src, dst, send, recv, device):
    return pltpu.make_async_remote_copy(
        src_ref=src, dst_ref=dst, send_sem=send, recv_sem=recv, device_id=device, device_id_type=MESH
    )


def params(collective_id, vmem=None):
    return pltpu.CompilerParams(
        collective_id=collective_id, has_side_effects=True, vmem_limit_bytes=vmem
    )


def group_peers():
    dp = lax.axis_index("dp")
    sq = lax.axis_index("seq")
    core = lax.rem(dp, 2)
    out = [(dp + 1 - 2 * core, sq)]
    for i in range(1, 8):
        for flip in range(2):
            out.append((dp + flip * (1 - 2 * core), lax.rem(sq + i, 8)))
    return out


def head_lanes(pair, core):
    return pl.ds(pl.multiple_of(((pair // 2 * 2 + core) * 2 + lax.rem(pair, 2)) * 128, 128), 128)


NT = (((1,), (1,)), ((), ()))


def normalize(v):
    center = v - jnp.mean(v, -1, keepdims=True)
    spread = jnp.mean(center * center, -1, keepdims=True)
    return center * lax.rsqrt(spread + NORM_EPS)


def ada_row(ada, k, img):
    return jnp.concatenate([ada[2 * k, img : img + 1, :], ada[2 * k + 1, img : img + 1, :]], axis=1)


def column_of(row):
    return jnp.transpose(jnp.broadcast_to(row, (128, 128)))


def forward_kernel(
    msg, slots, table, cond_w, x_in, attn_in, mlp_in, head_in,
    msg_all, slots_all, cond_all, emb_out, ada, loss_out, cond_low,
    w_o, wo_o, h1_o, h2_o, h3_o, hb_o, ot_o, att_o, x1_o, mlp_o, x2_o, f_o, u_o, dl_o,
    w, wo, h1, h2, h3, src, hb, oh, ot, att, x1, mlp, x2, acc, got_acc, f, u, dl,
    cond_own, ada_own, bias, qcol, tcol, wcol, stats,
    gs, gr, gl, os, orr, s1, r1, s2, r2, s3, r3, s4, r4, ps, pr, as_, ar, al, ts, tr, tl, outs_sem,
):
    x, y, z, c = place()
    dp = lax.axis_index("dp")
    sq = lax.axis_index("seq")
    zl = lax.rem(z, 2)
    up, down, far = lax.rem(y + 1, 4), lax.rem(y + 3, 4), lax.rem(y + 2, 4)
    yp, ym = at(x, y + 1, z, c), at(x, y - 1, z, c)
    zp, zm = at(x, y, z + 1, c), at(x, y, z - 1, c)
    xp, xm = at(x + 1, y, z, c), at(x - 1, y, z, c)
    zs = at(x, y, z + 1 - 2 * c, c)
    mate = at(x, y, z, 1 - c)
    base = dp - c
    row = [(lax.rem(dp + i, 16), sq) for i in range(1, 16)]
    group = group_peers()
    incoming = []
    for j in range(8):
        rows = pl.ds(512 * (j % 2), 512)
        source = (attn_in, mlp_in.at[0], mlp_in.at[1], head_in)[j // 2]
        incoming.append(pltpu.make_async_copy(source.at[rows], f.at[j], gl.at[j, 0]))
        incoming[-1].start()
    greet(row + group[1:] + [at(x, y, z + 2 * zl - 1, c)])

    pending = []

    def keep(k, src_ref, dst_ref):
        cp = pltpu.make_async_copy(src_ref, dst_ref, outs_sem.at[k])
        cp.start()
        pending.append(cp)
        return cp

    def rows_at(j, start, count):
        return pl.ds(512 * (j % 2) + start, count)

    def quarter(j, pos):
        start = 512 * (j % 2) + ROWS_YZ + QUARTER * lax.rem(pos + 4, 4)
        return pl.ds(pl.multiple_of(start, 16), QUARTER)

    sent = []

    def go(j, k, a, b, device):
        cp = remote(a, b, gs.at[j, k], gr.at[j, k], device)
        cp.start()
        sent.append(cp)

    def got(j, k, ref):
        remote(ref, ref, gs.at[j, k], gr.at[j, k], mate).wait_recv()

    def stage(kind, j):
        m = j // 2
        full, first = rows_at(j, 0, ROWS_YZ), rows_at(j, 0, HALF_YZ)
        second, mine = rows_at(j, HALF_YZ, HALF_YZ), quarter(j, x)
        if kind == "A":
            incoming[j].wait()
            w[zl, y, m, full, :] = f[j, 0:ROWS_YZ, :].astype(BF16)
            at_rows = pl.ds(pl.multiple_of(ROWS_YZ + QUARTER * x, 16), QUARTER)
            w[zl, y, m, mine, :] = f[j, at_rows, :].astype(BF16)
            go(j, 0, w.at[zl, y, m, full], w.at[zl, y, m, full], yp)
            go(j, 1, w.at[zl, y, m, full], w.at[zl, y, m, full], ym)
            go(j, 6, w.at[zl, y, m, mine], w.at[zl, y, m, mine], zs)
        if kind == "B":
            got(j, 6, w.at[1 - zl, y, m, mine])
            go(j, 7, w.at[:, y, m, mine], w.at[:, y, m, mine], yp)
            go(j, 8, w.at[:, y, m, mine], w.at[:, y, m, mine], ym)
            got(j, 0, w.at[zl, down, m, full])
            got(j, 1, w.at[zl, up, m, full])
            go(j, 2, w.at[zl, down, m, first], w.at[zl, down, m, first], yp)
            go(j, 3, w.at[zl, up, m, second], w.at[zl, up, m, second], ym)
        if kind == "C":
            got(j, 7, w.at[:, down, m, mine])
            got(j, 8, w.at[:, up, m, mine])
            go(j, 9, w.at[0, down, m, mine], w.at[0, down, m, mine], yp)
            go(j, 10, w.at[1, up, m, mine], w.at[1, up, m, mine], ym)
            got(j, 2, w.at[zl, far, m, first])
            got(j, 3, w.at[zl, far, m, second])
            go(j, 4, w.at[zl, :, m, first], w.at[zl, :, m, first], zp)
            go(j, 5, w.at[zl, :, m, second], w.at[zl, :, m, second], zm)
        if kind == "D":
            got(j, 9, w.at[0, far, m, mine])
            got(j, 10, w.at[1, far, m, mine])
            go(j, 11, w.at[:, :, m, mine], w.at[:, :, m, mine], xp)
            go(j, 12, w.at[:, :, m, mine], w.at[:, :, m, mine], xm)
        if kind == "E":
            left, right = quarter(j, x - 1), quarter(j, x + 1)
            got(j, 11, w.at[:, :, m, left])
            got(j, 12, w.at[:, :, m, right])
            go(j, 13, w.at[0, :, m, left], w.at[0, :, m, left], xp)
            go(j, 14, w.at[1, :, m, right], w.at[1, :, m, right], xm)
        if kind == "F":
            across = quarter(j, x + 2)
            got(j, 4, w.at[1 - zl, :, m, first])
            got(j, 5, w.at[1 - zl, :, m, second])
            got(j, 13, w.at[0, :, m, across])
            got(j, 14, w.at[1, :, m, across])
            if j % 2:
                keep(m, w.at[:, :, m], w_o.at[:, :, m])
            if j == 1:
                for i in range(2):
                    remote(w.at[1, 2 + i, 0], wo.at[2 * i + c], os.at[i], orr.at[i], mate).start()
                    pltpu.make_async_copy(w.at[1, 2 + i, 0], wo.at[2 * i + c], gl.at[i, 2]).start()

    wave = [
        ["A0", "A1"], ["B0", "B1", "A2"], ["C0", "C1", "B2", "D0", "D1", "A3"],
        ["E0", "E1", "C2", "B3", "A4"], ["F0", "F1"], ["D2", "C3", "B4", "A5"],
        ["E2", "D3", "C4", "B5", "A6"], ["F2", "E3", "D4", "C5", "B6", "A7"],
        ["F3", "E4", "D5", "C6", "B7"], ["F4", "E5", "D6", "C7"],
        ["F5", "E6", "D7"], ["F6", "E7"], ["F7"],
    ]

    def pump(n=1):
        for _ in range(n):
            if wave:
                for item in wave.pop(0):
                    stage(item[0], int(item[1]))

    firsts = []
    for i, to in enumerate(row):
        cp = remote(msg, msg_all.at[dp], s1.at[i], r1.at[i], to)
        cp.start()
        firsts.append(cp)
    msg_all[dp] = msg[...]
    pump()
    for cp in firsts:
        cp.wait()
    seen = msg_all[...]
    count = jnp.sum(seen[:, 10, 2:3], axis=0, keepdims=True)
    slots[8:9, :] = jnp.broadcast_to(count, (1, 128))
    for d in range(16):
        bias[pl.ds(10 * d, 10), :] = seen[d, 0:10, :]
    seconds = []
    for i, to in enumerate(group):
        cp = remote(slots, slots_all.at[sq * 2 + c], s2.at[i], r2.at[i], to)
        cp.start()
        seconds.append(cp)
    slots_all[sq * 2 + c] = slots[...]
    classes = table.shape[1]
    lane = lax.broadcasted_iota(jnp.int32, (32, classes), 1)
    labels = jnp.concatenate([seen[d, 10:11, i : i + 1] for d in range(16) for i in range(2)], axis=0)
    hit = jnp.where(lane == labels.astype(jnp.int32), 1.0, 0.0).astype(BF16)
    emb = lax.dot_general(hit, table[...].astype(BF16), NT, preferred_element_type=F32)
    emb_out[...] = emb
    cond_own[...] = (emb / (1.0 + jnp.exp(-emb))).astype(BF16)
    cond_all[dp] = cond_own[...]
    thirds = []
    for i, to in enumerate(row):
        cp = remote(cond_own, cond_all.at[dp], s3.at[i], r3.at[i], to)
        cp.start()
        thirds.append(cp)
    pump()
    for cp in thirds:
        cp.wait()
    total = jnp.zeros((32, 512), F32)
    for d in range(16):
        low = cond_w[pl.ds(64 * d, 64), :].astype(BF16)
        cond_low[pl.ds(64 * d, 64), :] = low
        total += jnp.dot(cond_all[d], low, preferred_element_type=F32)
    total += jnp.concatenate([bias[pl.ds(dp * 4 + i, 1), :] for i in range(4)], axis=1)
    for d in range(16):
        ada_own[d] = total[2 * d : 2 * d + 2]
    fourths = []
    for i in range(15):
        to = lax.rem(dp + 1 + i, 16)
        cp = remote(ada_own.at[to], ada.at[dp], s4.at[i], r4.at[i], (to, sq))
        cp.start()
        fourths.append(cp)
    ada[dp] = ada_own[dp]
    pump()
    for cp in fourths:
        cp.wait()
    for cp in seconds:
        cp.wait()

    owner = lax.rem(sq, 2)
    for img in range(2):
        for g in range(8):
            qcol[img, g] = column_of(slots_all[g * 2 + owner, pl.ds(2 + img, 1), :])
        for q in range(2):
            at_rows = pl.ds((q * 2 + img) * 128, 128)
            tcol[at_rows, :] = column_of(slots_all[sq * 2 + q, pl.ds(4 + img, 1), :])
            wcol[at_rows, :] = column_of(slots_all[sq * 2 + q, pl.ds(6 + img, 1), :])
    true_count = jnp.sum(
        jnp.concatenate([slots_all[2 * g, 8:9, 0:1] for g in range(8)], axis=0), axis=0, keepdims=True
    )

    def blocks(fn):
        for img in range(2):
            def body(i, carry, img=img):
                fn(img, pl.ds(pl.multiple_of(img * 128 + i * 32, 32), 32))
                return carry
            lax.fori_loop(0, 4, body, 0)

    def exchange(k, ref):
        cp = remote(ref.at[c], ref.at[c], ps.at[k], pr.at[k], mate)
        cp.start()
        return cp

    def modulated(img, v, scale, shift):
        return (normalize(v) * (1.0 + ada_row(ada, scale, img)) + ada_row(ada, shift, img)).astype(BF16)

    def do_h1(img, rows):
        h1[c, rows, :] = modulated(img, x_in[rows, :].astype(F32), 2, 4)

    blocks(do_h1)
    cp = exchange(0, h1)
    pump()
    cp.wait()
    keep(4, h1, h1_o)
    pump()

    def bias_row(start):
        return jnp.concatenate([bias[pl.ds(start, 1), :], bias[pl.ds(start + 1, 1), :]], axis=1)

    tokens = h1[...].reshape(512, 1024)
    for j in range(6):
        t, jj = j // 2, j % 2
        val = jnp.dot(tokens, w[j // 4, j % 4, 0], preferred_element_type=F32)
        if t != 1:
            val = val + bias_row(64 + (0 if t == 0 else 8) + (2 * jj + c) * 2)
        val = val.astype(BF16)
        for half in range(2):
            for ip in range(2):
                src[(jj * 2 + half) * 2 + ip, t] = val[
                    ip * 256 : ip * 256 + 256, half * 128 : half * 128 + 128
                ].reshape(2, 128, 128)
    cps = [[], []]
    for img in range(2):
        for i in range(1, 8):
            to = lax.rem(sq + i, 8)
            cp = remote(
                src.at[to, :, img], hb.at[sq, :, img], as_.at[i, img], ar.at[i, img], (dp, to)
            )
            cp.start()
            cps[img].append(cp)
    hb[sq] = src[sq]
    pump()

    low_lanes = lax.broadcasted_iota(jnp.int32, (256, 128), 1) < 64

    def attend_block(i, carry):
        img, qb = i // 4, lax.rem(i, 4)
        q = jnp.concatenate([hb[2 * qb, 0, img], hb[2 * qb + 1, 0, img]], axis=0)
        k = jnp.concatenate([hb[g, 1, img] for g in range(8)], axis=0)
        v = jnp.concatenate([hb[g, 2, img] for g in range(8)], axis=0)
        key = jnp.concatenate([slots_all[g * 2 + owner, pl.ds(img, 1), :] for g in range(8)], axis=1)
        query = jnp.concatenate([qcol[img, 2 * qb], qcol[img, 2 * qb + 1]], axis=0)[:, 0:1]
        seen_by = key <= query
        heads = []
        for h in range(2):
            mask = low_lanes if h == 0 else jnp.logical_not(low_lanes)
            qh = jnp.where(mask, q, jnp.zeros_like(q))
            sc = lax.dot_general(qh, k, NT, preferred_element_type=F32) * SCORE_SCALE
            sc = jnp.where(seen_by, sc, -1e30)
            e = jnp.exp(sc - jnp.max(sc, axis=-1, keepdims=True))
            p = (e / jnp.sum(e, axis=-1, keepdims=True)).astype(BF16)
            heads.append(jnp.dot(p, v, preferred_element_type=F32))
        o = jnp.where(low_lanes, heads[0], heads[1]).astype(BF16)
        oh[2 * qb, img] = o[:128]
        oh[2 * qb + 1, img] = o[128:]
        return carry

    pair = sq // 2
    lanes = head_lanes(pair, c)

    def o_copy(i, img):
        to = lax.rem(sq + i, 8)
        return remote(
            oh.at[to, img], ot.at[pl.ds(img * 128, 128), lanes], ts.at[i, img], tr.at[pair, c, img],
            (base + owner, to),
        )

    for img in range(2):
        for cp in cps[img]:
            cp.wait()
        lax.fori_loop(4 * img, 4 * img + 2, attend_block, 0)
        pump()
        lax.fori_loop(4 * img + 2, 4 * img + 4, attend_block, 0)
        for i in range(1, 8):
            o_copy(i, img).start()

        @pl.when(owner == c)
        def _():
            ot[pl.ds(img * 128, 128), lanes] = oh[sq, img]

        @pl.when(owner != c)
        def _():
            o_copy(0, img).start()

        pump()
    keep(5, hb, hb_o)
    for img in range(2):
        for p in range(4):
            for q in range(2):
                view = ot.at[pl.ds(img * 128, 128), pl.ds(((p // 2 * 2 + q) * 2 + p % 2) * 128, 128)]

                @pl.when(jnp.logical_or(sq != p * 2 + c, c != q))
                def _():
                    remote(view, view, ts.at[0, img], tr.at[p, q, img], mate).wait_recv()

    keep(6, ot, ot_o)
    for i in range(2):
        remote(w.at[1, 2 + i, 0], wo.at[2 * i + c], os.at[i], orr.at[i], mate).wait()
        pltpu.make_async_copy(w.at[1, 2 + i, 0], wo.at[2 * i + c], gl.at[i, 2]).wait()
    keep(7, wo, wo_o)
    for k in range(4):
        cols = pl.ds(256 * k, 256)
        att[:, cols] = jnp.dot(ot[...], wo[k], preferred_element_type=F32) + bias_row(80 + 2 * k)
    keep(8, att, att_o)

    def do_h2(img, rows):
        v = x_in[rows, :].astype(F32) + ada_row(ada, 0, img) * att[rows, :]
        x1[rows, :] = v
        h2[c, rows, :] = modulated(img, v, 3, 5)

    blocks(do_h2)
    cp = exchange(1, h2)
    keep(9, x1, x1_o)
    cp.wait()
    keep(10, h2, h2_o)
    pump()

    def chunk(ref, j, kind):
        return ref[j // 4, lax.rem(j, 4), kind]

    def do_f(j, carry):
        val = jnp.dot(h2[...].reshape(512, 1024), chunk(w, j, 1), preferred_element_type=F32)
        val = val + bias_row(88 + (2 * j + c) * 2)
        f[j] = val
        act = jax.nn.gelu(val, approximate=True).astype(BF16)
        u[j] = act
        part = lax.dot_general(act, chunk(w, j, 2), NT, preferred_element_type=F32).reshape(2, 256, 1024)

        @pl.when(j == 0)
        def _():
            acc[...] = part

        @pl.when(j > 0)
        def _():
            acc[...] += part

        return carry

    lax.fori_loop(0, 8, do_f, 0)
    f_copy = keep(11, f, f_o)
    keep(12, u, u_o)
    cp = remote(acc.at[1 - c], got_acc, ps.at[2], pr.at[2], mate)
    cp.start()
    pump()
    b_two = jnp.concatenate([bias[pl.ds(120 + i, 1), :] for i in range(8)], axis=1)
    cp.wait()

    def do_h3(img, rows):
        m = acc[c, rows, :] + got_acc[rows, :] + b_two
        mlp[rows, :] = m
        v = x1[rows, :] + ada_row(ada, 1, img) * m
        x2[rows, :] = v
        h3[c, rows, :] = modulated(img, v, 6, 7)

    blocks(do_h3)
    cp = exchange(3, h3)
    pump()
    keep(13, mlp, mlp_o)
    keep(14, x2, x2_o)
    f_copy.wait()
    pending[:] = [p for p in pending if p is not f_copy]
    cp.wait()
    keep(15, h3, h3_o)

    def do_logits(j, top):
        val = jnp.dot(h3[...].reshape(512, 1024), chunk(w, j, 3), preferred_element_type=F32)
        val = val + bias_row(128 + (2 * j + c) * 2)
        f[j] = val
        return jnp.maximum(top, jnp.max(val, axis=-1, keepdims=True))

    top = lax.fori_loop(0, 8, do_logits, jnp.full((512, 1), -jnp.inf, F32))
    inner = lax.broadcasted_iota(jnp.int32, (512, 256), 1)

    def target_hit(j):
        return inner == (tcol[:, 0:1].astype(jnp.int32) - (2 * j + c) * 256)

    def do_mass(j, carry):
        mass, picked = carry
        val = f[j]
        mass = mass + jnp.sum(jnp.exp(val - top), axis=-1, keepdims=True)
        picked = picked + jnp.sum(jnp.where(target_hit(j), val, 0.0), axis=-1, keepdims=True)
        return mass, picked

    zero = jnp.zeros((512, 1), F32)
    mass, picked = lax.fori_loop(0, 8, do_mass, (zero, zero))
    lane = lax.broadcasted_iota(jnp.int32, (512, 128), 1)
    stats[c] = jnp.where(lane == 0, top, jnp.where(lane == 1, mass, picked))
    cp = exchange(4, stats)
    cp.wait()
    both = [stats[0], stats[1]]
    top_all = jnp.maximum(both[0][:, 0:1], both[1][:, 0:1])
    mass_all = sum(b[:, 1:2] * jnp.exp(b[:, 0:1] - top_all) for b in both)
    log_total = top_all + jnp.log(mass_all)
    weight = wcol[:, 0:1]
    losses = weight * (log_total - (both[0][:, 2:3] + both[1][:, 2:3]))
    loss_out[...] = jnp.broadcast_to(0.5 * jnp.sum(losses, axis=0, keepdims=True), (8, 128))
    loss_out[7:8, :] = jnp.broadcast_to(true_count, (1, 128))
    share = weight / true_count

    def do_dlogits(j, carry):
        grad = share * (jnp.exp(f[j] - log_total) - jnp.where(target_hit(j), 1.0, 0.0))
        dl[j] = grad.astype(BF16)
        return carry

    lax.fori_loop(0, 8, do_dlogits, 0)
    keep(16, dl, dl_o)
    for img in range(2):
        for i in range(1, 8):
            o_copy(i, img).wait_send()

        @pl.when(owner != c)
        def _():
            o_copy(0, img).wait_send()

    for cp in sent:
        cp.wait_send()
    for cp in pending:
        cp.wait()


def forward_pass(msg, slots, table, cond_w, x_rows, matrices):
    dma = pltpu.SemaphoreType.DMA
    sd = jax.ShapeDtypeStruct
    kept = [
        sd((2, 4, 4, 1024, 256), BF16), sd((4, 1024, 256), BF16),
        sd((2, 256, 1024), BF16), sd((2, 256, 1024), BF16), sd((2, 256, 1024), BF16),
        sd((8, 3, 2, 128, 128), BF16), sd((256, 1024), BF16),
        sd((256, 1024), F32), sd((256, 1024), F32), sd((256, 1024), F32), sd((256, 1024), F32),
        sd((8, 512, 256), F32), sd((8, 512, 256), BF16), sd((8, 512, 256), BF16),
    ]
    vm = pltpu.VMEM
    return pl.pallas_call(
        forward_kernel,
        out_shape=[
            sd((16, 16, 128), F32), sd((16, 16, 128), F32), sd((16, 32, 64), BF16),
            sd((32, 64), F32), sd((16, 2, 512), F32), sd((8, 128), F32), sd((1024, 512), BF16),
        ] + kept,
        in_specs=[VM] * 5 + [ANY] * 3,
        out_specs=[VM] * 7 + [ANY] * len(kept),
        scratch_shapes=[
            vm((2, 4, 4, 1024, 256), BF16), vm((4, 1024, 256), BF16),
            vm((2, 256, 1024), BF16), vm((2, 256, 1024), BF16), vm((2, 256, 1024), BF16),
            vm((8, 3, 2, 128, 128), BF16), vm((8, 3, 2, 128, 128), BF16), vm((8, 2, 128, 128), BF16),
            vm((256, 1024), BF16),
            vm((256, 1024), F32), vm((256, 1024), F32), vm((256, 1024), F32), vm((256, 1024), F32),
            vm((2, 256, 1024), F32), vm((256, 1024), F32),
            vm((8, 512, 256), F32), vm((8, 512, 256), BF16), vm((8, 512, 256), BF16),
            vm((32, 64), BF16), vm((16, 2, 512), F32), vm((160, 128), F32),
            vm((2, 8, 128, 128), F32), vm((512, 128), F32), vm((512, 128), F32), vm((2, 512, 128), F32),
            dma((8, 15)), dma((8, 15)), dma((8, 3)), dma((2,)), dma((2,)),
            dma((15,)), dma((15,)), dma((15,)), dma((15,)), dma((15,)), dma((15,)), dma((15,)), dma((15,)),
            dma((5,)), dma((5,)), dma((8, 2)), dma((8, 2)), dma,
            dma((8, 2)), dma((4, 2, 2)), dma, dma((17,)),
        ],
        compiler_params=params(0, 63 * 2**20),
    )(msg, slots, table, cond_w, x_rows, *matrices)


PART_ROWS = (16, 24, 24)
PART_BASE = (0, 128, 320)
ORDERS = ("xyz", "yzx", "zxy")
SLOTS = 3
JOBS = 8


def block_cut(order, phase, rows):
    axis, later = order[phase], order[phase + 1 :]
    if axis != "z" and "z" in later:
        return ("zl", slice(0, 1), slice(1, 2))
    if "y" in later:
        return ("y", slice(0, 2), slice(2, 4))
    if "x" in later:
        return ("x", slice(0, 2), slice(2, 4))
    cut = (rows // 8 + 1) // 2 * 8
    return ("r", slice(0, cut), slice(cut, rows))


def block_dims(part, phase):
    later = ORDERS[part][phase + 1 :]
    return {
        "zl": 2 if "z" in later else 1,
        "y": 4 if "y" in later else 1,
        "x": 4 if "x" in later else 1,
        "zh": 2 if "z" in later else 1,
        "r": PART_ROWS[part],
    }


def recv_shapes():
    shapes = []
    for p in range(3):
        for ph in range(3):
            name, one, two = block_cut(ORDERS[p], ph, PART_ROWS[p])
            for k in range(4 if ph < 2 else 3):
                d = dict(block_dims(p, ph))
                if ph < 2 and k < 2:
                    cut = (one, two)[k]
                    d[name] = cut.stop - cut.start
                shapes.append((SLOTS, d["zl"], d["y"], d["x"], d["zh"], d["r"], 256))
    return shapes


def backward_kernel(*refs):
    names = [
        "msg_all", "slots_all", "cond_all", "emb", "ada", "loss", "cond_w", "x_in", "w_i", "wo_i",
        "h1_i", "h2_i", "h3_i", "hb_i", "ot_i", "att_i", "x1_i", "mlp_i", "x2_i", "f_i", "u_i", "dl_i",
        "out", "norm", "bias_sum", "gtable", "gcond", "wb", "dl", "u", "fb", "hh", "hT", "oT", "dm",
        "otp", "da", "acc", "got", "xa", "xb", "dx", "hb", "doh", "dov", "dkv", "dsrc", "dr", "dq6",
        "kcol", "dmod", "biasp", "smsg", "sgot", "smine", "sall", "spart", "sback", "gst", "gcs",
        "tile", "tiles",
    ]
    names += ["g%d" % i for i in range(3 * SLOTS)] + ["st0", "st1", "st2"]
    n = len(names)
    r = dict(zip(names, refs[:n]))
    rest = list(refs[n:])
    recv = {}
    for p in range(3):
        for ph in range(3):
            count = 4 if ph < 2 else 3
            recv[p, ph] = rest[:count]
            rest = rest[count:]
    (
        ls, fs, ps, pr, hs, hr, hl, as_, ar, js, jr, gss, grs, ol, credit,
        s1, r1, s2, r2, s3, r3, ns, nr, gl,
    ) = rest
    msg_all, slots_all, ada, biasp, dmod = r["msg_all"], r["slots_all"], r["ada"], r["biasp"], r["dmod"]
    dl, u, hT, oT, acc, got = r["dl"], r["u"], r["hT"], r["oT"], r["acc"], r["got"]
    dx, xa, xb, wb, hh = r["dx"], r["xa"], r["xb"], r["wb"], r["hh"]
    dm, otp, da, tile = r["dm"], r["otp"], r["da"], r["tile"]
    parts = [[r["g%d" % (s * 3 + p)] for p in range(3)] for s in range(SLOTS)]
    stage_out = [r["st0"], r["st1"], r["st2"]]
    out = r["out"]

    x, y, z, c = place()
    dp = lax.axis_index("dp")
    sq = lax.axis_index("seq")
    zl, zh = lax.rem(z, 2), z // 2
    base = dp - c
    owner = lax.rem(sq, 2)
    pair = sq // 2
    mate = at(x, y, z, 1 - c)
    row = [lax.rem(dp + i, 16) for i in range(1, 16)]
    line = [lax.rem(sq + i, 8) for i in range(1, 8)]
    greet([(d, sq) for d in row] + group_peers()[1:] + [at(x, y, z + 2 * zl - 1, c)])
    here = {"x": x, "y": y, "z": z}

    def step(axis, by):
        q = dict(here)
        q[axis] = q[axis] + by
        return at(q["x"], q["y"], q["z"], c)

    def load(k, src, dst):
        cp = pltpu.make_async_copy(src, dst, ls.at[k])
        cp.start()
        return cp

    loads = {
        "h3": load(0, r["h3_i"], hh),
        "dl": load(1, r["dl_i"], dl),
        "w3": load(2, r["w_i"].at[:, :, 3], wb),
        "x2": load(3, r["x2_i"], xa),
        "mlp": load(4, r["mlp_i"], xb),
        "u": load(5, r["u_i"], u),
        "hb": load(6, r["hb_i"], r["hb"]),
        "ot": load(8, r["ot_i"], otp.at[c]),
    }

    def view(ref, p, ph, index, half=None):
        order = ORDERS[p]
        sel = {}
        for i, a in enumerate(order):
            sel[a] = here[a] if i < ph else (lax.rem(index + 4, 4) if i == ph else None)
        idx = {
            "zl": slice(0, 2) if sel["z"] is None else pl.ds(lax.rem(sel["z"], 2), 1),
            "y": slice(0, 4) if sel["y"] is None else pl.ds(sel["y"], 1),
            "x": slice(0, 4) if sel["x"] is None else pl.ds(sel["x"], 1),
            "zh": slice(0, 2) if sel["z"] is None else pl.ds(sel["z"] // 2, 1),
            "r": slice(0, PART_ROWS[p]),
        }
        if half is not None:
            name, one, two = block_cut(order, ph, PART_ROWS[p])
            idx[name] = (one, two)[half]
        return ref.at[idx["zl"], idx["y"], idx["x"], idx["zh"], idx["r"]]

    def add(dst, srcs):
        d0, d1, d2, d3 = dst.shape[:4]

        def body(i, carry):
            a, b = i // d1, lax.rem(i, d1)
            for cc in range(d2):
                for d in range(d3):
                    val = dst[a, b, cc, d]
                    for s in srcs:
                        val = val + s[a, b, cc, d]
                    dst[a, b, cc, d] = val
            return carry

        if d0 * d1 == 1:
            body(0, 0)
        else:
            lax.fori_loop(0, d0 * d1, body, 0)

    neighbours = [step(a, b) for a in "xyz" for b in (1, -1)]
    unsent = []

    def phases(j, slot, again, reused):
        mine = []
        if again:
            pl.semaphore_wait(credit.at[slot], 6)

        def go(p, ph, k, src, dst, device):
            cp = remote(src, dst, js.at[j, p * 3 + ph, k], jr.at[j, p * 3 + ph, k], device)
            cp.start()
            mine.append(cp)

        def arrived(p, ph, k, ref):
            remote(ref, ref, js.at[j, p * 3 + ph, k], jr.at[j, p * 3 + ph, k], mate).wait_recv()

        for ph in range(3):
            info = []
            for p in range(3):
                a = ORDERS[p][ph]
                info.append((p, a, here[a], parts[slot][p], [b.at[slot] for b in recv[p, ph]]))
            if ph == 2:
                for p, a, i, g, bufs in info:
                    for k, by in enumerate((1, -1, 2)):
                        go(p, ph, k, view(g, p, ph, i + by), bufs[k], step(a, by))
                yield
                for p, a, i, g, bufs in info:
                    for k in range(3):
                        arrived(p, ph, k, bufs[k])
                    add(view(g, p, ph, i), bufs)
                break
            for p, a, i, g, bufs in info:
                go(p, ph, 0, view(g, p, ph, i + 2, 0), bufs[0], step(a, 1))
                go(p, ph, 1, view(g, p, ph, i + 2, 1), bufs[1], step(a, -1))
            yield
            for p, a, i, g, bufs in info:
                arrived(p, ph, 0, bufs[0])
                add(view(g, p, ph, i + 1, 0), [bufs[0]])
                go(p, ph, 2, view(g, p, ph, i + 1), bufs[2], step(a, 1))
                arrived(p, ph, 1, bufs[1])
                add(view(g, p, ph, i - 1, 1), [bufs[1]])
                go(p, ph, 3, view(g, p, ph, i - 1), bufs[3], step(a, -1))
            yield
            for p, a, i, g, bufs in info:
                arrived(p, ph, 2, bufs[2])
                arrived(p, ph, 3, bufs[3])
                add(view(g, p, ph, i), [bufs[2], bufs[3]])
        for p in range(3):
            val = parts[slot][p][zl, y, x, zh]
            stage_out[p][j] = val
            square = val * val
            total = tile[...]
            for t in range(PART_ROWS[p] // 8):
                for k in range(2):
                    total = total + square[8 * t : 8 * t + 8, 128 * k : 128 * k + 128]
            tile[...] = total
        for cp in mine:
            cp.wait_send()
        if reused():
            for device in neighbours:
                pl.semaphore_signal(credit.at[slot], inc=1, device_id=device, device_id_type=MESH)

    def tail(j):
        kind, half = JOB_KIND[j // 2], j % 2
        o = out.at[kind]

        def rows_of(p, xi, zi, count):
            n_rows = PART_ROWS[p]
            start = half * 512 + PART_BASE[p] + (lax.rem(xi + 4, 4) * 2 + zi) * n_rows
            return pl.ds(pl.multiple_of(start, 8), count * n_rows)

        def go(p, k, src, rows, device):
            cp = remote(src, o.at[rows], gss.at[j, p, k], grs.at[j, p, k], device)
            cp.start()
            unsent.append(cp)

        def arrived(p, k, rows):
            remote(o.at[rows], o.at[rows], gss.at[j, p, k], grs.at[j, p, k], mate).wait_recv()

        own = []
        for p in range(3):
            rows = rows_of(p, x, zh, 1)
            cp = pltpu.make_async_copy(stage_out[p].at[j], o.at[rows], ol.at[j, p])
            cp.start()
            own.append(cp)
            go(p, 0, stage_out[p].at[j], rows, step("z", 2))
        yield
        for p in range(3):
            own[p].wait()
            arrived(p, 0, rows_of(p, x, 1 - zh, 1))
            both = rows_of(p, x, 0, 2)
            go(p, 1, o.at[both], both, step("x", 1))
            go(p, 2, o.at[both], both, step("x", -1))
        yield
        for p in range(3):
            arrived(p, 1, rows_of(p, x - 1, 0, 2))
            arrived(p, 2, rows_of(p, x + 1, 0, 2))
            left, right = rows_of(p, x - 1, 0, 1), rows_of(p, x + 1, 1, 1)
            go(p, 3, o.at[left], left, step("x", 1))
            go(p, 4, o.at[right], right, step("x", -1))
        yield
        for p in range(3):
            arrived(p, 3, rows_of(p, x + 2, 0, 1))
            arrived(p, 4, rows_of(p, x + 2, 1, 1))

    JOB_KIND = (3, 2, 1, 0)

    def transpose_into(dst, src):
        def body(i, carry):
            cols = pl.ds(pl.multiple_of(i * 128, 128), 128)
            dst[cols, :] = jnp.transpose(src[:, :, cols].reshape(512, 128))
            return carry
        lax.fori_loop(0, 8, body, 0)

    def store_part(slot, a, b, val):
        for p in range(3):
            n_rows = PART_ROWS[p]
            for xi in range(4):
                for zi in range(2):
                    start = PART_BASE[p] + (xi * 2 + zi) * n_rows
                    parts[slot][p][a, b, xi, zi] = val[start : start + n_rows]

    prepared = set()

    def prepare(kind):
        if kind in prepared:
            return
        prepared.add(kind)
        if kind == 3:
            transpose_into(hT, hh)
        if kind == 2:
            transpose_into(hT, dm)
        if kind == 1:
            loads["h2"].wait()
            transpose_into(hT, hh)
            loads["h1"] = load(0, r["h1_i"], hh)
        if kind == 0:
            loads["h1"].wait()
            transpose_into(hT, hh)

    def fill(j, slot):
        kind, half = JOB_KIND[j // 2], j % 2
        prepare(kind)
        rows = pl.ds(half * 512, 512)
        right = {3: dl, 2: u, 1: dl}

        def body(i, carry):
            g = right[kind][i] if kind else r["dq6"][i]
            store_part(slot, i // 4, lax.rem(i, 4), jnp.dot(hT[rows, :], g, preferred_element_type=F32))
            return carry

        lax.fori_loop(0, 8 if kind else 6, body, 0)
        if kind == 0:
            for jj in range(2):
                cols = pl.ds(pl.multiple_of((2 * jj + c) * 256, 256), 256)
                g = da[:, :, cols].reshape(512, 256)
                store_part(slot, 1, 2 + jj, jnp.dot(oT[rows, :], g, preferred_element_type=F32))

    queue = list(range(JOBS))
    running = []
    tails = []
    free = list(range(SLOTS))
    ready = {3}
    used = set()

    steps_done = {}

    def launch():
        if not (queue and free and JOB_KIND[queue[0] // 2] in ready):
            return
        if running and steps_done[running[-1][1]] < 1:
            return
        j = queue.pop(0)
        slot = free.pop(0)
        fill(j, slot)
        gen = phases(j, slot, slot in used, lambda: len(queue) > len(free))
        used.add(slot)
        next(gen)
        steps_done[j] = 0
        running.append((gen, j, slot))

    def service(count=1):
        for _ in range(count):
            old = list(tails)
            for entry in list(running):
                gen, j, slot = entry
                try:
                    next(gen)
                    steps_done[j] += 1
                except StopIteration:
                    running[:] = [e for e in running if e is not entry]
                    free.append(slot)
                    t = tail(j)
                    next(t)
                    tails.append(t)
            launch()
            for gen in old:
                try:
                    next(gen)
                except StopIteration:
                    tails.remove(gen)

    tile[...] = jnp.zeros((8, 128), F32)
    biasp[...] = jnp.zeros((160, 128), F32)
    dmod[...] = jnp.zeros((2, 8, 1024), F32)
    loads["h3"].wait()
    loads["dl"].wait()
    launch()
    loads["h2"] = load(0, r["h2_i"], hh)

    def store_bias(start, val):
        for i in range(val.shape[1] // 128):
            biasp[pl.ds(start + i, 1), :] = val[:, 128 * i : 128 * i + 128]

    def blocks(fn):
        for img in range(2):
            def body(i, carry, img=img):
                fn(img, pl.ds(pl.multiple_of(img * 128 + i * 32, 32), 32))
                return carry
            lax.fori_loop(0, 4, body, 0)

    def exchange(k, ref):
        cp = remote(ref.at[c], ref.at[c], ps.at[k], pr.at[k], mate)
        cp.start()
        return cp

    def swap(k):
        cp = remote(acc.at[1 - c], got, ps.at[k], pr.at[k], mate)
        cp.start()
        return cp

    def back_rows(grad, count):
        def body(i, carry):
            for half in range(2):
                part = lax.dot_general(
                    grad[i, 256 * half : 256 * half + 256, :], wb[i // 4, lax.rem(i, 4)], NT,
                    preferred_element_type=F32,
                )

                @pl.when(i == 0)
                def _():
                    acc[half] = part

                @pl.when(i > 0)
                def _():
                    acc[half] += part

            return carry
        lax.fori_loop(0, count, body, 0)

    def norm_back(img, v, scale, shift, dy):
        center = v - jnp.mean(v, -1, keepdims=True)
        inv = lax.rsqrt(jnp.mean(center * center, -1, keepdims=True) + NORM_EPS)
        unit = center * inv
        dmod[img, scale : scale + 1, :] += jnp.sum(dy * unit, axis=0, keepdims=True)
        dmod[img, shift : shift + 1, :] += jnp.sum(dy, axis=0, keepdims=True)
        dn = dy * (1.0 + ada_row(ada, scale, img))
        return inv * (
            dn - jnp.mean(dn, -1, keepdims=True) - unit * jnp.mean(dn * unit, -1, keepdims=True)
        )

    loads["w3"].wait()
    back_rows(dl, 8)
    cp = swap(0)
    w_next = load(2, r["w_i"].at[:, :, 2], wb)

    def head_bias(i, carry):
        store_bias(128 + (2 * i + c) * 2, jnp.sum(dl[i].astype(F32), axis=0, keepdims=True))
        return carry

    lax.fori_loop(0, 8, head_bias, 0)
    service()
    loads["x2"].wait()
    loads["mlp"].wait()
    cp.wait()
    fc2_rows = jnp.zeros((1, 1024), F32)

    def do_x2(img, rows):
        grad = norm_back(img, xa[rows, :], 6, 7, acc[c, rows, :] + got[rows, :])
        dx[rows, :] = grad
        dmod[img, 1:2, :] += jnp.sum(grad * xb[rows, :], axis=0, keepdims=True)
        low = (ada_row(ada, 1, img) * grad).astype(BF16)
        dm[c, rows, :] = low
        r["gst"][0, 0:1, :] += jnp.sum(low.astype(F32), axis=0, keepdims=True)

    r["gst"][0, 0:1, :] = fc2_rows
    blocks(do_x2)
    cp = exchange(1, dm)
    store_bias(120, r["gst"][0, 0:1, :])
    loads["x1"] = load(3, r["x1_i"], xa)
    loads["att"] = load(4, r["att_i"], xb)
    cp.wait()
    loads["u"].wait()
    ready.add(2)
    service()
    w_next.wait()

    fb = r["fb"]

    def f_load(i):
        return pltpu.make_async_copy(r["f_i"].at[i], fb.at[lax.rem(i, 2)], fs.at[lax.rem(i, 2)])

    f_load(0).start()

    def do_df(i, carry):
        @pl.when(i < 7)
        def _():
            f_load(i + 1).start()

        du = jnp.dot(dm[...].reshape(512, 1024), wb[i // 4, lax.rem(i, 4)], preferred_element_type=F32)
        f_load(i).wait()
        v = fb[lax.rem(i, 2)]
        k0 = 0.7978845608028654
        th = jnp.tanh(k0 * (v + 0.044715 * (v * v * v)))
        slope = 0.5 * (1.0 + th) + 0.5 * v * (1.0 - th * th) * (k0 * (1.0 + 3.0 * 0.044715 * (v * v)))
        df = (slope * du).astype(BF16)
        dl[i] = df
        store_bias(88 + (2 * i + c) * 2, jnp.sum(df.astype(F32), axis=0, keepdims=True))
        return carry

    while 1 in queue:
        service()
    lax.fori_loop(0, 8, do_df, 0)
    ready.add(1)
    w_next = load(2, r["w_i"].at[:, :, 1], wb)
    service()
    w_next.wait()
    back_rows(dl, 8)
    cp = swap(2)
    w_next = load(2, r["wo_i"], wb.at[0])
    loads["x1"].wait()
    loads["att"].wait()
    loads["ot"].wait()
    ot_swap = exchange(3, otp)
    service()
    cp.wait()

    def do_x1(img, rows):
        grad = norm_back(img, xa[rows, :], 3, 5, acc[c, rows, :] + got[rows, :]) + dx[rows, :]
        dmod[img, 0:1, :] += jnp.sum(grad * xb[rows, :], axis=0, keepdims=True)
        low = (ada_row(ada, 0, img) * grad).astype(BF16)
        da[c, rows, :] = low
        r["gst"][0, 0:1, :] += jnp.sum(low.astype(F32), axis=0, keepdims=True)

    r["gst"][0, 0:1, :] = fc2_rows
    blocks(do_x1)
    da_swap = exchange(4, da)
    store_bias(80, r["gst"][0, 0:1, :])
    w_next.wait()
    dov, doh, hb = r["dov"], r["doh"], r["hb"]
    for img in range(2):
        rows = pl.ds(128 * img, 128)
        low = jnp.zeros((128, 1024), F32)
        for k in range(4):
            low += lax.dot_general(
                da[c, rows, 256 * k : 256 * k + 256], wb[0, k], NT, preferred_element_type=F32
            )
        dov[img] = low.astype(BF16)
    w_next = load(2, r["w_i"].at[:, :, 0], wb)

    def do_sends(fn, img):
        for p in range(4):
            for q in range(2):
                src = dov.at[img, :, pl.ds(((p // 2 * 2 + q) * 2 + p % 2) * 128, 128)]
                cp = remote(
                    src, doh.at[sq, img], hs.at[p, q, img], hr.at[sq, img], (base + q, p * 2 + c)
                )

                @pl.when(jnp.logical_not(jnp.logical_and(sq == p * 2 + c, c == q)))
                def _():
                    fn(cp)

    for img in range(2):
        do_sends(lambda cp: cp.start(), img)

    @pl.when(owner == c)
    def _():
        doh[sq] = dov[:, :, head_lanes(pair, c)]

    kcol = r["kcol"]
    for img in range(2):
        for g in range(8):
            kcol[img, g] = column_of(slots_all[g * 2 + owner, pl.ds(img, 1), :])
    service()
    ot_swap.wait()
    transpose_into(oT, otp)

    loads["hb"].wait()
    dkv, dsrc, dr, dq6 = r["dkv"], r["dsrc"], r["dr"], r["dq6"]
    low_lanes = lax.broadcasted_iota(jnp.int32, (256, 128), 1) < 64
    low_rows = lax.broadcasted_iota(jnp.int32, (128, 256), 0) < 64

    sends = []
    for img in range(2):
        for i in range(8):
            landed = doh.at[i, img]

            @pl.when(jnp.logical_or(sq != i, owner != c))
            def _():
                remote(landed, landed, hs.at[0, 0, img], hr.at[i, img], mate).wait_recv()

        dkv[...] = jnp.zeros((2, 1024, 128), F32)

        def attend_block(qb, carry, img=img):
            q = jnp.concatenate([hb[2 * qb, 0, img], hb[2 * qb + 1, 0, img]], axis=0)
            k = jnp.concatenate([hb[g, 1, img] for g in range(8)], axis=0)
            v = jnp.concatenate([hb[g, 2, img] for g in range(8)], axis=0)
            do = jnp.concatenate([doh[2 * qb, img], doh[2 * qb + 1, img]], axis=0)
            kT = jnp.transpose(k)
            key = jnp.concatenate([kcol[img, g] for g in range(8)], axis=0)[:, 0:1]
            query = jnp.concatenate(
                [slots_all[(2 * qb + i) * 2 + owner, 2 + img : 3 + img, :] for i in range(2)], axis=1
            )
            seen_by = key <= query
            heads = []
            for h in range(2):
                mask = low_lanes if h == 0 else jnp.logical_not(low_lanes)
                qh = jnp.where(mask, q, jnp.zeros_like(q))
                doh_h = jnp.where(mask, do, jnp.zeros_like(do))
                sc = lax.dot_general(k, qh, NT, preferred_element_type=F32) * SCORE_SCALE
                sc = jnp.where(seen_by, sc, -1e30)
                e = jnp.exp(sc - jnp.max(sc, axis=0, keepdims=True))
                p = e / jnp.sum(e, axis=0, keepdims=True)
                dpr = lax.dot_general(v, doh_h, NT, preferred_element_type=F32)
                inner = jnp.sum(p * dpr, axis=0, keepdims=True)
                ds = (p * (dpr - inner)).astype(BF16)
                dkv[0] += jnp.dot(ds, qh, preferred_element_type=F32)
                dkv[1] += jnp.dot(p.astype(BF16), doh_h, preferred_element_type=F32)
                heads.append(jnp.dot(kT, ds, preferred_element_type=F32))
            dq = jnp.transpose(jnp.where(low_rows, heads[0], heads[1]) * SCORE_SCALE).astype(BF16)
            dsrc[2 * qb, 0, img] = dq[:128]
            dsrc[2 * qb + 1, 0, img] = dq[128:]
            return carry

        lax.fori_loop(0, 4, attend_block, 0)
        for g in range(8):
            dsrc[g, 1, img] = (dkv[0, 128 * g : 128 * g + 128] * SCORE_SCALE).astype(BF16)
            dsrc[g, 2, img] = dkv[1, 128 * g : 128 * g + 128].astype(BF16)
        for i, to in enumerate(line):
            cp = remote(
                dsrc.at[to, :, img], dr.at[sq, :, img], as_.at[i, img], ar.at[i, img], (dp, to)
            )
            cp.start()
            sends.append(cp)
        if img == 0:
            service()
    dr[sq] = dsrc[sq]
    service(1)
    if queue[0] >= 6:
        prepare(0)
    service(1)
    for cp in sends:
        cp.wait()
    for t in range(3):
        for jj in range(2):
            for half in range(2):
                for ip in range(2):
                    dq6[t * 2 + jj, ip * 256 : ip * 256 + 256, half * 128 : half * 128 + 128] = dr[
                        (jj * 2 + half) * 2 + ip, t
                    ].reshape(256, 128)
    da_swap.wait()
    for jj in range(2):
        for start, t in ((64, 0), (72, 2)):
            store_bias(
                start + (2 * jj + c) * 2,
                jnp.sum(dq6[t * 2 + jj].astype(F32), axis=0, keepdims=True),
            )
    w_next.wait()
    back_rows(dq6, 6)
    cp = swap(5)
    ready.add(0)
    service()
    cp.wait()

    def do_x0(img, rows):
        norm_back(img, r["x_in"][rows, :].astype(F32), 2, 4, acc[c, rows, :] + got[rows, :])

    blocks(do_x0)
    for img in range(2):
        do_sends(lambda cp: cp.wait_send(), img)

    smsg, sgot, smine = r["smsg"], r["sgot"], r["smine"]
    sall, spart, sback = r["sall"], r["spart"], r["sback"]
    for k in range(8):
        both = dmod[0, k : k + 1, :] + dmod[1, k : k + 1, :]
        for i in range(8):
            biasp[8 * k + i : 8 * k + i + 1, :] = both[:, 128 * i : 128 * i + 128]
    for d in range(16):
        for img in range(2):
            for i in range(4):
                lo = (d % 2) * 512 + i * 128
                smsg[d, img * 4 + i : img * 4 + i + 1, :] = dmod[img, d // 2 : d // 2 + 1, lo : lo + 128]
        smsg[d, 8:18, :] = biasp[10 * d : 10 * d + 10, :]
        smsg[d, 18:24, :] = jnp.broadcast_to(r["loss"][0:1, :], (6, 128))
    cps = []
    for i, d in enumerate(row):
        cp = remote(smsg.at[d], sgot.at[dp], s1.at[i], r1.at[i], (d, sq))
        cp.start()
        cps.append(cp)
    sgot[dp] = smsg[dp]
    service()
    for cp in cps:
        cp.wait()
    for d in range(16):
        smine[d] = sgot[d, 0:8, :]
    for i in range(2):
        smine[16 + i] = sum(sgot[d, 8 + 8 * i : 16 + 8 * i, :] for d in range(16))
    cps = []
    for i, s in enumerate(line):
        cp = remote(smine, sall.at[sq], s2.at[i], r2.at[i], (dp, s))
        cp.start()
        cps.append(cp)
    sall[sq] = smine[...]
    service()
    for cp in cps:
        cp.wait()
    for k in range(18):
        smine[k] = sum(sall[s, k] for s in range(8))
    r["bias_sum"][0] = smine[16]
    r["bias_sum"][1] = smine[17]
    dada = jnp.concatenate(
        [
            jnp.concatenate([smine[d, 4 * i + k : 4 * i + k + 1, :] for k in range(4)], axis=1)
            for d in range(16)
            for i in range(2)
        ],
        axis=0,
    )

    def dcond_part(d, carry):
        rows = pl.ds(pl.multiple_of(64 * d, 64), 64)
        spart[d] = lax.dot_general(
            dada, r["cond_w"][rows, :].astype(F32), NT, precision=HIGH, preferred_element_type=F32
        )
        return carry

    lax.fori_loop(0, 16, dcond_part, 0)
    cps = []
    for i, d in enumerate(row):
        cp = remote(spart.at[d], sback.at[dp], s3.at[i], r3.at[i], (d, sq))
        cp.start()
        cps.append(cp)
    sback[dp] = spart[dp]
    service()
    squares = jnp.zeros((8, 128), F32)

    def fold(val):
        total = jnp.zeros((8, 128), F32)
        for i in range(val.shape[0] // 8):
            for k in range(val.shape[1] // 128):
                total = total + val[8 * i : 8 * i + 8, 128 * k : 128 * k + 128]
        return total

    gcs = r["gcs"]

    def gcond_copy(d):
        slot = lax.rem(d, 2)
        rows = pl.ds(pl.multiple_of(64 * d, 64), 64)
        return pltpu.make_async_copy(gcs.at[slot], r["gcond"].at[rows], gl.at[slot])

    def gcond_part(d, total):
        @pl.when(d > 1)
        def _():
            gcond_copy(d - 2).wait()

        val = lax.dot_general(
            r["cond_all"][d].astype(F32), dada, (((0,), (0,)), ((), ())),
            precision=HIGH, preferred_element_type=F32,
        )
        gcs[lax.rem(d, 2)] = val
        gcond_copy(d).start()
        return total + fold(val * val)

    squares = squares + lax.fori_loop(0, 16, gcond_part, squares)
    gcond_copy(14).wait()
    gcond_copy(15).wait()
    for cp in cps:
        cp.wait()
    dcond = sum(sback[d] for d in range(16))
    emb = r["emb"][...]
    sig = 1.0 / (1.0 + jnp.exp(-emb))
    demb = dcond * (sig * (1.0 + emb * (1.0 - sig)))
    labels = jnp.concatenate(
        [msg_all[d, 10:11, i : i + 1] for d in range(16) for i in range(2)], axis=0
    ).astype(jnp.int32)
    hit = jnp.where(lax.broadcasted_iota(jnp.int32, (32, 1000), 1) == labels, 1.0, 0.0)
    gtable = jnp.dot(jnp.transpose(demb), hit, precision=HIGH, preferred_element_type=F32)
    r["gtable"][...] = gtable
    table_squares = jnp.sum(jnp.sum(gtable * gtable, axis=1, keepdims=True), axis=0, keepdims=True)
    bias_rows = jnp.concatenate([smine[16], smine[17][0:2]], axis=0)
    bias_squares = jnp.sum(jnp.sum(bias_rows * bias_rows, axis=1, keepdims=True), axis=0, keepdims=True)
    spot = jnp.logical_and(
        lax.broadcasted_iota(jnp.int32, (8, 128), 0) == 0, lax.broadcasted_iota(jnp.int32, (8, 128), 1) == 0
    )
    squares = squares + jnp.where(spot, table_squares + bias_squares, 0.0)
    while queue or running:
        service()
    tile[...] += squares * 0.125
    tiles = r["tiles"]
    cps = []
    for i, d in enumerate(row):
        cp = remote(tile, tiles.at[i], ns.at[i], nr.at[i], (d, sq))
        cp.start()
        cps.append(cp)
    for cp in cps:
        cp.wait()
    tile[...] += sum(tiles[i] for i in range(15))
    cps = []
    for i, d in enumerate(line):
        cp = remote(tile, tiles.at[15 + i], ns.at[15 + i], nr.at[15 + i], (dp, d))
        cp.start()
        cps.append(cp)
    service()
    for cp in cps:
        cp.wait()
    total = tile[...] + sum(tiles[15 + i] for i in range(7))
    total = jnp.sum(jnp.sum(total, axis=1, keepdims=True), axis=0, keepdims=True)
    r["norm"][...] = jnp.broadcast_to(total, (8, 128))
    while tails:
        service()
    for cp in unsent:
        cp.wait_send()


def backward_pass(small, kept):
    dma = pltpu.SemaphoreType.DMA
    sd = jax.ShapeDtypeStruct
    vm = pltpu.VMEM
    scratch = [
        vm((2, 4, 1024, 256), BF16),
        vm((8, 512, 256), BF16), vm((8, 512, 256), BF16), vm((2, 512, 256), F32),
        vm((2, 256, 1024), BF16), vm((1024, 512), BF16), vm((1024, 512), BF16),
        vm((2, 256, 1024), BF16), vm((2, 256, 1024), BF16), vm((2, 256, 1024), BF16),
        vm((2, 256, 1024), F32), vm((256, 1024), F32), vm((256, 1024), F32), vm((256, 1024), F32),
        vm((256, 1024), F32),
        vm((8, 3, 2, 128, 128), BF16), vm((8, 2, 128, 128), BF16), vm((2, 128, 1024), BF16),
        vm((2, 1024, 128), F32), vm((8, 3, 2, 128, 128), BF16), vm((8, 3, 2, 128, 128), BF16),
        vm((6, 512, 256), BF16), vm((2, 8, 128, 128), F32), vm((2, 8, 1024), F32), vm((160, 128), F32),
        vm((16, 24, 128), F32), vm((16, 24, 128), F32), vm((18, 8, 128), F32), vm((8, 18, 8, 128), F32),
        vm((16, 32, 64), F32), vm((16, 32, 64), F32), vm((1, 8, 1024), F32),
        vm((2, 64, 512), F32),
        vm((8, 128), F32), vm((22, 8, 128), F32),
    ]
    for _ in range(SLOTS):
        for p in range(3):
            scratch.append(vm((2, 4, 4, 2, PART_ROWS[p], 256), F32))
    for p in range(3):
        scratch.append(vm((JOBS, PART_ROWS[p], 256), F32))
    scratch += [vm(shape, F32) for shape in recv_shapes()]
    scratch += [
        dma((9,)), dma((2,)), dma((6,)), dma((6,)), dma((4, 2, 2)), dma((8, 2)), dma, dma((7, 2)), dma((7, 2)),
        dma((JOBS, 9, 4)), dma((JOBS, 9, 4)), dma((JOBS, 3, 5)), dma((JOBS, 3, 5)), dma((JOBS, 3)),
        pltpu.SemaphoreType.REGULAR((SLOTS,)),
        dma((15,)), dma((15,)), dma((7,)), dma((7,)), dma((15,)), dma((15,)), dma((22,)), dma((22,)),
        dma((2,)),
    ]
    return pl.pallas_call(
        backward_kernel,
        out_shape=[
            sd((4, 1024, 256), F32), sd((8, 128), F32), sd((2, 8, 128), F32),
            sd((64, 1000), F32), sd((1024, 512), F32),
        ],
        in_specs=[VM] * len(small) + [ANY] * len(kept),
        out_specs=[ANY, VM, VM, VM, ANY],
        scratch_shapes=scratch,
        compiler_params=params(1, 64 * 2**20 - 2**17),
    )(*small, *kept)


def adamw(weight, first, second, grad, factor):
    clipped = grad * factor
    first_new = BETA_ONE * first + (1.0 - BETA_ONE) * clipped
    second_new = BETA_TWO * second + (1.0 - BETA_TWO) * clipped * clipped
    first_hat = first_new / (1.0 - BETA_ONE**STEP)
    second_hat = second_new / (1.0 - BETA_TWO**STEP)
    weight_new = weight - LEARN * (first_hat / (jnp.sqrt(second_hat) + ADAM_EPS) + DECAY * weight)
    return (weight_new, first_new, second_new)


def local(
    x_in, scale_ids, pad_mask, loss_weights, targets, labels,
    cond_w, attn_w, mlp_w, head_w, class_table, biases,
    first_cond, first_attn, first_mlp, first_head, first_table, first_bias,
    second_cond, second_attn, second_mlp, second_head, second_table, second_bias,
):

    x_rows = x_in.reshape(256, 1024)
    count_part = jnp.sum(pad_mask.astype(F32))
    row = jnp.concatenate([labels.astype(F32), count_part[None], jnp.zeros((125,), F32)])
    rounded = lax.reduce_precision(biases, 8, 7).reshape(10, 128)
    msg = jnp.concatenate([rounded, row[None], jnp.zeros((5, 128), F32)])
    level = jnp.where(pad_mask > 0, scale_ids, 1000).astype(F32)
    weight_own = (loss_weights * pad_mask).astype(F32)
    slots = jnp.concatenate(
        [level, scale_ids.astype(F32), targets.astype(F32), weight_own, jnp.zeros((8, 128), F32)]
    )
    (
        msg_all, slots_all, cond_all, embedded, ada, loss_tile, wb_cond,
        w, wo, h1, h2, h3, heads, o, att, x1, mlp, x2, f, u, dlogits,
    ) = forward_pass(msg, slots, class_table.T, cond_w, x_rows, (attn_w, mlp_w, head_w))
    true_count = loss_tile[7, 0]
    summed, squares, bias_sum, grad_table, grad_cond = backward_pass(
        (msg_all, slots_all, cond_all, embedded, ada, loss_tile, wb_cond, x_rows),
        (w, wo, h1, h2, h3, heads, o, att, x1, mlp, x2, f, u, dlogits),
    )
    bias_sum = bias_sum.reshape(16, 128)
    loss_total = bias_sum[10, 0]
    grad_bias = bias_sum[:10].reshape(1280)
    grad_norm = jnp.sqrt(squares[0, 0])
    factor = jnp.minimum(1.0, CLIP / grad_norm)
    grads = (grad_cond, summed[0], summed[1:3], summed[3], grad_table, grad_bias)
    weights = (cond_w, attn_w, mlp_w, head_w, class_table.T, biases)
    firsts = (first_cond, first_attn, first_mlp, first_head, first_table.T, first_bias)
    seconds = (second_cond, second_attn, second_mlp, second_head, second_table.T, second_bias)
    results = [
        adamw(weight, first, second, grad, factor)
        for weight, first, second, grad in zip(weights, firsts, seconds, grads)
    ]
    new_weights = [entry[0] for entry in results]
    new_first = [entry[1] for entry in results]
    new_second = [entry[2] for entry in results]
    copies = [weight.astype(BF16) for weight in new_weights]
    for group in (new_weights, new_first, new_second, copies):
        group[4] = group[4].T
    return tuple(new_weights + new_first + new_second + copies + [grad_norm, loss_total, true_count])


def solution(mesh):
    split = (P(None, "dp"), P(None, "dp"), P(None, None, "dp"), P(None, "dp"), P(None, "dp"), P("dp"))
    in_specs = (P("dp", "seq", None),) + (P("dp", "seq"),) * 4 + (P("dp"),) + split * 3
    out_specs = split * 4 + (P(), P(), P())
    return jax.shard_map(local, mesh=mesh, in_specs=in_specs, out_specs=out_specs, check_vma=False)
```

```python
import functools

import jax
import jax.numpy as jnp
from jax import lax
from jax.experimental import pallas as pl
from jax.experimental.pallas import tpu as pltpu
from jax.sharding import PartitionSpec as P

STEP = 5
HIGH = lax.Precision.HIGHEST
NORM_EPS = 1e-06
CLIP = 0.01
LEARN = 0.02
DECAY = 0.1
BETA_ONE = 0.5
BETA_TWO = 0.5
ADAM_EPS = 1e-08
SCORE_SCALE = 0.125
MESH = pl.DeviceIdType.MESH
F32 = jnp.float32
BF16 = jnp.bfloat16
ANY = pl.BlockSpec(memory_space=pl.ANY)
VM = pl.BlockSpec(memory_space=pltpu.VMEM)

ROWS_YZ = 320
HALF_YZ = 160
QUARTER = 48


def place():
    dp = lax.axis_index("dp")
    sq = lax.axis_index("seq")
    core = lax.rem(dp, 2)
    y = lax.rem(dp // 2, 4)
    z = lax.rem(sq, 2) * 2 + dp // 8
    return sq // 2, y, z, core


def at(x, y, z, core):
    x, y, z = lax.rem(x + 4, 4), lax.rem(y + 4, 4), lax.rem(z + 4, 4)
    return (lax.rem(z, 2) * 8 + y * 2 + core, x * 2 + z // 2)


def greet(devices):
    bar = pltpu.get_barrier_semaphore()
    for device in devices:
        pl.semaphore_signal(bar, inc=1, device_id=device, device_id_type=MESH)
    pl.semaphore_wait(bar, len(devices))


def remote(src, dst, send, recv, device):
    return pltpu.make_async_remote_copy(
        src_ref=src, dst_ref=dst, send_sem=send, recv_sem=recv, device_id=device, device_id_type=MESH
    )


def params(collective_id, vmem=None):
    return pltpu.CompilerParams(
        collective_id=collective_id, has_side_effects=True, vmem_limit_bytes=vmem
    )


def group_peers():
    dp = lax.axis_index("dp")
    sq = lax.axis_index("seq")
    core = lax.rem(dp, 2)
    out = [(dp + 1 - 2 * core, sq)]
    for i in range(1, 8):
        for flip in range(2):
            out.append((dp + flip * (1 - 2 * core), lax.rem(sq + i, 8)))
    return out


def head_lanes(pair, core):
    return pl.ds(pl.multiple_of(((pair // 2 * 2 + core) * 2 + lax.rem(pair, 2)) * 128, 128), 128)


NT = (((1,), (1,)), ((), ()))


def normalize(v):
    center = v - jnp.mean(v, -1, keepdims=True)
    spread = jnp.mean(center * center, -1, keepdims=True)
    return center * lax.rsqrt(spread + NORM_EPS)


def ada_row(ada, k, img):
    return jnp.concatenate([ada[2 * k, img : img + 1, :], ada[2 * k + 1, img : img + 1, :]], axis=1)


def column_of(row):
    return jnp.transpose(jnp.broadcast_to(row, (128, 128)))


def forward_kernel(
    labels_in, bias_in, scale_in, pad_in, weight_in, target_in, table, cond_w, x_in, attn_in, mlp_in, head_in,
    msg_all, slots_all, cond_all, emb_out, ada, loss_out, cond_low,
    w_o, wo_o, h1_o, h2_o, h3_o, hb_o, ot_o, att_o, x1_o, mlp_o, x2_o, f_o, u_o, dl_o,
    msg, slots, w, wo, h1, h2, h3, src, hb, oh, ot, att, x1, mlp, x2, acc, got_acc, f, u, dl,
    cond_own, ada_own, bias, qcol, tcol, wcol, stats,
    gs, gr, gl, os, orr, s1, r1, s2, r2, s3, r3, s4, r4, ps, pr, as_, ar, al, ts, tr, tl, outs_sem,
):
    x, y, z, c = place()
    dp = lax.axis_index("dp")
    sq = lax.axis_index("seq")
    zl = lax.rem(z, 2)
    up, down, far = lax.rem(y + 1, 4), lax.rem(y + 3, 4), lax.rem(y + 2, 4)
    yp, ym = at(x, y + 1, z, c), at(x, y - 1, z, c)
    zp, zm = at(x, y, z + 1, c), at(x, y, z - 1, c)
    xp, xm = at(x + 1, y, z, c), at(x - 1, y, z, c)
    zs = at(x, y, z + 1 - 2 * c, c)
    mate = at(x, y, z, 1 - c)
    base = dp - c
    row = [(lax.rem(dp + i, 16), sq) for i in range(1, 16)]
    group = group_peers()
    incoming = []
    for j in range(8):
        rows = pl.ds(512 * (j % 2), 512)
        source = (attn_in, mlp_in.at[0], mlp_in.at[1], head_in)[j // 2]
        incoming.append(pltpu.make_async_copy(source.at[rows], f.at[j], gl.at[j, 0]))
        incoming[-1].start()
    pad = pad_in[...]
    scale = scale_in[...].astype(F32)
    slots[...] = jnp.zeros((16, 128), F32)
    slots[0:2, :] = jnp.where(pad > 0, scale, 1000.0)
    slots[2:4, :] = scale
    slots[4:6, :] = target_in[...].astype(F32)
    slots[6:8, :] = (weight_in[...] * pad).astype(F32)
    real = jnp.sum(jnp.sum(pad.astype(F32), axis=1, keepdims=True), axis=0, keepdims=True)
    spot = lax.broadcasted_iota(jnp.int32, (1, 128), 1)
    label = labels_in[...].astype(F32)
    msg[...] = jnp.zeros((16, 128), F32)
    msg[0:10, :] = bias_in[...].astype(BF16).astype(F32)
    msg[10:11, :] = jnp.where(
        spot == 0, label[:, 0:1], jnp.where(spot == 1, label[:, 1:2], jnp.where(spot == 2, real, 0.0))
    )
    greet(row + group[1:] + [at(x, y, z + 2 * zl - 1, c)])

    pending = []

    def keep(k, src_ref, dst_ref):
        cp = pltpu.make_async_copy(src_ref, dst_ref, outs_sem.at[k])
        cp.start()
        pending.append(cp)
        return cp

    def rows_at(j, start, count):
        return pl.ds(512 * (j % 2) + start, count)

    def quarter(j, pos):
        start = 512 * (j % 2) + ROWS_YZ + QUARTER * lax.rem(pos + 4, 4)
        return pl.ds(pl.multiple_of(start, 16), QUARTER)

    sent = []

    def go(j, k, a, b, device):
        cp = remote(a, b, gs.at[j, k], gr.at[j, k], device)
        cp.start()
        sent.append(cp)

    def got(j, k, ref):
        remote(ref, ref, gs.at[j, k], gr.at[j, k], mate).wait_recv()

    def stage(kind, j):
        m = j // 2
        full, first = rows_at(j, 0, ROWS_YZ), rows_at(j, 0, HALF_YZ)
        second, mine = rows_at(j, HALF_YZ, HALF_YZ), quarter(j, x)
        if kind == "A":
            incoming[j].wait()
            w[zl, y, m, full, :] = f[j, 0:ROWS_YZ, :].astype(BF16)
            at_rows = pl.ds(pl.multiple_of(ROWS_YZ + QUARTER * x, 16), QUARTER)
            w[zl, y, m, mine, :] = f[j, at_rows, :].astype(BF16)
            go(j, 0, w.at[zl, y, m, full], w.at[zl, y, m, full], yp)
            go(j, 1, w.at[zl, y, m, full], w.at[zl, y, m, full], ym)
            go(j, 6, w.at[zl, y, m, mine], w.at[zl, y, m, mine], zs)
        if kind == "B":
            got(j, 6, w.at[1 - zl, y, m, mine])
            go(j, 7, w.at[:, y, m, mine], w.at[:, y, m, mine], yp)
            go(j, 8, w.at[:, y, m, mine], w.at[:, y, m, mine], ym)
            got(j, 0, w.at[zl, down, m, full])
            got(j, 1, w.at[zl, up, m, full])
            go(j, 2, w.at[zl, down, m, first], w.at[zl, down, m, first], yp)
            go(j, 3, w.at[zl, up, m, second], w.at[zl, up, m, second], ym)
        if kind == "C":
            got(j, 7, w.at[:, down, m, mine])
            got(j, 8, w.at[:, up, m, mine])
            go(j, 9, w.at[0, down, m, mine], w.at[0, down, m, mine], yp)
            go(j, 10, w.at[1, up, m, mine], w.at[1, up, m, mine], ym)
            got(j, 2, w.at[zl, far, m, first])
            got(j, 3, w.at[zl, far, m, second])
            go(j, 4, w.at[zl, :, m, first], w.at[zl, :, m, first], zp)
            go(j, 5, w.at[zl, :, m, second], w.at[zl, :, m, second], zm)
        if kind == "D":
            got(j, 9, w.at[0, far, m, mine])
            got(j, 10, w.at[1, far, m, mine])
            go(j, 11, w.at[:, :, m, mine], w.at[:, :, m, mine], xp)
            go(j, 12, w.at[:, :, m, mine], w.at[:, :, m, mine], xm)
        if kind == "E":
            left, right = quarter(j, x - 1), quarter(j, x + 1)
            got(j, 11, w.at[:, :, m, left])
            got(j, 12, w.at[:, :, m, right])
            go(j, 13, w.at[0, :, m, left], w.at[0, :, m, left], xp)
            go(j, 14, w.at[1, :, m, right], w.at[1, :, m, right], xm)
        if kind == "F":
            across = quarter(j, x + 2)
            got(j, 4, w.at[1 - zl, :, m, first])
            got(j, 5, w.at[1 - zl, :, m, second])
            got(j, 13, w.at[0, :, m, across])
            got(j, 14, w.at[1, :, m, across])
            if j % 2:
                keep(m, w.at[:, :, m], w_o.at[:, :, m])
            if j == 1:
                for i in range(2):
                    remote(w.at[1, 2 + i, 0], wo.at[2 * i + c], os.at[i], orr.at[i], mate).start()
                    pltpu.make_async_copy(w.at[1, 2 + i, 0], wo.at[2 * i + c], gl.at[i, 2]).start()

    wave = [
        ["A0", "A1"], ["B0", "B1", "A2"], ["C0", "C1", "B2", "D0", "D1", "A3"],
        ["E0", "E1", "C2", "B3", "A4"], ["F0", "F1"], ["D2", "C3", "B4", "A5"],
        ["E2", "D3", "C4", "B5", "A6"], ["F2", "E3", "D4", "C5", "B6", "A7"],
        ["F3", "E4", "D5", "C6", "B7"], ["F4", "E5", "D6", "C7"],
        ["F5", "E6", "D7"], ["F6", "E7"], ["F7"],
    ]

    def pump(n=1):
        for _ in range(n):
            if wave:
                for item in wave.pop(0):
                    stage(item[0], int(item[1]))

    firsts = []
    for i, to in enumerate(row):
        cp = remote(msg, msg_all.at[dp], s1.at[i], r1.at[i], to)
        cp.start()
        firsts.append(cp)
    msg_all[dp] = msg[...]
    pump()
    for cp in firsts:
        cp.wait()
    seen = msg_all[...]
    count = jnp.sum(seen[:, 10, 2:3], axis=0, keepdims=True)
    slots[8:9, :] = jnp.broadcast_to(count, (1, 128))
    for d in range(16):
        bias[pl.ds(10 * d, 10), :] = seen[d, 0:10, :]
    seconds = []
    for i, to in enumerate(group):
        cp = remote(slots, slots_all.at[sq * 2 + c], s2.at[i], r2.at[i], to)
        cp.start()
        seconds.append(cp)
    slots_all[sq * 2 + c] = slots[...]
    classes = table.shape[1]
    lane = lax.broadcasted_iota(jnp.int32, (32, classes), 1)
    labels = jnp.concatenate([seen[d, 10:11, i : i + 1] for d in range(16) for i in range(2)], axis=0)
    hit = jnp.where(lane == labels.astype(jnp.int32), 1.0, 0.0).astype(BF16)
    emb = lax.dot_general(hit, table[...].astype(BF16), NT, preferred_element_type=F32)
    emb_out[...] = emb
    cond_own[...] = (emb / (1.0 + jnp.exp(-emb))).astype(BF16)
    cond_all[dp] = cond_own[...]
    thirds = []
    for i, to in enumerate(row):
        cp = remote(cond_own, cond_all.at[dp], s3.at[i], r3.at[i], to)
        cp.start()
        thirds.append(cp)
    pump()
    for cp in thirds:
        cp.wait()
    total = jnp.zeros((32, 512), F32)
    for d in range(16):
        low = cond_w[pl.ds(64 * d, 64), :].astype(BF16)
        cond_low[pl.ds(64 * d, 64), :] = low
        total += jnp.dot(cond_all[d], low, preferred_element_type=F32)
    total += jnp.concatenate([bias[pl.ds(dp * 4 + i, 1), :] for i in range(4)], axis=1)
    for d in range(16):
        ada_own[d] = total[2 * d : 2 * d + 2]
    fourths = []
    for i in range(15):
        to = lax.rem(dp + 1 + i, 16)
        cp = remote(ada_own.at[to], ada.at[dp], s4.at[i], r4.at[i], (to, sq))
        cp.start()
        fourths.append(cp)
    ada[dp] = ada_own[dp]
    pump()
    for cp in fourths:
        cp.wait()
    for cp in seconds:
        cp.wait()

    owner = lax.rem(sq, 2)
    for img in range(2):
        for g in range(8):
            qcol[img, g] = column_of(slots_all[g * 2 + owner, pl.ds(2 + img, 1), :])
        for q in range(2):
            at_rows = pl.ds((q * 2 + img) * 128, 128)
            tcol[at_rows, :] = column_of(slots_all[sq * 2 + q, pl.ds(4 + img, 1), :])
            wcol[at_rows, :] = column_of(slots_all[sq * 2 + q, pl.ds(6 + img, 1), :])
    true_count = jnp.sum(
        jnp.concatenate([slots_all[2 * g, 8:9, 0:1] for g in range(8)], axis=0), axis=0, keepdims=True
    )

    def blocks(fn):
        for img in range(2):
            def body(i, carry, img=img):
                fn(img, pl.ds(pl.multiple_of(img * 128 + i * 32, 32), 32))
                return carry
            lax.fori_loop(0, 4, body, 0)

    def exchange(k, ref):
        cp = remote(ref.at[c], ref.at[c], ps.at[k], pr.at[k], mate)
        cp.start()
        return cp

    def modulated(img, v, scale, shift):
        return (normalize(v) * (1.0 + ada_row(ada, scale, img)) + ada_row(ada, shift, img)).astype(BF16)

    def do_h1(img, rows):
        h1[c, rows, :] = modulated(img, x_in[rows, :].astype(F32), 2, 4)

    blocks(do_h1)
    cp = exchange(0, h1)
    pump()
    cp.wait()
    keep(4, h1, h1_o)
    pump()

    def bias_row(start):
        return jnp.concatenate([bias[pl.ds(start, 1), :], bias[pl.ds(start + 1, 1), :]], axis=1)

    tokens = h1[...].reshape(512, 1024)
    for j in range(6):
        t, jj = j // 2, j % 2
        val = jnp.dot(tokens, w[j // 4, j % 4, 0], preferred_element_type=F32)
        if t != 1:
            val = val + bias_row(64 + (0 if t == 0 else 8) + (2 * jj + c) * 2)
        val = val.astype(BF16)
        for half in range(2):
            for ip in range(2):
                src[(jj * 2 + half) * 2 + ip, t] = val[
                    ip * 256 : ip * 256 + 256, half * 128 : half * 128 + 128
                ].reshape(2, 128, 128)
    cps = [[], []]
    for img in range(2):
        for i in range(1, 8):
            to = lax.rem(sq + i, 8)
            cp = remote(
                src.at[to, :, img], hb.at[sq, :, img], as_.at[i, img], ar.at[i, img], (dp, to)
            )
            cp.start()
            cps[img].append(cp)
    hb[sq] = src[sq]
    pump()

    low_lanes = lax.broadcasted_iota(jnp.int32, (256, 128), 1) < 64

    def attend_block(i, carry):
        img, qb = i // 4, lax.rem(i, 4)
        q = jnp.concatenate([hb[2 * qb, 0, img], hb[2 * qb + 1, 0, img]], axis=0)
        k = jnp.concatenate([hb[g, 1, img] for g in range(8)], axis=0)
        v = jnp.concatenate([hb[g, 2, img] for g in range(8)], axis=0)
        key = jnp.concatenate([slots_all[g * 2 + owner, pl.ds(img, 1), :] for g in range(8)], axis=1)
        query = jnp.concatenate([qcol[img, 2 * qb], qcol[img, 2 * qb + 1]], axis=0)[:, 0:1]
        seen_by = key <= query
        heads = []
        for h in range(2):
            mask = low_lanes if h == 0 else jnp.logical_not(low_lanes)
            qh = jnp.where(mask, q, jnp.zeros_like(q))
            sc = lax.dot_general(qh, k, NT, preferred_element_type=F32) * SCORE_SCALE
            sc = jnp.where(seen_by, sc, -1e30)
            e = jnp.exp(sc - jnp.max(sc, axis=-1, keepdims=True))
            p = (e / jnp.sum(e, axis=-1, keepdims=True)).astype(BF16)
            heads.append(jnp.dot(p, v, preferred_element_type=F32))
        o = jnp.where(low_lanes, heads[0], heads[1]).astype(BF16)
        oh[2 * qb, img] = o[:128]
        oh[2 * qb + 1, img] = o[128:]
        return carry

    pair = sq // 2
    lanes = head_lanes(pair, c)

    def o_copy(i, img):
        to = lax.rem(sq + i, 8)
        return remote(
            oh.at[to, img], ot.at[pl.ds(img * 128, 128), lanes], ts.at[i, img], tr.at[pair, c, img],
            (base + owner, to),
        )

    for img in range(2):
        for cp in cps[img]:
            cp.wait()
        lax.fori_loop(4 * img, 4 * img + 2, attend_block, 0)
        pump()
        lax.fori_loop(4 * img + 2, 4 * img + 4, attend_block, 0)
        for i in range(1, 8):
            o_copy(i, img).start()

        @pl.when(owner == c)
        def _():
            ot[pl.ds(img * 128, 128), lanes] = oh[sq, img]

        @pl.when(owner != c)
        def _():
            o_copy(0, img).start()

        pump()
    keep(5, hb, hb_o)
    for img in range(2):
        for p in range(4):
            for q in range(2):
                view = ot.at[pl.ds(img * 128, 128), pl.ds(((p // 2 * 2 + q) * 2 + p % 2) * 128, 128)]

                @pl.when(jnp.logical_or(sq != p * 2 + c, c != q))
                def _():
                    remote(view, view, ts.at[0, img], tr.at[p, q, img], mate).wait_recv()

    keep(6, ot, ot_o)
    for i in range(2):
        remote(w.at[1, 2 + i, 0], wo.at[2 * i + c], os.at[i], orr.at[i], mate).wait()
        pltpu.make_async_copy(w.at[1, 2 + i, 0], wo.at[2 * i + c], gl.at[i, 2]).wait()
    keep(7, wo, wo_o)
    for k in range(4):
        cols = pl.ds(256 * k, 256)
        att[:, cols] = jnp.dot(ot[...], wo[k], preferred_element_type=F32) + bias_row(80 + 2 * k)
    keep(8, att, att_o)

    def do_h2(img, rows):
        v = x_in[rows, :].astype(F32) + ada_row(ada, 0, img) * att[rows, :]
        x1[rows, :] = v
        h2[c, rows, :] = modulated(img, v, 3, 5)

    blocks(do_h2)
    cp = exchange(1, h2)
    keep(9, x1, x1_o)
    cp.wait()
    keep(10, h2, h2_o)
    pump()

    def chunk(ref, j, kind):
        return ref[j // 4, lax.rem(j, 4), kind]

    def do_f(j, carry):
        val = jnp.dot(h2[...].reshape(512, 1024), chunk(w, j, 1), preferred_element_type=F32)
        val = val + bias_row(88 + (2 * j + c) * 2)
        f[j] = val
        act = jax.nn.gelu(val, approximate=True).astype(BF16)
        u[j] = act
        part = lax.dot_general(act, chunk(w, j, 2), NT, preferred_element_type=F32).reshape(2, 256, 1024)

        @pl.when(j == 0)
        def _():
            acc[...] = part

        @pl.when(j > 0)
        def _():
            acc[...] += part

        return carry

    lax.fori_loop(0, 8, do_f, 0)
    f_copy = keep(11, f, f_o)
    keep(12, u, u_o)
    cp = remote(acc.at[1 - c], got_acc, ps.at[2], pr.at[2], mate)
    cp.start()
    pump()
    b_two = jnp.concatenate([bias[pl.ds(120 + i, 1), :] for i in range(8)], axis=1)
    cp.wait()

    def do_h3(img, rows):
        m = acc[c, rows, :] + got_acc[rows, :] + b_two
        mlp[rows, :] = m
        v = x1[rows, :] + ada_row(ada, 1, img) * m
        x2[rows, :] = v
        h3[c, rows, :] = modulated(img, v, 6, 7)

    blocks(do_h3)
    cp = exchange(3, h3)
    pump()
    keep(13, mlp, mlp_o)
    keep(14, x2, x2_o)
    f_copy.wait()
    pending[:] = [p for p in pending if p is not f_copy]
    cp.wait()
    keep(15, h3, h3_o)

    def do_logits(j, top):
        val = jnp.dot(h3[...].reshape(512, 1024), chunk(w, j, 3), preferred_element_type=F32)
        val = val + bias_row(128 + (2 * j + c) * 2)
        f[j] = val
        return jnp.maximum(top, jnp.max(val, axis=-1, keepdims=True))

    top = lax.fori_loop(0, 8, do_logits, jnp.full((512, 1), -jnp.inf, F32))
    inner = lax.broadcasted_iota(jnp.int32, (512, 256), 1)

    def target_hit(j):
        return inner == (tcol[:, 0:1].astype(jnp.int32) - (2 * j + c) * 256)

    def do_mass(j, carry):
        mass, picked = carry
        val = f[j]
        mass = mass + jnp.sum(jnp.exp(val - top), axis=-1, keepdims=True)
        picked = picked + jnp.sum(jnp.where(target_hit(j), val, 0.0), axis=-1, keepdims=True)
        return mass, picked

    zero = jnp.zeros((512, 1), F32)
    mass, picked = lax.fori_loop(0, 8, do_mass, (zero, zero))
    lane = lax.broadcasted_iota(jnp.int32, (512, 128), 1)
    stats[c] = jnp.where(lane == 0, top, jnp.where(lane == 1, mass, picked))
    cp = exchange(4, stats)
    cp.wait()
    both = [stats[0], stats[1]]
    top_all = jnp.maximum(both[0][:, 0:1], both[1][:, 0:1])
    mass_all = sum(b[:, 1:2] * jnp.exp(b[:, 0:1] - top_all) for b in both)
    log_total = top_all + jnp.log(mass_all)
    weight = wcol[:, 0:1]
    losses = weight * (log_total - (both[0][:, 2:3] + both[1][:, 2:3]))
    loss_out[...] = jnp.broadcast_to(0.5 * jnp.sum(losses, axis=0, keepdims=True), (8, 128))
    loss_out[7:8, :] = jnp.broadcast_to(true_count, (1, 128))
    share = weight / true_count

    def do_dlogits(j, carry):
        grad = share * (jnp.exp(f[j] - log_total) - jnp.where(target_hit(j), 1.0, 0.0))
        dl[j] = grad.astype(BF16)
        return carry

    lax.fori_loop(0, 8, do_dlogits, 0)
    keep(16, dl, dl_o)
    for img in range(2):
        for i in range(1, 8):
            o_copy(i, img).wait_send()

        @pl.when(owner != c)
        def _():
            o_copy(0, img).wait_send()

    for cp in sent:
        cp.wait_send()
    for cp in pending:
        cp.wait()


def forward_pass(small, matrices):
    dma = pltpu.SemaphoreType.DMA
    sd = jax.ShapeDtypeStruct
    kept = [
        sd((2, 4, 4, 1024, 256), BF16), sd((4, 1024, 256), BF16),
        sd((2, 256, 1024), BF16), sd((2, 256, 1024), BF16), sd((2, 256, 1024), BF16),
        sd((8, 3, 2, 128, 128), BF16), sd((256, 1024), BF16),
        sd((256, 1024), F32), sd((256, 1024), F32), sd((256, 1024), F32), sd((256, 1024), F32),
        sd((8, 512, 256), F32), sd((8, 512, 256), BF16), sd((8, 512, 256), BF16),
    ]
    vm = pltpu.VMEM
    return pl.pallas_call(
        forward_kernel,
        out_shape=[
            sd((16, 16, 128), F32), sd((16, 16, 128), F32), sd((16, 32, 64), BF16),
            sd((32, 64), F32), sd((16, 2, 512), F32), sd((8, 128), F32), sd((1024, 512), BF16),
        ] + kept,
        in_specs=[VM] * len(small) + [ANY] * 3,
        out_specs=[VM] * 7 + [ANY] * len(kept),
        scratch_shapes=[
            vm((16, 128), F32), vm((16, 128), F32),
            vm((2, 4, 4, 1024, 256), BF16), vm((4, 1024, 256), BF16),
            vm((2, 256, 1024), BF16), vm((2, 256, 1024), BF16), vm((2, 256, 1024), BF16),
            vm((8, 3, 2, 128, 128), BF16), vm((8, 3, 2, 128, 128), BF16), vm((8, 2, 128, 128), BF16),
            vm((256, 1024), BF16),
            vm((256, 1024), F32), vm((256, 1024), F32), vm((256, 1024), F32), vm((256, 1024), F32),
            vm((2, 256, 1024), F32), vm((256, 1024), F32),
            vm((8, 512, 256), F32), vm((8, 512, 256), BF16), vm((8, 512, 256), BF16),
            vm((32, 64), BF16), vm((16, 2, 512), F32), vm((160, 128), F32),
            vm((2, 8, 128, 128), F32), vm((512, 128), F32), vm((512, 128), F32), vm((2, 512, 128), F32),
            dma((8, 15)), dma((8, 15)), dma((8, 3)), dma((2,)), dma((2,)),
            dma((15,)), dma((15,)), dma((15,)), dma((15,)), dma((15,)), dma((15,)), dma((15,)), dma((15,)),
            dma((5,)), dma((5,)), dma((8, 2)), dma((8, 2)), dma,
            dma((8, 2)), dma((4, 2, 2)), dma, dma((17,)),
        ],
        compiler_params=params(0, 63 * 2**20),
    )(*small, *matrices)


PART_ROWS = (16, 24, 24)
PART_BASE = (0, 128, 320)
ORDERS = (("xyz", "yzx", "zxy"), ("xyz", "yxz", "zyx"))
SLOTS = 3
JOBS = 8


def block_cut(order, phase, rows):
    axis, later = order[phase], order[phase + 1 :]
    if axis != "z" and "z" in later:
        return ("zl", slice(0, 1), slice(1, 2))
    if "y" in later:
        return ("y", slice(0, 2), slice(2, 4))
    if "x" in later:
        return ("x", slice(0, 2), slice(2, 4))
    cut = (rows // 8 + 1) // 2 * 8
    return ("r", slice(0, cut), slice(cut, rows))


def block_dims(order, part, phase):
    later = order[phase + 1 :]
    return {
        "zl": 2 if "z" in later else 1,
        "y": 4 if "y" in later else 1,
        "x": 4 if "x" in later else 1,
        "zh": 2 if "z" in later else 1,
        "r": PART_ROWS[part],
    }


def recv_plan():
    for kind in range(2):
        for p in range(3):
            for ph in range(3):
                if kind == 0 or (p > 0 and ph == 1):
                    yield kind, p, ph, 4 if ph < 2 else 3


def recv_shapes():
    shapes = []
    for kind, p, ph, count in recv_plan():
        order = ORDERS[kind][p]
        name, one, two = block_cut(order, ph, PART_ROWS[p])
        for k in range(count):
            d = dict(block_dims(order, p, ph))
            if ph < 2 and k < 2:
                cut = (one, two)[k]
                d[name] = cut.stop - cut.start
            shapes.append((SLOTS, d["zl"], d["y"], d["x"], d["zh"], d["r"], 256))
    return shapes


def backward_kernel(*refs):
    names = [
        "msg_all", "slots_all", "cond_all", "emb", "ada", "loss", "cond_w", "x_in", "w_i", "wo_i",
        "h1_i", "h2_i", "h3_i", "hb_i", "ot_i", "att_i", "x1_i", "mlp_i", "x2_i", "f_i", "u_i", "dl_i",
        "out", "norm", "bias_sum", "gtable", "gcond", "wb", "dl", "u", "fb", "hh", "hT", "oT", "dm",
        "otp", "da", "acc", "got", "xa", "xb", "dx", "hb", "doh", "dov", "dkv", "dsrc", "dr", "dq6",
        "kcol", "dmod", "biasp", "smsg", "sgot", "smine", "sall", "spart", "sback", "gst", "gcs",
        "tile", "tiles",
    ]
    names += ["g%d" % i for i in range(3 * SLOTS)] + ["st0", "st1", "st2"]
    n = len(names)
    r = dict(zip(names, refs[:n]))
    rest = list(refs[n:])
    recv = {}
    for kind, p, ph, count in recv_plan():
        recv[kind, p, ph] = rest[:count]
        rest = rest[count:]
    (
        ls, fs, ps, pr, hs, hr, hl, as_, ar, js, jr, gss, grs, ol, credit,
        s1, r1, s2, r2, s3, r3, ns, nr, gl,
    ) = rest
    msg_all, slots_all, ada, biasp, dmod = r["msg_all"], r["slots_all"], r["ada"], r["biasp"], r["dmod"]
    dl, u, hT, oT, acc, got = r["dl"], r["u"], r["hT"], r["oT"], r["acc"], r["got"]
    dx, xa, xb, wb, hh = r["dx"], r["xa"], r["xb"], r["wb"], r["hh"]
    dm, otp, da, tile = r["dm"], r["otp"], r["da"], r["tile"]
    parts = [[r["g%d" % (s * 3 + p)] for p in range(3)] for s in range(SLOTS)]
    stage_out = [r["st0"], r["st1"], r["st2"]]
    out = r["out"]

    x, y, z, c = place()
    dp = lax.axis_index("dp")
    sq = lax.axis_index("seq")
    zl, zh = lax.rem(z, 2), z // 2
    base = dp - c
    owner = lax.rem(sq, 2)
    pair = sq // 2
    mate = at(x, y, z, 1 - c)
    row = [lax.rem(dp + i, 16) for i in range(1, 16)]
    line = [lax.rem(sq + i, 8) for i in range(1, 8)]
    greet([(d, sq) for d in row] + group_peers()[1:] + [at(x, y, z + 2 * zl - 1, c)])
    here = {"x": x, "y": y, "z": z}

    def step(axis, by):
        q = dict(here)
        q[axis] = q[axis] + by
        return at(q["x"], q["y"], q["z"], c)

    def load(k, src, dst):
        cp = pltpu.make_async_copy(src, dst, ls.at[k])
        cp.start()
        return cp

    loads = {
        "h3": load(0, r["h3_i"], hh),
        "dl": load(1, r["dl_i"], dl),
        "w3": load(2, r["w_i"].at[:, :, 3], wb),
        "x2": load(3, r["x2_i"], xa),
        "mlp": load(4, r["mlp_i"], xb),
        "u": load(5, r["u_i"], u),
        "hb": load(6, r["hb_i"], r["hb"]),
        "ot": load(8, r["ot_i"], otp.at[c]),
    }

    def view(ref, order, p, ph, index, half=None):
        sel = {}
        for i, a in enumerate(order):
            sel[a] = here[a] if i < ph else (lax.rem(index + 4, 4) if i == ph else None)
        idx = {
            "zl": slice(0, 2) if sel["z"] is None else pl.ds(lax.rem(sel["z"], 2), 1),
            "y": slice(0, 4) if sel["y"] is None else pl.ds(sel["y"], 1),
            "x": slice(0, 4) if sel["x"] is None else pl.ds(sel["x"], 1),
            "zh": slice(0, 2) if sel["z"] is None else pl.ds(sel["z"] // 2, 1),
            "r": slice(0, PART_ROWS[p]),
        }
        if half is not None:
            name, one, two = block_cut(order, ph, PART_ROWS[p])
            idx[name] = (one, two)[half]
        return ref.at[idx["zl"], idx["y"], idx["x"], idx["zh"], idx["r"]]

    def add(dst, srcs):
        d0, d1, d2, d3 = dst.shape[:4]

        def body(i, carry):
            a, b = i // d1, lax.rem(i, d1)
            for cc in range(d2):
                for d in range(d3):
                    val = dst[a, b, cc, d]
                    for s in srcs:
                        val = val + s[a, b, cc, d]
                    dst[a, b, cc, d] = val
            return carry

        if d0 * d1 == 1:
            body(0, 0)
        else:
            lax.fori_loop(0, d0 * d1, body, 0)

    neighbours = [step(a, b) for a in "xyz" for b in (1, -1)]
    unsent = []

    def phases(j, slot, again, reused):
        mine = []
        kind = j % 2
        if again:
            pl.semaphore_wait(credit.at[slot], 6)

        def go(p, ph, k, src, dst, device):
            cp = remote(src, dst, js.at[j, p * 3 + ph, k], jr.at[j, p * 3 + ph, k], device)
            cp.start()
            mine.append(cp)

        def arrived(p, ph, k, ref):
            remote(ref, ref, js.at[j, p * 3 + ph, k], jr.at[j, p * 3 + ph, k], mate).wait_recv()

        for ph in range(3):
            info = []
            for p in range(3):
                order = ORDERS[kind][p]
                a = order[ph]
                buffers = recv.get((kind, p, ph), recv[0, p, ph])
                bufs = [b.at[slot] for b in buffers]
                info.append((p, a, here[a], functools.partial(view, parts[slot][p], order, p, ph), bufs))
            if ph == 2:
                for p, a, i, g, bufs in info:
                    for k, by in enumerate((1, -1, 2)):
                        go(p, ph, k, g(i + by), bufs[k], step(a, by))
                yield
                for p, a, i, g, bufs in info:
                    for k in range(3):
                        arrived(p, ph, k, bufs[k])
                    add(g(i), bufs)
                break
            for p, a, i, g, bufs in info:
                go(p, ph, 0, g(i + 2, 0), bufs[0], step(a, 1))
                go(p, ph, 1, g(i + 2, 1), bufs[1], step(a, -1))
            yield
            for p, a, i, g, bufs in info:
                arrived(p, ph, 0, bufs[0])
                add(g(i + 1, 0), [bufs[0]])
                go(p, ph, 2, g(i + 1), bufs[2], step(a, 1))
                arrived(p, ph, 1, bufs[1])
                add(g(i - 1, 1), [bufs[1]])
                go(p, ph, 3, g(i - 1), bufs[3], step(a, -1))
            yield
            for p, a, i, g, bufs in info:
                arrived(p, ph, 2, bufs[2])
                arrived(p, ph, 3, bufs[3])
                add(g(i), [bufs[2], bufs[3]])
        for p in range(3):
            val = parts[slot][p][zl, y, x, zh]
            stage_out[p][j] = val
            square = val * val
            total = tile[...]
            for t in range(PART_ROWS[p] // 8):
                for k in range(2):
                    total = total + square[8 * t : 8 * t + 8, 128 * k : 128 * k + 128]
            tile[...] = total
        for cp in mine:
            cp.wait_send()
        if reused():
            for device in neighbours:
                pl.semaphore_signal(credit.at[slot], inc=1, device_id=device, device_id_type=MESH)

    def tail(j):
        kind, half = JOB_KIND[j // 2], j % 2
        o = out.at[kind]

        def rows_of(p, xi, zi, count):
            n_rows = PART_ROWS[p]
            start = half * 512 + PART_BASE[p] + (lax.rem(xi + 4, 4) * 2 + zi) * n_rows
            return pl.ds(pl.multiple_of(start, 8), count * n_rows)

        def go(p, k, src, rows, device):
            cp = remote(src, o.at[rows], gss.at[j, p, k], grs.at[j, p, k], device)
            cp.start()
            unsent.append(cp)

        def arrived(p, k, rows):
            remote(o.at[rows], o.at[rows], gss.at[j, p, k], grs.at[j, p, k], mate).wait_recv()

        own = []
        for p in range(3):
            rows = rows_of(p, x, zh, 1)
            cp = pltpu.make_async_copy(stage_out[p].at[j], o.at[rows], ol.at[j, p])
            cp.start()
            own.append(cp)
            go(p, 0, stage_out[p].at[j], rows, step("z", 2))
        yield
        for p in range(3):
            own[p].wait()
            arrived(p, 0, rows_of(p, x, 1 - zh, 1))
            both = rows_of(p, x, 0, 2)
            go(p, 1, o.at[both], both, step("x", 1))
            go(p, 2, o.at[both], both, step("x", -1))
        yield
        for p in range(3):
            arrived(p, 1, rows_of(p, x - 1, 0, 2))
            arrived(p, 2, rows_of(p, x + 1, 0, 2))
            left, right = rows_of(p, x - 1, 0, 1), rows_of(p, x + 1, 1, 1)
            go(p, 3, o.at[left], left, step("x", 1))
            go(p, 4, o.at[right], right, step("x", -1))
        yield
        for p in range(3):
            arrived(p, 3, rows_of(p, x + 2, 0, 1))
            arrived(p, 4, rows_of(p, x + 2, 1, 1))

    JOB_KIND = (3, 2, 1, 0)

    def transpose_into(dst, src):
        def body(i, carry):
            cols = pl.ds(pl.multiple_of(i * 128, 128), 128)
            dst[cols, :] = jnp.transpose(src[:, :, cols].reshape(512, 128))
            return carry
        lax.fori_loop(0, 8, body, 0)

    def store_part(slot, a, b, val):
        for p in range(3):
            n_rows = PART_ROWS[p]
            for xi in range(4):
                for zi in range(2):
                    start = PART_BASE[p] + (xi * 2 + zi) * n_rows
                    parts[slot][p][a, b, xi, zi] = val[start : start + n_rows]

    prepared = set()

    def prepare(kind):
        if kind in prepared:
            return
        prepared.add(kind)
        if kind == 3:
            transpose_into(hT, hh)
        if kind == 2:
            transpose_into(hT, dm)
        if kind == 1:
            loads["h2"].wait()
            transpose_into(hT, hh)
            loads["h1"] = load(0, r["h1_i"], hh)
        if kind == 0:
            loads["h1"].wait()
            transpose_into(hT, hh)

    def fill(j, slot):
        kind, half = JOB_KIND[j // 2], j % 2
        prepare(kind)
        rows = pl.ds(half * 512, 512)
        right = {3: dl, 2: u, 1: dl}

        def body(i, carry):
            g = right[kind][i] if kind else r["dq6"][i]
            store_part(slot, i // 4, lax.rem(i, 4), jnp.dot(hT[rows, :], g, preferred_element_type=F32))
            return carry

        lax.fori_loop(0, 8 if kind else 6, body, 0)
        if kind == 0:
            for jj in range(2):
                cols = pl.ds(pl.multiple_of((2 * jj + c) * 256, 256), 256)
                g = da[:, :, cols].reshape(512, 256)
                store_part(slot, 1, 2 + jj, jnp.dot(oT[rows, :], g, preferred_element_type=F32))

    queue = list(range(JOBS))
    running = []
    tails = []
    free = list(range(SLOTS))
    ready = {3}
    used = set()

    steps_done = {}

    def launch():
        if not (queue and free and JOB_KIND[queue[0] // 2] in ready):
            return
        if running and steps_done[running[-1][1]] < 1:
            return
        j = queue.pop(0)
        slot = free.pop(0)
        fill(j, slot)
        gen = phases(j, slot, slot in used, lambda: len(queue) > len(free))
        used.add(slot)
        next(gen)
        steps_done[j] = 0
        running.append((gen, j, slot))

    def service(count=1):
        for _ in range(count):
            old = list(tails)
            for entry in list(running):
                gen, j, slot = entry
                try:
                    next(gen)
                    steps_done[j] += 1
                except StopIteration:
                    running[:] = [e for e in running if e is not entry]
                    free.append(slot)
                    t = tail(j)
                    next(t)
                    tails.append(t)
            launch()
            for gen in old:
                try:
                    next(gen)
                except StopIteration:
                    tails.remove(gen)

    tile[...] = jnp.zeros((8, 128), F32)
    biasp[...] = jnp.zeros((160, 128), F32)
    dmod[...] = jnp.zeros((2, 8, 1024), F32)
    loads["h3"].wait()
    loads["dl"].wait()
    launch()
    loads["h2"] = load(0, r["h2_i"], hh)

    def store_bias(start, val):
        for i in range(val.shape[1] // 128):
            biasp[pl.ds(start + i, 1), :] = val[:, 128 * i : 128 * i + 128]

    def blocks(fn):
        for img in range(2):
            def body(i, carry, img=img):
                fn(img, pl.ds(pl.multiple_of(img * 128 + i * 32, 32), 32))
                return carry
            lax.fori_loop(0, 4, body, 0)

    def exchange(k, ref):
        cp = remote(ref.at[c], ref.at[c], ps.at[k], pr.at[k], mate)
        cp.start()
        return cp

    def swap(k):
        cp = remote(acc.at[1 - c], got, ps.at[k], pr.at[k], mate)
        cp.start()
        return cp

    def back_rows(grad, count):
        def body(i, carry):
            for half in range(2):
                part = lax.dot_general(
                    grad[i, 256 * half : 256 * half + 256, :], wb[i // 4, lax.rem(i, 4)], NT,
                    preferred_element_type=F32,
                )

                @pl.when(i == 0)
                def _():
                    acc[half] = part

                @pl.when(i > 0)
                def _():
                    acc[half] += part

            return carry
        lax.fori_loop(0, count, body, 0)

    def norm_back(img, v, scale, shift, dy):
        center = v - jnp.mean(v, -1, keepdims=True)
        inv = lax.rsqrt(jnp.mean(center * center, -1, keepdims=True) + NORM_EPS)
        unit = center * inv
        dmod[img, scale : scale + 1, :] += jnp.sum(dy * unit, axis=0, keepdims=True)
        dmod[img, shift : shift + 1, :] += jnp.sum(dy, axis=0, keepdims=True)
        dn = dy * (1.0 + ada_row(ada, scale, img))
        return inv * (
            dn - jnp.mean(dn, -1, keepdims=True) - unit * jnp.mean(dn * unit, -1, keepdims=True)
        )

    loads["w3"].wait()
    back_rows(dl, 8)
    cp = swap(0)
    w_next = load(2, r["w_i"].at[:, :, 2], wb)

    def head_bias(i, carry):
        store_bias(128 + (2 * i + c) * 2, jnp.sum(dl[i].astype(F32), axis=0, keepdims=True))
        return carry

    lax.fori_loop(0, 8, head_bias, 0)
    service()
    loads["x2"].wait()
    loads["mlp"].wait()
    cp.wait()
    fc2_rows = jnp.zeros((1, 1024), F32)

    def do_x2(img, rows):
        grad = norm_back(img, xa[rows, :], 6, 7, acc[c, rows, :] + got[rows, :])
        dx[rows, :] = grad
        dmod[img, 1:2, :] += jnp.sum(grad * xb[rows, :], axis=0, keepdims=True)
        low = (ada_row(ada, 1, img) * grad).astype(BF16)
        dm[c, rows, :] = low
        r["gst"][0, 0:1, :] += jnp.sum(low.astype(F32), axis=0, keepdims=True)

    r["gst"][0, 0:1, :] = fc2_rows
    blocks(do_x2)
    cp = exchange(1, dm)
    store_bias(120, r["gst"][0, 0:1, :])
    loads["x1"] = load(3, r["x1_i"], xa)
    loads["att"] = load(4, r["att_i"], xb)
    cp.wait()
    loads["u"].wait()
    ready.add(2)
    service()
    w_next.wait()

    fb = r["fb"]

    def f_load(i):
        return pltpu.make_async_copy(r["f_i"].at[i], fb.at[lax.rem(i, 2)], fs.at[lax.rem(i, 2)])

    f_load(0).start()

    def do_df(i, carry):
        @pl.when(i < 7)
        def _():
            f_load(i + 1).start()

        du = jnp.dot(dm[...].reshape(512, 1024), wb[i // 4, lax.rem(i, 4)], preferred_element_type=F32)
        f_load(i).wait()
        v = fb[lax.rem(i, 2)]
        k0 = 0.7978845608028654
        th = jnp.tanh(k0 * (v + 0.044715 * (v * v * v)))
        slope = 0.5 * (1.0 + th) + 0.5 * v * (1.0 - th * th) * (k0 * (1.0 + 3.0 * 0.044715 * (v * v)))
        df = (slope * du).astype(BF16)
        dl[i] = df
        store_bias(88 + (2 * i + c) * 2, jnp.sum(df.astype(F32), axis=0, keepdims=True))
        return carry

    while 1 in queue:
        service()
    lax.fori_loop(0, 8, do_df, 0)
    ready.add(1)
    w_next = load(2, r["w_i"].at[:, :, 1], wb)
    service()
    w_next.wait()
    back_rows(dl, 8)
    cp = swap(2)
    w_next = load(2, r["wo_i"], wb.at[0])
    loads["x1"].wait()
    loads["att"].wait()
    loads["ot"].wait()
    ot_swap = exchange(3, otp)
    service()
    cp.wait()

    def do_x1(img, rows):
        grad = norm_back(img, xa[rows, :], 3, 5, acc[c, rows, :] + got[rows, :]) + dx[rows, :]
        dmod[img, 0:1, :] += jnp.sum(grad * xb[rows, :], axis=0, keepdims=True)
        low = (ada_row(ada, 0, img) * grad).astype(BF16)
        da[c, rows, :] = low
        r["gst"][0, 0:1, :] += jnp.sum(low.astype(F32), axis=0, keepdims=True)

    r["gst"][0, 0:1, :] = fc2_rows
    blocks(do_x1)
    da_swap = exchange(4, da)
    store_bias(80, r["gst"][0, 0:1, :])
    w_next.wait()
    dov, doh, hb = r["dov"], r["doh"], r["hb"]
    for img in range(2):
        rows = pl.ds(128 * img, 128)
        low = jnp.zeros((128, 1024), F32)
        for k in range(4):
            low += lax.dot_general(
                da[c, rows, 256 * k : 256 * k + 256], wb[0, k], NT, preferred_element_type=F32
            )
        dov[img] = low.astype(BF16)
    w_next = load(2, r["w_i"].at[:, :, 0], wb)

    def do_sends(fn, img):
        for p in range(4):
            for q in range(2):
                src = dov.at[img, :, pl.ds(((p // 2 * 2 + q) * 2 + p % 2) * 128, 128)]
                cp = remote(
                    src, doh.at[sq, img], hs.at[p, q, img], hr.at[sq, img], (base + q, p * 2 + c)
                )

                @pl.when(jnp.logical_not(jnp.logical_and(sq == p * 2 + c, c == q)))
                def _():
                    fn(cp)

    for img in range(2):
        do_sends(lambda cp: cp.start(), img)

    @pl.when(owner == c)
    def _():
        doh[sq] = dov[:, :, head_lanes(pair, c)]

    kcol = r["kcol"]
    for img in range(2):
        for g in range(8):
            kcol[img, g] = column_of(slots_all[g * 2 + owner, pl.ds(img, 1), :])
    service()
    ot_swap.wait()
    transpose_into(oT, otp)

    loads["hb"].wait()
    dkv, dsrc, dr, dq6 = r["dkv"], r["dsrc"], r["dr"], r["dq6"]
    low_lanes = lax.broadcasted_iota(jnp.int32, (256, 128), 1) < 64
    low_rows = lax.broadcasted_iota(jnp.int32, (128, 256), 0) < 64

    sends = []
    for img in range(2):
        for i in range(8):
            landed = doh.at[i, img]

            @pl.when(jnp.logical_or(sq != i, owner != c))
            def _():
                remote(landed, landed, hs.at[0, 0, img], hr.at[i, img], mate).wait_recv()

        dkv[...] = jnp.zeros((2, 1024, 128), F32)

        def attend_block(qb, carry, img=img):
            q = jnp.concatenate([hb[2 * qb, 0, img], hb[2 * qb + 1, 0, img]], axis=0)
            k = jnp.concatenate([hb[g, 1, img] for g in range(8)], axis=0)
            v = jnp.concatenate([hb[g, 2, img] for g in range(8)], axis=0)
            do = jnp.concatenate([doh[2 * qb, img], doh[2 * qb + 1, img]], axis=0)
            kT = jnp.transpose(k)
            key = jnp.concatenate([kcol[img, g] for g in range(8)], axis=0)[:, 0:1]
            query = jnp.concatenate(
                [slots_all[(2 * qb + i) * 2 + owner, 2 + img : 3 + img, :] for i in range(2)], axis=1
            )
            seen_by = key <= query
            heads = []
            for h in range(2):
                mask = low_lanes if h == 0 else jnp.logical_not(low_lanes)
                qh = jnp.where(mask, q, jnp.zeros_like(q))
                doh_h = jnp.where(mask, do, jnp.zeros_like(do))
                sc = lax.dot_general(k, qh, NT, preferred_element_type=F32) * SCORE_SCALE
                sc = jnp.where(seen_by, sc, -1e30)
                e = jnp.exp(sc - jnp.max(sc, axis=0, keepdims=True))
                p = e / jnp.sum(e, axis=0, keepdims=True)
                dpr = lax.dot_general(v, doh_h, NT, preferred_element_type=F32)
                inner = jnp.sum(p * dpr, axis=0, keepdims=True)
                ds = (p * (dpr - inner)).astype(BF16)
                dkv[0] += jnp.dot(ds, qh, preferred_element_type=F32)
                dkv[1] += jnp.dot(p.astype(BF16), doh_h, preferred_element_type=F32)
                heads.append(jnp.dot(kT, ds, preferred_element_type=F32))
            dq = jnp.transpose(jnp.where(low_rows, heads[0], heads[1]) * SCORE_SCALE).astype(BF16)
            dsrc[2 * qb, 0, img] = dq[:128]
            dsrc[2 * qb + 1, 0, img] = dq[128:]
            return carry

        lax.fori_loop(0, 4, attend_block, 0)
        for g in range(8):
            dsrc[g, 1, img] = (dkv[0, 128 * g : 128 * g + 128] * SCORE_SCALE).astype(BF16)
            dsrc[g, 2, img] = dkv[1, 128 * g : 128 * g + 128].astype(BF16)
        for i, to in enumerate(line):
            cp = remote(
                dsrc.at[to, :, img], dr.at[sq, :, img], as_.at[i, img], ar.at[i, img], (dp, to)
            )
            cp.start()
            sends.append(cp)
        if img == 0:
            service()
    dr[sq] = dsrc[sq]
    service(1)
    if queue[0] >= 6:
        prepare(0)
    service(1)
    for cp in sends:
        cp.wait()
    for t in range(3):
        for jj in range(2):
            for half in range(2):
                for ip in range(2):
                    dq6[t * 2 + jj, ip * 256 : ip * 256 + 256, half * 128 : half * 128 + 128] = dr[
                        (jj * 2 + half) * 2 + ip, t
                    ].reshape(256, 128)
    da_swap.wait()
    for jj in range(2):
        for start, t in ((64, 0), (72, 2)):
            store_bias(
                start + (2 * jj + c) * 2,
                jnp.sum(dq6[t * 2 + jj].astype(F32), axis=0, keepdims=True),
            )
    w_next.wait()
    back_rows(dq6, 6)
    cp = swap(5)
    ready.add(0)
    service()
    cp.wait()

    def do_x0(img, rows):
        norm_back(img, r["x_in"][rows, :].astype(F32), 2, 4, acc[c, rows, :] + got[rows, :])

    blocks(do_x0)
    for img in range(2):
        do_sends(lambda cp: cp.wait_send(), img)

    smsg, sgot, smine = r["smsg"], r["sgot"], r["smine"]
    sall, spart, sback = r["sall"], r["spart"], r["sback"]
    for k in range(8):
        both = dmod[0, k : k + 1, :] + dmod[1, k : k + 1, :]
        for i in range(8):
            biasp[8 * k + i : 8 * k + i + 1, :] = both[:, 128 * i : 128 * i + 128]
    for d in range(16):
        for img in range(2):
            for i in range(4):
                lo = (d % 2) * 512 + i * 128
                smsg[d, img * 4 + i : img * 4 + i + 1, :] = dmod[img, d // 2 : d // 2 + 1, lo : lo + 128]
        smsg[d, 8:18, :] = biasp[10 * d : 10 * d + 10, :]
        smsg[d, 18:24, :] = jnp.broadcast_to(r["loss"][0:1, :], (6, 128))
    cps = []
    for i, d in enumerate(row):
        cp = remote(smsg.at[d], sgot.at[dp], s1.at[i], r1.at[i], (d, sq))
        cp.start()
        cps.append(cp)
    sgot[dp] = smsg[dp]
    service()
    for cp in cps:
        cp.wait()
    for d in range(16):
        smine[d] = sgot[d, 0:8, :]
    for i in range(2):
        smine[16 + i] = sum(sgot[d, 8 + 8 * i : 16 + 8 * i, :] for d in range(16))
    cps = []
    for i, s in enumerate(line):
        cp = remote(smine, sall.at[sq], s2.at[i], r2.at[i], (dp, s))
        cp.start()
        cps.append(cp)
    sall[sq] = smine[...]
    service()
    for cp in cps:
        cp.wait()
    for k in range(18):
        smine[k] = sum(sall[s, k] for s in range(8))
    r["bias_sum"][0] = smine[16]
    r["bias_sum"][1] = smine[17]
    dada = jnp.concatenate(
        [
            jnp.concatenate([smine[d, 4 * i + k : 4 * i + k + 1, :] for k in range(4)], axis=1)
            for d in range(16)
            for i in range(2)
        ],
        axis=0,
    )

    def dcond_part(d, carry):
        rows = pl.ds(pl.multiple_of(64 * d, 64), 64)
        spart[d] = lax.dot_general(
            dada, r["cond_w"][rows, :].astype(F32), NT, precision=HIGH, preferred_element_type=F32
        )
        return carry

    lax.fori_loop(0, 16, dcond_part, 0)
    cps = []
    for i, d in enumerate(row):
        cp = remote(spart.at[d], sback.at[dp], s3.at[i], r3.at[i], (d, sq))
        cp.start()
        cps.append(cp)
    sback[dp] = spart[dp]
    service()
    squares = jnp.zeros((8, 128), F32)

    def fold(val):
        total = jnp.zeros((8, 128), F32)
        for i in range(val.shape[0] // 8):
            for k in range(val.shape[1] // 128):
                total = total + val[8 * i : 8 * i + 8, 128 * k : 128 * k + 128]
        return total

    gcs = r["gcs"]

    def gcond_copy(d):
        slot = lax.rem(d, 2)
        rows = pl.ds(pl.multiple_of(64 * d, 64), 64)
        return pltpu.make_async_copy(gcs.at[slot], r["gcond"].at[rows], gl.at[slot])

    def gcond_part(d, total):
        @pl.when(d > 1)
        def _():
            gcond_copy(d - 2).wait()

        val = lax.dot_general(
            r["cond_all"][d].astype(F32), dada, (((0,), (0,)), ((), ())),
            precision=HIGH, preferred_element_type=F32,
        )
        gcs[lax.rem(d, 2)] = val
        gcond_copy(d).start()
        return total + fold(val * val)

    squares = squares + lax.fori_loop(0, 16, gcond_part, squares)
    gcond_copy(14).wait()
    gcond_copy(15).wait()
    for cp in cps:
        cp.wait()
    dcond = sum(sback[d] for d in range(16))
    emb = r["emb"][...]
    sig = 1.0 / (1.0 + jnp.exp(-emb))
    demb = dcond * (sig * (1.0 + emb * (1.0 - sig)))
    labels = jnp.concatenate(
        [msg_all[d, 10:11, i : i + 1] for d in range(16) for i in range(2)], axis=0
    ).astype(jnp.int32)
    hit = jnp.where(lax.broadcasted_iota(jnp.int32, (32, 1000), 1) == labels, 1.0, 0.0)
    gtable = jnp.dot(jnp.transpose(demb), hit, precision=HIGH, preferred_element_type=F32)
    r["gtable"][...] = gtable
    table_squares = jnp.sum(jnp.sum(gtable * gtable, axis=1, keepdims=True), axis=0, keepdims=True)
    bias_rows = jnp.concatenate([smine[16], smine[17][0:2]], axis=0)
    bias_squares = jnp.sum(jnp.sum(bias_rows * bias_rows, axis=1, keepdims=True), axis=0, keepdims=True)
    spot = jnp.logical_and(
        lax.broadcasted_iota(jnp.int32, (8, 128), 0) == 0, lax.broadcasted_iota(jnp.int32, (8, 128), 1) == 0
    )
    squares = squares + jnp.where(spot, table_squares + bias_squares, 0.0)
    while queue or running:
        service()
    tile[...] += squares * 0.125
    tiles = r["tiles"]
    cps = []
    for i, d in enumerate(row):
        cp = remote(tile, tiles.at[i], ns.at[i], nr.at[i], (d, sq))
        cp.start()
        cps.append(cp)
    for cp in cps:
        cp.wait()
    tile[...] += sum(tiles[i] for i in range(15))
    cps = []
    for i, d in enumerate(line):
        cp = remote(tile, tiles.at[15 + i], ns.at[15 + i], nr.at[15 + i], (dp, d))
        cp.start()
        cps.append(cp)
    service()
    for cp in cps:
        cp.wait()
    total = tile[...] + sum(tiles[15 + i] for i in range(7))
    total = jnp.sum(jnp.sum(total, axis=1, keepdims=True), axis=0, keepdims=True)
    r["norm"][...] = jnp.broadcast_to(total, (8, 128))
    while tails:
        service()
    for cp in unsent:
        cp.wait_send()


def backward_pass(small, kept):
    dma = pltpu.SemaphoreType.DMA
    sd = jax.ShapeDtypeStruct
    vm = pltpu.VMEM
    scratch = [
        vm((2, 4, 1024, 256), BF16),
        vm((8, 512, 256), BF16), vm((8, 512, 256), BF16), vm((2, 512, 256), F32),
        vm((2, 256, 1024), BF16), vm((1024, 512), BF16), vm((1024, 512), BF16),
        vm((2, 256, 1024), BF16), vm((2, 256, 1024), BF16), vm((2, 256, 1024), BF16),
        vm((2, 256, 1024), F32), vm((256, 1024), F32), vm((256, 1024), F32), vm((256, 1024), F32),
        vm((256, 1024), F32),
        vm((8, 3, 2, 128, 128), BF16), vm((8, 2, 128, 128), BF16), vm((2, 128, 1024), BF16),
        vm((2, 1024, 128), F32), vm((8, 3, 2, 128, 128), BF16), vm((8, 3, 2, 128, 128), BF16),
        vm((6, 512, 256), BF16), vm((2, 8, 128, 128), F32), vm((2, 8, 1024), F32), vm((160, 128), F32),
        vm((16, 24, 128), F32), vm((16, 24, 128), F32), vm((18, 8, 128), F32), vm((8, 18, 8, 128), F32),
        vm((16, 32, 64), F32), vm((16, 32, 64), F32), vm((1, 8, 1024), F32),
        vm((2, 64, 512), F32),
        vm((8, 128), F32), vm((22, 8, 128), F32),
    ]
    for _ in range(SLOTS):
        for p in range(3):
            scratch.append(vm((2, 4, 4, 2, PART_ROWS[p], 256), F32))
    for p in range(3):
        scratch.append(vm((JOBS, PART_ROWS[p], 256), F32))
    scratch += [vm(shape, F32) for shape in recv_shapes()]
    scratch += [
        dma((9,)), dma((2,)), dma((6,)), dma((6,)), dma((4, 2, 2)), dma((8, 2)), dma, dma((7, 2)), dma((7, 2)),
        dma((JOBS, 9, 4)), dma((JOBS, 9, 4)), dma((JOBS, 3, 5)), dma((JOBS, 3, 5)), dma((JOBS, 3)),
        pltpu.SemaphoreType.REGULAR((SLOTS,)),
        dma((15,)), dma((15,)), dma((7,)), dma((7,)), dma((15,)), dma((15,)), dma((22,)), dma((22,)),
        dma((2,)),
    ]
    return pl.pallas_call(
        backward_kernel,
        out_shape=[
            sd((4, 1024, 256), F32), sd((8, 128), F32), sd((2, 8, 128), F32),
            sd((64, 1000), F32), sd((1024, 512), F32),
        ],
        in_specs=[VM] * len(small) + [ANY] * len(kept),
        out_specs=[ANY, VM, VM, VM, ANY],
        scratch_shapes=scratch,
        compiler_params=params(1, 64 * 2**20 - 2**17),
    )(*small, *kept)


def adamw(weight, first, second, grad, factor):
    clipped = grad * factor
    first_new = BETA_ONE * first + (1.0 - BETA_ONE) * clipped
    second_new = BETA_TWO * second + (1.0 - BETA_TWO) * clipped * clipped
    first_hat = first_new / (1.0 - BETA_ONE**STEP)
    second_hat = second_new / (1.0 - BETA_TWO**STEP)
    weight_new = weight - LEARN * (first_hat / (jnp.sqrt(second_hat) + ADAM_EPS) + DECAY * weight)
    return (weight_new, first_new, second_new)


def local(
    x_in, scale_ids, pad_mask, loss_weights, targets, labels,
    cond_w, attn_w, mlp_w, head_w, class_table, biases,
    first_cond, first_attn, first_mlp, first_head, first_table, first_bias,
    second_cond, second_attn, second_mlp, second_head, second_table, second_bias,
):

    x_rows = x_in.reshape(256, 1024)
    small = (labels.reshape(1, 2), biases.reshape(10, 128), scale_ids, pad_mask, loss_weights, targets)
    (
        msg_all, slots_all, cond_all, embedded, ada, loss_tile, wb_cond,
        w, wo, h1, h2, h3, heads, o, att, x1, mlp, x2, f, u, dlogits,
    ) = forward_pass(small + (class_table.T, cond_w, x_rows), (attn_w, mlp_w, head_w))
    true_count = loss_tile[7, 0]
    summed, squares, bias_sum, grad_table, grad_cond = backward_pass(
        (msg_all, slots_all, cond_all, embedded, ada, loss_tile, wb_cond, x_rows),
        (w, wo, h1, h2, h3, heads, o, att, x1, mlp, x2, f, u, dlogits),
    )
    bias_sum = bias_sum.reshape(16, 128)
    loss_total = bias_sum[10, 0]
    grad_bias = bias_sum[:10].reshape(1280)
    grad_norm = jnp.sqrt(squares[0, 0])
    factor = jnp.minimum(1.0, CLIP / grad_norm)
    grads = (grad_cond, summed[0], summed[1:3], summed[3], grad_table, grad_bias)
    weights = (cond_w, attn_w, mlp_w, head_w, class_table.T, biases)
    firsts = (first_cond, first_attn, first_mlp, first_head, first_table.T, first_bias)
    seconds = (second_cond, second_attn, second_mlp, second_head, second_table.T, second_bias)
    results = [
        adamw(weight, first, second, grad, factor)
        for weight, first, second, grad in zip(weights, firsts, seconds, grads)
    ]
    new_weights = [entry[0] for entry in results]
    new_first = [entry[1] for entry in results]
    new_second = [entry[2] for entry in results]
    copies = [weight.astype(BF16) for weight in new_weights]
    for group in (new_weights, new_first, new_second, copies):
        group[4] = group[4].T
    return tuple(new_weights + new_first + new_second + copies + [grad_norm, loss_total, true_count])


def solution(mesh):
    split = (P(None, "dp"), P(None, "dp"), P(None, None, "dp"), P(None, "dp"), P(None, "dp"), P("dp"))
    in_specs = (P("dp", "seq", None),) + (P("dp", "seq"),) * 4 + (P("dp"),) + split * 3
    out_specs = split * 4 + (P(), P(), P())
    return jax.shard_map(local, mesh=mesh, in_specs=in_specs, out_specs=out_specs, check_vma=False)
```

```python
import functools

import jax
import jax.numpy as jnp
from jax import lax
from jax.experimental import pallas as pl
from jax.experimental.pallas import tpu as pltpu
from jax.sharding import PartitionSpec as P

STEP = 5
HIGH = lax.Precision.HIGHEST
NORM_EPS = 1e-06
CLIP = 0.01
LEARN = 0.02
DECAY = 0.1
BETA_ONE = 0.5
BETA_TWO = 0.5
ADAM_EPS = 1e-08
SCORE_SCALE = 0.125
MESH = pl.DeviceIdType.MESH
F32 = jnp.float32
BF16 = jnp.bfloat16
ANY = pl.BlockSpec(memory_space=pl.ANY)
VM = pl.BlockSpec(memory_space=pltpu.VMEM)

ROWS_YZ = 320
HALF_YZ = 160
QUARTER = 48


def place():
    dp = lax.axis_index("dp")
    sq = lax.axis_index("seq")
    core = lax.rem(dp, 2)
    y = lax.rem(dp // 2, 4)
    z = lax.rem(sq, 2) * 2 + dp // 8
    return sq // 2, y, z, core


def at(x, y, z, core):
    x, y, z = lax.rem(x + 4, 4), lax.rem(y + 4, 4), lax.rem(z + 4, 4)
    return (lax.rem(z, 2) * 8 + y * 2 + core, x * 2 + z // 2)


def greet(devices):
    bar = pltpu.get_barrier_semaphore()
    for device in devices:
        pl.semaphore_signal(bar, inc=1, device_id=device, device_id_type=MESH)
    pl.semaphore_wait(bar, len(devices))


def remote(src, dst, send, recv, device):
    return pltpu.make_async_remote_copy(
        src_ref=src, dst_ref=dst, send_sem=send, recv_sem=recv, device_id=device, device_id_type=MESH
    )


def params(collective_id, vmem=None):
    return pltpu.CompilerParams(
        collective_id=collective_id, has_side_effects=True, vmem_limit_bytes=vmem
    )


def group_peers():
    dp = lax.axis_index("dp")
    sq = lax.axis_index("seq")
    core = lax.rem(dp, 2)
    out = [(dp + 1 - 2 * core, sq)]
    for i in range(1, 8):
        for flip in range(2):
            out.append((dp + flip * (1 - 2 * core), lax.rem(sq + i, 8)))
    return out


def head_lanes(pair, core):
    return pl.ds(pl.multiple_of(((pair // 2 * 2 + core) * 2 + lax.rem(pair, 2)) * 128, 128), 128)


NT = (((1,), (1,)), ((), ()))


def normalize(v):
    center = v - jnp.mean(v, -1, keepdims=True)
    spread = jnp.mean(center * center, -1, keepdims=True)
    return center * lax.rsqrt(spread + NORM_EPS)


def ada_row(ada, k, img):
    return jnp.concatenate([ada[2 * k, img : img + 1, :], ada[2 * k + 1, img : img + 1, :]], axis=1)


def column_of(row):
    return jnp.transpose(jnp.broadcast_to(row, (128, 128)))


def forward_kernel(
    labels_in, bias_in, scale_in, pad_in, weight_in, target_in, table, cond_w, x_in, attn_in, mlp_in, head_in,
    msg_all, slots_all, cond_all, emb_out, ada, loss_out, cond_low,
    w_o, wo_o, h1_o, h2_o, h3_o, hb_o, ot_o, att_o, x1_o, mlp_o, x2_o, f_o, u_o, dl_o,
    msg, slots, w, wo, h1, h2, h3, src, hb, oh, ot, att, x1, mlp, x2, acc, got_acc, f, u, dl,
    cond_own, ada_own, bias, qcol, tcol, wcol, stats,
    gs, gr, gl, os, orr, s1, r1, s2, r2, s3, r3, s4, r4, ps, pr, as_, ar, al, ts, tr, tl, outs_sem,
):
    x, y, z, c = place()
    dp = lax.axis_index("dp")
    sq = lax.axis_index("seq")
    zl = lax.rem(z, 2)
    up, down, far = lax.rem(y + 1, 4), lax.rem(y + 3, 4), lax.rem(y + 2, 4)
    yp, ym = at(x, y + 1, z, c), at(x, y - 1, z, c)
    zp, zm = at(x, y, z + 1, c), at(x, y, z - 1, c)
    xp, xm = at(x + 1, y, z, c), at(x - 1, y, z, c)
    zs = at(x, y, z + 1 - 2 * c, c)
    mate = at(x, y, z, 1 - c)
    base = dp - c
    row = [(lax.rem(dp + i, 16), sq) for i in range(1, 16)]
    group = group_peers()
    incoming = []
    for j in range(8):
        rows = pl.ds(512 * (j % 2), 512)
        source = (attn_in, mlp_in.at[0], mlp_in.at[1], head_in)[j // 2]
        incoming.append(pltpu.make_async_copy(source.at[rows], f.at[j], gl.at[j, 0]))
        incoming[-1].start()
    pad = pad_in[...]
    scale = scale_in[...].astype(F32)
    slots[...] = jnp.zeros((16, 128), F32)
    slots[0:2, :] = jnp.where(pad > 0, scale, 1000.0)
    slots[2:4, :] = scale
    slots[4:6, :] = target_in[...].astype(F32)
    slots[6:8, :] = (weight_in[...] * pad).astype(F32)
    real = jnp.sum(jnp.sum(pad.astype(F32), axis=1, keepdims=True), axis=0, keepdims=True)
    spot = lax.broadcasted_iota(jnp.int32, (1, 128), 1)
    label = labels_in[...].astype(F32)
    msg[...] = jnp.zeros((16, 128), F32)
    msg[0:10, :] = bias_in[...].astype(BF16).astype(F32)
    msg[10:11, :] = jnp.where(
        spot == 0, label[:, 0:1], jnp.where(spot == 1, label[:, 1:2], jnp.where(spot == 2, real, 0.0))
    )
    greet(row + group[1:] + [at(x, y, z + 2 * zl - 1, c)])

    pending = []

    def keep(k, src_ref, dst_ref):
        cp = pltpu.make_async_copy(src_ref, dst_ref, outs_sem.at[k])
        cp.start()
        pending.append(cp)
        return cp

    def rows_at(j, start, count):
        return pl.ds(512 * (j % 2) + start, count)

    def quarter(j, pos):
        start = 512 * (j % 2) + ROWS_YZ + QUARTER * lax.rem(pos + 4, 4)
        return pl.ds(pl.multiple_of(start, 16), QUARTER)

    sent = []

    def go(j, k, a, b, device):
        cp = remote(a, b, gs.at[j, k], gr.at[j, k], device)
        cp.start()
        sent.append(cp)

    def got(j, k, ref):
        remote(ref, ref, gs.at[j, k], gr.at[j, k], mate).wait_recv()

    def stage(kind, j):
        m = j // 2
        full, first = rows_at(j, 0, ROWS_YZ), rows_at(j, 0, HALF_YZ)
        second, mine = rows_at(j, HALF_YZ, HALF_YZ), quarter(j, x)
        if kind == "A":
            incoming[j].wait()
            w[zl, y, m, full, :] = f[j, 0:ROWS_YZ, :].astype(BF16)
            at_rows = pl.ds(pl.multiple_of(ROWS_YZ + QUARTER * x, 16), QUARTER)
            w[zl, y, m, mine, :] = f[j, at_rows, :].astype(BF16)
            go(j, 0, w.at[zl, y, m, full], w.at[zl, y, m, full], yp)
            go(j, 1, w.at[zl, y, m, full], w.at[zl, y, m, full], ym)
            go(j, 6, w.at[zl, y, m, mine], w.at[zl, y, m, mine], zs)
        if kind == "B":
            got(j, 6, w.at[1 - zl, y, m, mine])
            go(j, 7, w.at[:, y, m, mine], w.at[:, y, m, mine], yp)
            go(j, 8, w.at[:, y, m, mine], w.at[:, y, m, mine], ym)
            got(j, 0, w.at[zl, down, m, full])
            got(j, 1, w.at[zl, up, m, full])
            go(j, 2, w.at[zl, down, m, first], w.at[zl, down, m, first], yp)
            go(j, 3, w.at[zl, up, m, second], w.at[zl, up, m, second], ym)
        if kind == "C":
            got(j, 7, w.at[:, down, m, mine])
            got(j, 8, w.at[:, up, m, mine])
            go(j, 9, w.at[0, down, m, mine], w.at[0, down, m, mine], yp)
            go(j, 10, w.at[1, up, m, mine], w.at[1, up, m, mine], ym)
            got(j, 2, w.at[zl, far, m, first])
            got(j, 3, w.at[zl, far, m, second])
            go(j, 4, w.at[zl, :, m, first], w.at[zl, :, m, first], zp)
            go(j, 5, w.at[zl, :, m, second], w.at[zl, :, m, second], zm)
        if kind == "D":
            got(j, 9, w.at[0, far, m, mine])
            got(j, 10, w.at[1, far, m, mine])
            go(j, 11, w.at[:, :, m, mine], w.at[:, :, m, mine], xp)
            go(j, 12, w.at[:, :, m, mine], w.at[:, :, m, mine], xm)
        if kind == "E":
            left, right = quarter(j, x - 1), quarter(j, x + 1)
            got(j, 11, w.at[:, :, m, left])
            got(j, 12, w.at[:, :, m, right])
            go(j, 13, w.at[0, :, m, left], w.at[0, :, m, left], xp)
            go(j, 14, w.at[1, :, m, right], w.at[1, :, m, right], xm)
        if kind == "F":
            across = quarter(j, x + 2)
            got(j, 4, w.at[1 - zl, :, m, first])
            got(j, 5, w.at[1 - zl, :, m, second])
            got(j, 13, w.at[0, :, m, across])
            got(j, 14, w.at[1, :, m, across])
            if j % 2:
                keep(m, w.at[:, :, m], w_o.at[:, :, m])
            if j == 1:
                for i in range(2):
                    remote(w.at[1, 2 + i, 0], wo.at[2 * i + c], os.at[i], orr.at[i], mate).start()
                    pltpu.make_async_copy(w.at[1, 2 + i, 0], wo.at[2 * i + c], gl.at[i, 2]).start()

    wave = [
        ["A0", "A1"], ["B0", "B1", "A2"], ["C0", "C1", "B2", "D0", "D1", "A3"],
        ["E0", "E1", "C2", "B3", "A4"], ["F0", "F1"], ["D2", "C3", "B4", "A5"],
        ["E2", "D3", "C4", "B5", "A6"], ["F2", "E3", "D4", "C5", "B6", "A7"],
        ["F3", "E4", "D5", "C6", "B7"], ["F4", "E5", "D6", "C7"],
        ["F5", "E6", "D7"], ["F6", "E7"], ["F7"],
    ]

    def pump(n=1):
        for _ in range(n):
            if wave:
                for item in wave.pop(0):
                    stage(item[0], int(item[1]))

    firsts = []
    for i, to in enumerate(row):
        cp = remote(msg, msg_all.at[dp], s1.at[i], r1.at[i], to)
        cp.start()
        firsts.append(cp)
    msg_all[dp] = msg[...]
    pump()
    for cp in firsts:
        cp.wait()
    seen = msg_all[...]
    count = jnp.sum(seen[:, 10, 2:3], axis=0, keepdims=True)
    slots[8:9, :] = jnp.broadcast_to(count, (1, 128))
    for d in range(16):
        bias[pl.ds(10 * d, 10), :] = seen[d, 0:10, :]
    seconds = []
    for i, to in enumerate(group):
        cp = remote(slots, slots_all.at[sq * 2 + c], s2.at[i], r2.at[i], to)
        cp.start()
        seconds.append(cp)
    slots_all[sq * 2 + c] = slots[...]
    classes = table.shape[1]
    lane = lax.broadcasted_iota(jnp.int32, (32, classes), 1)
    labels = jnp.concatenate([seen[d, 10:11, i : i + 1] for d in range(16) for i in range(2)], axis=0)
    hit = jnp.where(lane == labels.astype(jnp.int32), 1.0, 0.0).astype(BF16)
    emb = lax.dot_general(hit, table[...].astype(BF16), NT, preferred_element_type=F32)
    emb_out[...] = emb
    cond_own[...] = (emb / (1.0 + jnp.exp(-emb))).astype(BF16)
    cond_all[dp] = cond_own[...]
    thirds = []
    for i, to in enumerate(row):
        cp = remote(cond_own, cond_all.at[dp], s3.at[i], r3.at[i], to)
        cp.start()
        thirds.append(cp)
    pump()
    for cp in thirds:
        cp.wait()
    total = jnp.zeros((32, 512), F32)
    for d in range(16):
        low = cond_w[pl.ds(64 * d, 64), :].astype(BF16)
        cond_low[pl.ds(64 * d, 64), :] = low
        total += jnp.dot(cond_all[d], low, preferred_element_type=F32)
    total += jnp.concatenate([bias[pl.ds(dp * 4 + i, 1), :] for i in range(4)], axis=1)
    for d in range(16):
        ada_own[d] = total[2 * d : 2 * d + 2]
    fourths = []
    for i in range(15):
        to = lax.rem(dp + 1 + i, 16)
        cp = remote(ada_own.at[to], ada.at[dp], s4.at[i], r4.at[i], (to, sq))
        cp.start()
        fourths.append(cp)
    ada[dp] = ada_own[dp]
    pump()
    for cp in fourths:
        cp.wait()
    for cp in seconds:
        cp.wait()

    owner = lax.rem(sq, 2)
    for img in range(2):
        for g in range(8):
            qcol[img, g] = column_of(slots_all[g * 2 + owner, pl.ds(2 + img, 1), :])
        for q in range(2):
            at_rows = pl.ds((q * 2 + img) * 128, 128)
            tcol[at_rows, :] = column_of(slots_all[sq * 2 + q, pl.ds(4 + img, 1), :])
            wcol[at_rows, :] = column_of(slots_all[sq * 2 + q, pl.ds(6 + img, 1), :])
    true_count = jnp.sum(
        jnp.concatenate([slots_all[2 * g, 8:9, 0:1] for g in range(8)], axis=0), axis=0, keepdims=True
    )

    def blocks(fn):
        for img in range(2):
            def body(i, carry, img=img):
                fn(img, pl.ds(pl.multiple_of(img * 128 + i * 32, 32), 32))
                return carry
            lax.fori_loop(0, 4, body, 0)

    def exchange(k, ref):
        cp = remote(ref.at[c], ref.at[c], ps.at[k], pr.at[k], mate)
        cp.start()
        return cp

    def modulated(img, v, scale, shift):
        return (normalize(v) * (1.0 + ada_row(ada, scale, img)) + ada_row(ada, shift, img)).astype(BF16)

    def do_h1(img, rows):
        h1[c, rows, :] = modulated(img, x_in[rows, :].astype(F32), 2, 4)

    blocks(do_h1)
    cp = exchange(0, h1)
    pump()
    cp.wait()
    keep(4, h1, h1_o)
    pump()

    def bias_row(start):
        return jnp.concatenate([bias[pl.ds(start, 1), :], bias[pl.ds(start + 1, 1), :]], axis=1)

    tokens = h1[...].reshape(512, 1024)
    for j in range(6):
        t, jj = j // 2, j % 2
        val = jnp.dot(tokens, w[j // 4, j % 4, 0], preferred_element_type=F32)
        if t != 1:
            val = val + bias_row(64 + (0 if t == 0 else 8) + (2 * jj + c) * 2)
        val = val.astype(BF16)
        for half in range(2):
            for ip in range(2):
                src[(jj * 2 + half) * 2 + ip, t] = val[
                    ip * 256 : ip * 256 + 256, half * 128 : half * 128 + 128
                ].reshape(2, 128, 128)
    cps = [[], []]
    for img in range(2):
        for i in range(1, 8):
            to = lax.rem(sq + i, 8)
            cp = remote(
                src.at[to, :, img], hb.at[sq, :, img], as_.at[i, img], ar.at[i, img], (dp, to)
            )
            cp.start()
            cps[img].append(cp)
    hb[sq] = src[sq]
    pump()

    low_lanes = lax.broadcasted_iota(jnp.int32, (256, 128), 1) < 64

    def attend_block(i, carry):
        img, qb = i // 4, lax.rem(i, 4)
        q = jnp.concatenate([hb[2 * qb, 0, img], hb[2 * qb + 1, 0, img]], axis=0)
        k = jnp.concatenate([hb[g, 1, img] for g in range(8)], axis=0)
        v = jnp.concatenate([hb[g, 2, img] for g in range(8)], axis=0)
        key = jnp.concatenate([slots_all[g * 2 + owner, pl.ds(img, 1), :] for g in range(8)], axis=1)
        query = jnp.concatenate([qcol[img, 2 * qb], qcol[img, 2 * qb + 1]], axis=0)[:, 0:1]
        seen_by = key <= query
        heads = []
        for h in range(2):
            mask = low_lanes if h == 0 else jnp.logical_not(low_lanes)
            qh = jnp.where(mask, q, jnp.zeros_like(q))
            sc = lax.dot_general(qh, k, NT, preferred_element_type=F32) * SCORE_SCALE
            sc = jnp.where(seen_by, sc, -1e30)
            e = jnp.exp(sc - jnp.max(sc, axis=-1, keepdims=True))
            p = (e / jnp.sum(e, axis=-1, keepdims=True)).astype(BF16)
            heads.append(jnp.dot(p, v, preferred_element_type=F32))
        o = jnp.where(low_lanes, heads[0], heads[1]).astype(BF16)
        oh[2 * qb, img] = o[:128]
        oh[2 * qb + 1, img] = o[128:]
        return carry

    pair = sq // 2
    lanes = head_lanes(pair, c)

    def o_copy(i, img):
        to = lax.rem(sq + i, 8)
        return remote(
            oh.at[to, img], ot.at[pl.ds(img * 128, 128), lanes], ts.at[i, img], tr.at[pair, c, img],
            (base + owner, to),
        )

    for img in range(2):
        for cp in cps[img]:
            cp.wait()
        lax.fori_loop(4 * img, 4 * img + 2, attend_block, 0)
        pump()
        lax.fori_loop(4 * img + 2, 4 * img + 4, attend_block, 0)
        for i in range(1, 8):
            o_copy(i, img).start()

        @pl.when(owner == c)
        def _():
            ot[pl.ds(img * 128, 128), lanes] = oh[sq, img]

        @pl.when(owner != c)
        def _():
            o_copy(0, img).start()

        pump()
    keep(5, hb, hb_o)
    for img in range(2):
        for p in range(4):
            for q in range(2):
                view = ot.at[pl.ds(img * 128, 128), pl.ds(((p // 2 * 2 + q) * 2 + p % 2) * 128, 128)]

                @pl.when(jnp.logical_or(sq != p * 2 + c, c != q))
                def _():
                    remote(view, view, ts.at[0, img], tr.at[p, q, img], mate).wait_recv()

    keep(6, ot, ot_o)
    for i in range(2):
        remote(w.at[1, 2 + i, 0], wo.at[2 * i + c], os.at[i], orr.at[i], mate).wait()
        pltpu.make_async_copy(w.at[1, 2 + i, 0], wo.at[2 * i + c], gl.at[i, 2]).wait()
    keep(7, wo, wo_o)
    for k in range(4):
        cols = pl.ds(256 * k, 256)
        att[:, cols] = jnp.dot(ot[...], wo[k], preferred_element_type=F32) + bias_row(80 + 2 * k)
    keep(8, att, att_o)

    def do_h2(img, rows):
        v = x_in[rows, :].astype(F32) + ada_row(ada, 0, img) * att[rows, :]
        x1[rows, :] = v
        h2[c, rows, :] = modulated(img, v, 3, 5)

    blocks(do_h2)
    cp = exchange(1, h2)
    keep(9, x1, x1_o)
    cp.wait()
    keep(10, h2, h2_o)
    pump()

    def chunk(ref, j, kind):
        return ref[j // 4, lax.rem(j, 4), kind]

    def do_f(j, carry):
        val = jnp.dot(h2[...].reshape(512, 1024), chunk(w, j, 1), preferred_element_type=F32)
        val = val + bias_row(88 + (2 * j + c) * 2)
        f[j] = val
        act = jax.nn.gelu(val, approximate=True).astype(BF16)
        u[j] = act
        part = lax.dot_general(act, chunk(w, j, 2), NT, preferred_element_type=F32).reshape(2, 256, 1024)

        @pl.when(j == 0)
        def _():
            acc[...] = part

        @pl.when(j > 0)
        def _():
            acc[...] += part

        return carry

    lax.fori_loop(0, 8, do_f, 0)
    f_copy = keep(11, f, f_o)
    keep(12, u, u_o)
    cp = remote(acc.at[1 - c], got_acc, ps.at[2], pr.at[2], mate)
    cp.start()
    pump()
    b_two = jnp.concatenate([bias[pl.ds(120 + i, 1), :] for i in range(8)], axis=1)
    cp.wait()

    def do_h3(img, rows):
        m = acc[c, rows, :] + got_acc[rows, :] + b_two
        mlp[rows, :] = m
        v = x1[rows, :] + ada_row(ada, 1, img) * m
        x2[rows, :] = v
        h3[c, rows, :] = modulated(img, v, 6, 7)

    blocks(do_h3)
    cp = exchange(3, h3)
    pump()
    keep(13, mlp, mlp_o)
    keep(14, x2, x2_o)
    f_copy.wait()
    pending[:] = [p for p in pending if p is not f_copy]
    cp.wait()
    keep(15, h3, h3_o)

    def do_logits(j, top):
        val = jnp.dot(h3[...].reshape(512, 1024), chunk(w, j, 3), preferred_element_type=F32)
        val = val + bias_row(128 + (2 * j + c) * 2)
        f[j] = val
        return jnp.maximum(top, jnp.max(val, axis=-1, keepdims=True))

    top = lax.fori_loop(0, 8, do_logits, jnp.full((512, 1), -jnp.inf, F32))
    inner = lax.broadcasted_iota(jnp.int32, (512, 256), 1)

    def target_hit(j):
        return inner == (tcol[:, 0:1].astype(jnp.int32) - (2 * j + c) * 256)

    def do_mass(j, carry):
        mass, picked = carry
        val = f[j]
        mass = mass + jnp.sum(jnp.exp(val - top), axis=-1, keepdims=True)
        picked = picked + jnp.sum(jnp.where(target_hit(j), val, 0.0), axis=-1, keepdims=True)
        return mass, picked

    zero = jnp.zeros((512, 1), F32)
    mass, picked = lax.fori_loop(0, 8, do_mass, (zero, zero))
    lane = lax.broadcasted_iota(jnp.int32, (512, 128), 1)
    stats[c] = jnp.where(lane == 0, top, jnp.where(lane == 1, mass, picked))
    cp = exchange(4, stats)
    cp.wait()
    both = [stats[0], stats[1]]
    top_all = jnp.maximum(both[0][:, 0:1], both[1][:, 0:1])
    mass_all = sum(b[:, 1:2] * jnp.exp(b[:, 0:1] - top_all) for b in both)
    log_total = top_all + jnp.log(mass_all)
    weight = wcol[:, 0:1]
    losses = weight * (log_total - (both[0][:, 2:3] + both[1][:, 2:3]))
    loss_out[...] = jnp.broadcast_to(0.5 * jnp.sum(losses, axis=0, keepdims=True), (8, 128))
    loss_out[7:8, :] = jnp.broadcast_to(true_count, (1, 128))
    share = weight / true_count

    def do_dlogits(j, carry):
        grad = share * (jnp.exp(f[j] - log_total) - jnp.where(target_hit(j), 1.0, 0.0))
        dl[j] = grad.astype(BF16)
        return carry

    lax.fori_loop(0, 8, do_dlogits, 0)
    keep(16, dl, dl_o)
    for img in range(2):
        for i in range(1, 8):
            o_copy(i, img).wait_send()

        @pl.when(owner != c)
        def _():
            o_copy(0, img).wait_send()

    for cp in sent:
        cp.wait_send()
    for cp in pending:
        cp.wait()


def forward_pass(small, matrices):
    dma = pltpu.SemaphoreType.DMA
    sd = jax.ShapeDtypeStruct
    kept = [
        sd((2, 4, 4, 1024, 256), BF16), sd((4, 1024, 256), BF16),
        sd((2, 256, 1024), BF16), sd((2, 256, 1024), BF16), sd((2, 256, 1024), BF16),
        sd((8, 3, 2, 128, 128), BF16), sd((256, 1024), BF16),
        sd((256, 1024), F32), sd((256, 1024), F32), sd((256, 1024), F32), sd((256, 1024), F32),
        sd((8, 512, 256), F32), sd((8, 512, 256), BF16), sd((8, 512, 256), BF16),
    ]
    vm = pltpu.VMEM
    return pl.pallas_call(
        forward_kernel,
        out_shape=[
            sd((16, 16, 128), F32), sd((16, 16, 128), F32), sd((16, 32, 64), BF16),
            sd((32, 64), F32), sd((16, 2, 512), F32), sd((8, 128), F32), sd((1024, 512), BF16),
        ] + kept,
        in_specs=[VM] * len(small) + [ANY] * 3,
        out_specs=[VM] * 7 + [ANY] * len(kept),
        scratch_shapes=[
            vm((16, 128), F32), vm((16, 128), F32),
            vm((2, 4, 4, 1024, 256), BF16), vm((4, 1024, 256), BF16),
            vm((2, 256, 1024), BF16), vm((2, 256, 1024), BF16), vm((2, 256, 1024), BF16),
            vm((8, 3, 2, 128, 128), BF16), vm((8, 3, 2, 128, 128), BF16), vm((8, 2, 128, 128), BF16),
            vm((256, 1024), BF16),
            vm((256, 1024), F32), vm((256, 1024), F32), vm((256, 1024), F32), vm((256, 1024), F32),
            vm((2, 256, 1024), F32), vm((256, 1024), F32),
            vm((8, 512, 256), F32), vm((8, 512, 256), BF16), vm((8, 512, 256), BF16),
            vm((32, 64), BF16), vm((16, 2, 512), F32), vm((160, 128), F32),
            vm((2, 8, 128, 128), F32), vm((512, 128), F32), vm((512, 128), F32), vm((2, 512, 128), F32),
            dma((8, 15)), dma((8, 15)), dma((8, 3)), dma((2,)), dma((2,)),
            dma((15,)), dma((15,)), dma((15,)), dma((15,)), dma((15,)), dma((15,)), dma((15,)), dma((15,)),
            dma((5,)), dma((5,)), dma((8, 2)), dma((8, 2)), dma,
            dma((8, 2)), dma((4, 2, 2)), dma, dma((17,)),
        ],
        compiler_params=params(0, 63 * 2**20),
    )(*small, *matrices)


PART_ROWS = (16, 24, 24)
PART_BASE = (0, 128, 320)
ORDERS = (("xyz", "yzx", "zxy"), ("xyz", "yxz", "zyx"))
SLOTS = 3
JOBS = 8


def block_cut(order, phase, rows):
    axis, later = order[phase], order[phase + 1 :]
    if axis != "z" and "z" in later:
        return ("zl", slice(0, 1), slice(1, 2))
    if "y" in later:
        return ("y", slice(0, 2), slice(2, 4))
    if "x" in later:
        return ("x", slice(0, 2), slice(2, 4))
    cut = (rows // 8 + 1) // 2 * 8
    return ("r", slice(0, cut), slice(cut, rows))


def block_dims(order, part, phase):
    later = order[phase + 1 :]
    return {
        "zl": 2 if "z" in later else 1,
        "y": 4 if "y" in later else 1,
        "x": 4 if "x" in later else 1,
        "zh": 2 if "z" in later else 1,
        "r": PART_ROWS[part],
    }


def recv_plan():
    for kind in range(2):
        for p in range(3):
            for ph in range(3):
                if kind == 0 or (p > 0 and ph == 1):
                    yield kind, p, ph, 4 if ph < 2 else 3


def recv_shapes():
    shapes = []
    for kind, p, ph, count in recv_plan():
        order = ORDERS[kind][p]
        name, one, two = block_cut(order, ph, PART_ROWS[p])
        for k in range(count):
            d = dict(block_dims(order, p, ph))
            if ph < 2 and k < 2:
                cut = (one, two)[k]
                d[name] = cut.stop - cut.start
            shapes.append((SLOTS, d["zl"], d["y"], d["x"], d["zh"], d["r"], 256))
    return shapes


def backward_kernel(*refs):
    names = [
        "msg_all", "slots_all", "cond_all", "emb", "ada", "loss", "cond_w", "x_in", "w_i", "wo_i",
        "h1_i", "h2_i", "h3_i", "hb_i", "ot_i", "att_i", "x1_i", "mlp_i", "x2_i", "f_i", "u_i", "dl_i",
        "out", "norm", "bias_sum", "gtable", "gcond", "wb", "dl", "u", "fb", "hh", "hT", "oT", "dm",
        "otp", "da", "acc", "got", "xa", "xb", "dx", "hb", "doh", "dov", "dkv", "dsrc", "dr", "dq6",
        "kcol", "dmod", "biasp", "smsg", "sgot", "smine", "sall", "spart", "sback", "gst", "gcs",
        "tile", "tiles",
    ]
    names += ["g%d" % i for i in range(3 * SLOTS)] + ["st0", "st1", "st2"]
    n = len(names)
    r = dict(zip(names, refs[:n]))
    rest = list(refs[n:])
    recv = {}
    for kind, p, ph, count in recv_plan():
        recv[kind, p, ph] = rest[:count]
        rest = rest[count:]
    (
        ls, fs, ps, pr, hs, hr, hl, as_, ar, js, jr, gss, grs, ol, credit,
        s1, r1, s2, r2, s3, r3, ns, nr, gl,
    ) = rest
    msg_all, slots_all, ada, biasp, dmod = r["msg_all"], r["slots_all"], r["ada"], r["biasp"], r["dmod"]
    dl, u, hT, oT, acc, got = r["dl"], r["u"], r["hT"], r["oT"], r["acc"], r["got"]
    dx, xa, xb, wb, hh = r["dx"], r["xa"], r["xb"], r["wb"], r["hh"]
    dm, otp, da, tile = r["dm"], r["otp"], r["da"], r["tile"]
    parts = [[r["g%d" % (s * 3 + p)] for p in range(3)] for s in range(SLOTS)]
    stage_out = [r["st0"], r["st1"], r["st2"]]
    out = r["out"]

    x, y, z, c = place()
    dp = lax.axis_index("dp")
    sq = lax.axis_index("seq")
    zl, zh = lax.rem(z, 2), z // 2
    base = dp - c
    owner = lax.rem(sq, 2)
    pair = sq // 2
    mate = at(x, y, z, 1 - c)
    row = [lax.rem(dp + i, 16) for i in range(1, 16)]
    line = [lax.rem(sq + i, 8) for i in range(1, 8)]
    greet([(d, sq) for d in row] + group_peers()[1:] + [at(x, y, z + 2 * zl - 1, c)])
    here = {"x": x, "y": y, "z": z}

    def step(axis, by):
        q = dict(here)
        q[axis] = q[axis] + by
        return at(q["x"], q["y"], q["z"], c)

    def load(k, src, dst):
        cp = pltpu.make_async_copy(src, dst, ls.at[k])
        cp.start()
        return cp

    loads = {
        "h3": load(0, r["h3_i"], hh),
        "dl": load(1, r["dl_i"], dl),
        "w3": load(2, r["w_i"].at[:, :, 3], wb),
        "x2": load(3, r["x2_i"], xa),
        "mlp": load(4, r["mlp_i"], xb),
        "u": load(5, r["u_i"], u),
        "hb": load(6, r["hb_i"], r["hb"]),
        "ot": load(8, r["ot_i"], otp.at[c]),
    }

    def view(ref, order, p, ph, index, half=None):
        sel = {}
        for i, a in enumerate(order):
            sel[a] = here[a] if i < ph else (lax.rem(index + 4, 4) if i == ph else None)
        idx = {
            "zl": slice(0, 2) if sel["z"] is None else pl.ds(lax.rem(sel["z"], 2), 1),
            "y": slice(0, 4) if sel["y"] is None else pl.ds(sel["y"], 1),
            "x": slice(0, 4) if sel["x"] is None else pl.ds(sel["x"], 1),
            "zh": slice(0, 2) if sel["z"] is None else pl.ds(sel["z"] // 2, 1),
            "r": slice(0, PART_ROWS[p]),
        }
        if half is not None:
            name, one, two = block_cut(order, ph, PART_ROWS[p])
            idx[name] = (one, two)[half]
        return ref.at[idx["zl"], idx["y"], idx["x"], idx["zh"], idx["r"]]

    def add(dst, srcs):
        d0, d1, d2, d3 = dst.shape[:4]

        def body(i, carry):
            a, b = i // d1, lax.rem(i, d1)
            for cc in range(d2):
                for d in range(d3):
                    val = dst[a, b, cc, d]
                    for s in srcs:
                        val = val + s[a, b, cc, d]
                    dst[a, b, cc, d] = val
            return carry

        if d0 * d1 == 1:
            body(0, 0)
        else:
            lax.fori_loop(0, d0 * d1, body, 0)

    neighbours = [step(a, b) for a in "xyz" for b in (1, -1)]
    unsent = []

    def phases(j, slot, again, reused):
        mine = []
        kind = j % 2
        if again:
            pl.semaphore_wait(credit.at[slot], 6)

        def go(p, ph, k, src, dst, device):
            cp = remote(src, dst, js.at[j, p * 3 + ph, k], jr.at[j, p * 3 + ph, k], device)
            cp.start()
            mine.append(cp)

        def arrived(p, ph, k, ref):
            remote(ref, ref, js.at[j, p * 3 + ph, k], jr.at[j, p * 3 + ph, k], mate).wait_recv()

        for ph in range(3):
            info = []
            for p in range(3):
                order = ORDERS[kind][p]
                a = order[ph]
                buffers = recv.get((kind, p, ph), recv[0, p, ph])
                bufs = [b.at[slot] for b in buffers]
                info.append((p, a, here[a], functools.partial(view, parts[slot][p], order, p, ph), bufs))
            if ph == 2:
                for p, a, i, g, bufs in info:
                    for k, by in enumerate((1, -1, 2)):
                        go(p, ph, k, g(i + by), bufs[k], step(a, by))
                yield
                for p, a, i, g, bufs in info:
                    for k in range(3):
                        arrived(p, ph, k, bufs[k])
                    add(g(i), bufs)
                break
            for p, a, i, g, bufs in info:
                go(p, ph, 0, g(i + 2, 0), bufs[0], step(a, 1))
                go(p, ph, 1, g(i + 2, 1), bufs[1], step(a, -1))
            yield
            for p, a, i, g, bufs in info:
                arrived(p, ph, 0, bufs[0])
                add(g(i + 1, 0), [bufs[0]])
                go(p, ph, 2, g(i + 1), bufs[2], step(a, 1))
                arrived(p, ph, 1, bufs[1])
                add(g(i - 1, 1), [bufs[1]])
                go(p, ph, 3, g(i - 1), bufs[3], step(a, -1))
            yield
            for p, a, i, g, bufs in info:
                arrived(p, ph, 2, bufs[2])
                arrived(p, ph, 3, bufs[3])
                add(g(i), [bufs[2], bufs[3]])
        for p in range(3):
            val = parts[slot][p][zl, y, x, zh]
            stage_out[p][j] = val
            square = val * val
            total = tile[...]
            for t in range(PART_ROWS[p] // 8):
                for k in range(2):
                    total = total + square[8 * t : 8 * t + 8, 128 * k : 128 * k + 128]
            tile[...] = total
        for cp in mine:
            cp.wait_send()
        if reused():
            for device in neighbours:
                pl.semaphore_signal(credit.at[slot], inc=1, device_id=device, device_id_type=MESH)

    def tail(j):
        kind, half = JOB_KIND[j // 2], j % 2
        o = out.at[kind]

        def rows_of(p, xi, zi, count):
            n_rows = PART_ROWS[p]
            start = half * 512 + PART_BASE[p] + (lax.rem(xi + 4, 4) * 2 + zi) * n_rows
            return pl.ds(pl.multiple_of(start, 8), count * n_rows)

        def go(p, k, src, rows, device):
            cp = remote(src, o.at[rows], gss.at[j, p, k], grs.at[j, p, k], device)
            cp.start()
            unsent.append(cp)

        def arrived(p, k, rows):
            remote(o.at[rows], o.at[rows], gss.at[j, p, k], grs.at[j, p, k], mate).wait_recv()

        own = []
        for p in range(3):
            rows = rows_of(p, x, zh, 1)
            cp = pltpu.make_async_copy(stage_out[p].at[j], o.at[rows], ol.at[j, p])
            cp.start()
            own.append(cp)
            go(p, 0, stage_out[p].at[j], rows, step("z", 2))
        yield
        for p in range(3):
            own[p].wait()
            arrived(p, 0, rows_of(p, x, 1 - zh, 1))
            both = rows_of(p, x, 0, 2)
            go(p, 1, o.at[both], both, step("x", 1))
            go(p, 2, o.at[both], both, step("x", -1))
        yield
        for p in range(3):
            arrived(p, 1, rows_of(p, x - 1, 0, 2))
            arrived(p, 2, rows_of(p, x + 1, 0, 2))
            left, right = rows_of(p, x - 1, 0, 1), rows_of(p, x + 1, 1, 1)
            go(p, 3, o.at[left], left, step("x", 1))
            go(p, 4, o.at[right], right, step("x", -1))
        yield
        for p in range(3):
            arrived(p, 3, rows_of(p, x + 2, 0, 1))
            arrived(p, 4, rows_of(p, x + 2, 1, 1))

    JOB_KIND = (3, 2, 1, 0)

    def transpose_into(dst, src):
        def body(i, carry):
            cols = pl.ds(pl.multiple_of(i * 128, 128), 128)
            dst[cols, :] = jnp.transpose(src[:, :, cols].reshape(512, 128))
            return carry
        lax.fori_loop(0, 8, body, 0)

    def store_part(slot, a, b, val):
        for p in range(3):
            n_rows = PART_ROWS[p]
            for xi in range(4):
                for zi in range(2):
                    start = PART_BASE[p] + (xi * 2 + zi) * n_rows
                    parts[slot][p][a, b, xi, zi] = val[start : start + n_rows]

    prepared = set()

    def prepare(kind):
        if kind in prepared:
            return
        prepared.add(kind)
        if kind == 3:
            transpose_into(hT, hh)
        if kind == 2:
            transpose_into(hT, dm)
        if kind == 1:
            loads["h2"].wait()
            transpose_into(hT, hh)
            loads["h1"] = load(0, r["h1_i"], hh)
        if kind == 0:
            loads["h1"].wait()
            transpose_into(hT, hh)

    def fill(j, slot):
        kind, half = JOB_KIND[j // 2], j % 2
        prepare(kind)
        rows = pl.ds(half * 512, 512)
        right = {3: dl, 2: u, 1: dl}

        def body(i, carry):
            g = right[kind][i] if kind else r["dq6"][i]
            store_part(slot, i // 4, lax.rem(i, 4), jnp.dot(hT[rows, :], g, preferred_element_type=F32))
            return carry

        lax.fori_loop(0, 8 if kind else 6, body, 0)
        if kind == 0:
            for jj in range(2):
                cols = pl.ds(pl.multiple_of((2 * jj + c) * 256, 256), 256)
                g = da[:, :, cols].reshape(512, 256)
                store_part(slot, 1, 2 + jj, jnp.dot(oT[rows, :], g, preferred_element_type=F32))

    queue = list(range(JOBS))
    running = []
    tails = []
    free = list(range(SLOTS))
    ready = {3}
    used = set()

    steps_done = {}

    def launch():
        if not (queue and free and JOB_KIND[queue[0] // 2] in ready):
            return
        if running and steps_done[running[-1][1]] < 1:
            return
        j = queue.pop(0)
        slot = free.pop(0)
        fill(j, slot)
        gen = phases(j, slot, slot in used, lambda: len(queue) > len(free))
        used.add(slot)
        next(gen)
        steps_done[j] = 0
        running.append((gen, j, slot))

    def service(count=1):
        for _ in range(count):
            old = list(tails)
            for entry in list(running):
                gen, j, slot = entry
                try:
                    next(gen)
                    steps_done[j] += 1
                except StopIteration:
                    running[:] = [e for e in running if e is not entry]
                    free.append(slot)
                    t = tail(j)
                    next(t)
                    tails.append(t)
            launch()
            for gen in old:
                try:
                    next(gen)
                except StopIteration:
                    tails.remove(gen)

    tile[...] = jnp.zeros((8, 128), F32)
    biasp[...] = jnp.zeros((160, 128), F32)
    dmod[...] = jnp.zeros((2, 8, 1024), F32)
    loads["h3"].wait()
    loads["dl"].wait()
    launch()
    loads["h2"] = load(0, r["h2_i"], hh)

    def store_bias(start, val):
        for i in range(val.shape[1] // 128):
            biasp[pl.ds(start + i, 1), :] = val[:, 128 * i : 128 * i + 128]

    def blocks(fn):
        for img in range(2):
            def body(i, carry, img=img):
                fn(img, pl.ds(pl.multiple_of(img * 128 + i * 32, 32), 32))
                return carry
            lax.fori_loop(0, 4, body, 0)

    def exchange(k, ref):
        cp = remote(ref.at[c], ref.at[c], ps.at[k], pr.at[k], mate)
        cp.start()
        return cp

    def swap(k):
        cp = remote(acc.at[1 - c], got, ps.at[k], pr.at[k], mate)
        cp.start()
        return cp

    def back_rows(grad, count):
        def body(i, carry):
            for half in range(2):
                part = lax.dot_general(
                    grad[i, 256 * half : 256 * half + 256, :], wb[i // 4, lax.rem(i, 4)], NT,
                    preferred_element_type=F32,
                )

                @pl.when(i == 0)
                def _():
                    acc[half] = part

                @pl.when(i > 0)
                def _():
                    acc[half] += part

            return carry
        lax.fori_loop(0, count, body, 0)

    def norm_back(img, v, scale, shift, dy):
        center = v - jnp.mean(v, -1, keepdims=True)
        inv = lax.rsqrt(jnp.mean(center * center, -1, keepdims=True) + NORM_EPS)
        unit = center * inv
        dmod[img, scale : scale + 1, :] += jnp.sum(dy * unit, axis=0, keepdims=True)
        dmod[img, shift : shift + 1, :] += jnp.sum(dy, axis=0, keepdims=True)
        dn = dy * (1.0 + ada_row(ada, scale, img))
        return inv * (
            dn - jnp.mean(dn, -1, keepdims=True) - unit * jnp.mean(dn * unit, -1, keepdims=True)
        )

    loads["w3"].wait()
    back_rows(dl, 8)
    cp = swap(0)
    w_next = load(2, r["w_i"].at[:, :, 2], wb)

    def head_bias(i, carry):
        store_bias(128 + (2 * i + c) * 2, jnp.sum(dl[i].astype(F32), axis=0, keepdims=True))
        return carry

    lax.fori_loop(0, 8, head_bias, 0)
    service()
    loads["x2"].wait()
    loads["mlp"].wait()
    cp.wait()
    fc2_rows = jnp.zeros((1, 1024), F32)

    def do_x2(img, rows):
        grad = norm_back(img, xa[rows, :], 6, 7, acc[c, rows, :] + got[rows, :])
        dx[rows, :] = grad
        dmod[img, 1:2, :] += jnp.sum(grad * xb[rows, :], axis=0, keepdims=True)
        low = (ada_row(ada, 1, img) * grad).astype(BF16)
        dm[c, rows, :] = low
        r["gst"][0, 0:1, :] += jnp.sum(low.astype(F32), axis=0, keepdims=True)

    r["gst"][0, 0:1, :] = fc2_rows
    blocks(do_x2)
    cp = exchange(1, dm)
    store_bias(120, r["gst"][0, 0:1, :])
    loads["x1"] = load(3, r["x1_i"], xa)
    loads["att"] = load(4, r["att_i"], xb)
    cp.wait()
    loads["u"].wait()
    ready.add(2)
    service()
    w_next.wait()

    fb = r["fb"]

    def f_load(i):
        return pltpu.make_async_copy(r["f_i"].at[i], fb.at[lax.rem(i, 2)], fs.at[lax.rem(i, 2)])

    f_load(0).start()

    def do_df(i, carry):
        @pl.when(i < 7)
        def _():
            f_load(i + 1).start()

        du = jnp.dot(dm[...].reshape(512, 1024), wb[i // 4, lax.rem(i, 4)], preferred_element_type=F32)
        f_load(i).wait()
        v = fb[lax.rem(i, 2)]
        k0 = 0.7978845608028654
        th = jnp.tanh(k0 * (v + 0.044715 * (v * v * v)))
        slope = 0.5 * (1.0 + th) + 0.5 * v * (1.0 - th * th) * (k0 * (1.0 + 3.0 * 0.044715 * (v * v)))
        df = (slope * du).astype(BF16)
        dl[i] = df
        store_bias(88 + (2 * i + c) * 2, jnp.sum(df.astype(F32), axis=0, keepdims=True))
        return carry

    while 1 in queue:
        service()
    lax.fori_loop(0, 8, do_df, 0)
    ready.add(1)
    w_next = load(2, r["w_i"].at[:, :, 1], wb)
    service()
    w_next.wait()
    back_rows(dl, 8)
    cp = swap(2)
    w_next = load(2, r["wo_i"], wb.at[0])
    loads["x1"].wait()
    loads["att"].wait()
    loads["ot"].wait()
    ot_swap = exchange(3, otp)
    service()
    cp.wait()

    def do_x1(img, rows):
        grad = norm_back(img, xa[rows, :], 3, 5, acc[c, rows, :] + got[rows, :]) + dx[rows, :]
        dmod[img, 0:1, :] += jnp.sum(grad * xb[rows, :], axis=0, keepdims=True)
        low = (ada_row(ada, 0, img) * grad).astype(BF16)
        da[c, rows, :] = low
        r["gst"][0, 0:1, :] += jnp.sum(low.astype(F32), axis=0, keepdims=True)

    r["gst"][0, 0:1, :] = fc2_rows
    blocks(do_x1)
    da_swap = exchange(4, da)
    store_bias(80, r["gst"][0, 0:1, :])
    w_next.wait()
    dov, doh, hb = r["dov"], r["doh"], r["hb"]
    for img in range(2):
        rows = pl.ds(128 * img, 128)
        low = jnp.zeros((128, 1024), F32)
        for k in range(4):
            low += lax.dot_general(
                da[c, rows, 256 * k : 256 * k + 256], wb[0, k], NT, preferred_element_type=F32
            )
        dov[img] = low.astype(BF16)
    w_next = load(2, r["w_i"].at[:, :, 0], wb)

    def do_sends(fn, img):
        for p in range(4):
            for q in range(2):
                src = dov.at[img, :, pl.ds(((p // 2 * 2 + q) * 2 + p % 2) * 128, 128)]
                cp = remote(
                    src, doh.at[sq, img], hs.at[p, q, img], hr.at[sq, img], (base + q, p * 2 + c)
                )

                @pl.when(jnp.logical_not(jnp.logical_and(sq == p * 2 + c, c == q)))
                def _():
                    fn(cp)

    for img in range(2):
        do_sends(lambda cp: cp.start(), img)

    @pl.when(owner == c)
    def _():
        doh[sq] = dov[:, :, head_lanes(pair, c)]

    kcol = r["kcol"]
    for img in range(2):
        for g in range(8):
            kcol[img, g] = column_of(slots_all[g * 2 + owner, pl.ds(img, 1), :])
    service()
    ot_swap.wait()
    transpose_into(oT, otp)

    loads["hb"].wait()
    dkv, dsrc, dr, dq6 = r["dkv"], r["dsrc"], r["dr"], r["dq6"]
    low_lanes = lax.broadcasted_iota(jnp.int32, (256, 128), 1) < 64
    low_rows = lax.broadcasted_iota(jnp.int32, (128, 256), 0) < 64

    sends = []
    for img in range(2):
        for i in range(8):
            landed = doh.at[i, img]

            @pl.when(jnp.logical_or(sq != i, owner != c))
            def _():
                remote(landed, landed, hs.at[0, 0, img], hr.at[i, img], mate).wait_recv()

        dkv[...] = jnp.zeros((2, 1024, 128), F32)

        def attend_block(qb, carry, img=img):
            q = jnp.concatenate([hb[2 * qb, 0, img], hb[2 * qb + 1, 0, img]], axis=0)
            k = jnp.concatenate([hb[g, 1, img] for g in range(8)], axis=0)
            v = jnp.concatenate([hb[g, 2, img] for g in range(8)], axis=0)
            do = jnp.concatenate([doh[2 * qb, img], doh[2 * qb + 1, img]], axis=0)
            kT = jnp.transpose(k)
            key = jnp.concatenate([kcol[img, g] for g in range(8)], axis=0)[:, 0:1]
            query = jnp.concatenate(
                [slots_all[(2 * qb + i) * 2 + owner, 2 + img : 3 + img, :] for i in range(2)], axis=1
            )
            seen_by = key <= query
            heads = []
            for h in range(2):
                mask = low_lanes if h == 0 else jnp.logical_not(low_lanes)
                qh = jnp.where(mask, q, jnp.zeros_like(q))
                doh_h = jnp.where(mask, do, jnp.zeros_like(do))
                sc = lax.dot_general(k, qh, NT, preferred_element_type=F32) * SCORE_SCALE
                sc = jnp.where(seen_by, sc, -1e30)
                e = jnp.exp(sc - jnp.max(sc, axis=0, keepdims=True))
                p = e / jnp.sum(e, axis=0, keepdims=True)
                dpr = lax.dot_general(v, doh_h, NT, preferred_element_type=F32)
                inner = jnp.sum(p * dpr, axis=0, keepdims=True)
                ds = (p * (dpr - inner)).astype(BF16)
                dkv[0] += jnp.dot(ds, qh, preferred_element_type=F32)
                dkv[1] += jnp.dot(p.astype(BF16), doh_h, preferred_element_type=F32)
                heads.append(jnp.dot(kT, ds, preferred_element_type=F32))
            dq = jnp.transpose(jnp.where(low_rows, heads[0], heads[1]) * SCORE_SCALE).astype(BF16)
            dsrc[2 * qb, 0, img] = dq[:128]
            dsrc[2 * qb + 1, 0, img] = dq[128:]
            return carry

        lax.fori_loop(0, 4, attend_block, 0)
        for g in range(8):
            dsrc[g, 1, img] = (dkv[0, 128 * g : 128 * g + 128] * SCORE_SCALE).astype(BF16)
            dsrc[g, 2, img] = dkv[1, 128 * g : 128 * g + 128].astype(BF16)
        for i, to in enumerate(line):
            cp = remote(
                dsrc.at[to, :, img], dr.at[sq, :, img], as_.at[i, img], ar.at[i, img], (dp, to)
            )
            cp.start()
            sends.append(cp)
        if img == 0:
            service()
    dr[sq] = dsrc[sq]
    service(1)
    if queue and queue[0] >= 6:
        prepare(0)
    for cp in sends:
        cp.wait()
    for t in range(3):
        for jj in range(2):
            for half in range(2):
                for ip in range(2):
                    dq6[t * 2 + jj, ip * 256 : ip * 256 + 256, half * 128 : half * 128 + 128] = dr[
                        (jj * 2 + half) * 2 + ip, t
                    ].reshape(256, 128)
    da_swap.wait()
    for jj in range(2):
        for start, t in ((64, 0), (72, 2)):
            store_bias(
                start + (2 * jj + c) * 2,
                jnp.sum(dq6[t * 2 + jj].astype(F32), axis=0, keepdims=True),
            )
    w_next.wait()
    back_rows(dq6, 6)
    cp = swap(5)
    ready.add(0)
    service()
    cp.wait()

    def do_x0(img, rows):
        norm_back(img, r["x_in"][rows, :].astype(F32), 2, 4, acc[c, rows, :] + got[rows, :])

    blocks(do_x0)
    for img in range(2):
        do_sends(lambda cp: cp.wait_send(), img)

    smsg, sgot, smine = r["smsg"], r["sgot"], r["smine"]
    sall, spart, sback = r["sall"], r["spart"], r["sback"]
    for k in range(8):
        both = dmod[0, k : k + 1, :] + dmod[1, k : k + 1, :]
        for i in range(8):
            biasp[8 * k + i : 8 * k + i + 1, :] = both[:, 128 * i : 128 * i + 128]
    for d in range(16):
        for img in range(2):
            for i in range(4):
                lo = (d % 2) * 512 + i * 128
                smsg[d, img * 4 + i : img * 4 + i + 1, :] = dmod[img, d // 2 : d // 2 + 1, lo : lo + 128]
        smsg[d, 8:18, :] = biasp[10 * d : 10 * d + 10, :]
        smsg[d, 18:24, :] = jnp.broadcast_to(r["loss"][0:1, :], (6, 128))
    cps = []
    for i, d in enumerate(row):
        cp = remote(smsg.at[d], sgot.at[dp], s1.at[i], r1.at[i], (d, sq))
        cp.start()
        cps.append(cp)
    sgot[dp] = smsg[dp]
    service()
    for cp in cps:
        cp.wait()
    for d in range(16):
        smine[d] = sgot[d, 0:8, :]
    for i in range(2):
        smine[16 + i] = sum(sgot[d, 8 + 8 * i : 16 + 8 * i, :] for d in range(16))
    cps = []
    for i, s in enumerate(line):
        cp = remote(smine, sall.at[sq], s2.at[i], r2.at[i], (dp, s))
        cp.start()
        cps.append(cp)
    sall[sq] = smine[...]
    service()
    for cp in cps:
        cp.wait()
    for k in range(18):
        smine[k] = sum(sall[s, k] for s in range(8))
    r["bias_sum"][0] = smine[16]
    r["bias_sum"][1] = smine[17]
    dada = jnp.concatenate(
        [
            jnp.concatenate([smine[d, 4 * i + k : 4 * i + k + 1, :] for k in range(4)], axis=1)
            for d in range(16)
            for i in range(2)
        ],
        axis=0,
    )

    def dcond_part(d, carry):
        rows = pl.ds(pl.multiple_of(64 * d, 64), 64)
        spart[d] = lax.dot_general(
            dada, r["cond_w"][rows, :].astype(F32), NT, precision=HIGH, preferred_element_type=F32
        )
        return carry

    lax.fori_loop(0, 16, dcond_part, 0)
    cps = []
    for i, d in enumerate(row):
        cp = remote(spart.at[d], sback.at[dp], s3.at[i], r3.at[i], (d, sq))
        cp.start()
        cps.append(cp)
    sback[dp] = spart[dp]
    service()
    squares = jnp.zeros((8, 128), F32)

    def fold(val):
        total = jnp.zeros((8, 128), F32)
        for i in range(val.shape[0] // 8):
            for k in range(val.shape[1] // 128):
                total = total + val[8 * i : 8 * i + 8, 128 * k : 128 * k + 128]
        return total

    gcs = r["gcs"]

    def gcond_copy(d):
        slot = lax.rem(d, 2)
        rows = pl.ds(pl.multiple_of(64 * d, 64), 64)
        return pltpu.make_async_copy(gcs.at[slot], r["gcond"].at[rows], gl.at[slot])

    def gcond_part(d, total):
        @pl.when(d > 1)
        def _():
            gcond_copy(d - 2).wait()

        val = lax.dot_general(
            r["cond_all"][d].astype(F32), dada, (((0,), (0,)), ((), ())),
            precision=HIGH, preferred_element_type=F32,
        )
        gcs[lax.rem(d, 2)] = val
        gcond_copy(d).start()
        return total + fold(val * val)

    squares = squares + lax.fori_loop(0, 16, gcond_part, squares)
    gcond_copy(14).wait()
    gcond_copy(15).wait()
    for cp in cps:
        cp.wait()
    dcond = sum(sback[d] for d in range(16))
    emb = r["emb"][...]
    sig = 1.0 / (1.0 + jnp.exp(-emb))
    demb = dcond * (sig * (1.0 + emb * (1.0 - sig)))
    labels = jnp.concatenate(
        [msg_all[d, 10:11, i : i + 1] for d in range(16) for i in range(2)], axis=0
    ).astype(jnp.int32)
    hit = jnp.where(lax.broadcasted_iota(jnp.int32, (32, 1000), 1) == labels, 1.0, 0.0)
    gtable = jnp.dot(jnp.transpose(demb), hit, precision=HIGH, preferred_element_type=F32)
    r["gtable"][...] = gtable
    table_squares = jnp.sum(jnp.sum(gtable * gtable, axis=1, keepdims=True), axis=0, keepdims=True)
    bias_rows = jnp.concatenate([smine[16], smine[17][0:2]], axis=0)
    bias_squares = jnp.sum(jnp.sum(bias_rows * bias_rows, axis=1, keepdims=True), axis=0, keepdims=True)
    spot = jnp.logical_and(
        lax.broadcasted_iota(jnp.int32, (8, 128), 0) == 0, lax.broadcasted_iota(jnp.int32, (8, 128), 1) == 0
    )
    squares = squares + jnp.where(spot, table_squares + bias_squares, 0.0)
    while queue or running:
        service()
    tile[...] += squares * 0.125
    tiles = r["tiles"]
    cps = []
    for i, d in enumerate(row):
        cp = remote(tile, tiles.at[i], ns.at[i], nr.at[i], (d, sq))
        cp.start()
        cps.append(cp)
    for cp in cps:
        cp.wait()
    tile[...] += sum(tiles[i] for i in range(15))
    cps = []
    for i, d in enumerate(line):
        cp = remote(tile, tiles.at[15 + i], ns.at[15 + i], nr.at[15 + i], (dp, d))
        cp.start()
        cps.append(cp)
    service()
    for cp in cps:
        cp.wait()
    total = tile[...] + sum(tiles[15 + i] for i in range(7))
    total = jnp.sum(jnp.sum(total, axis=1, keepdims=True), axis=0, keepdims=True)
    r["norm"][...] = jnp.broadcast_to(total, (8, 128))
    while tails:
        service()
    for cp in unsent:
        cp.wait_send()


def backward_pass(small, kept):
    dma = pltpu.SemaphoreType.DMA
    sd = jax.ShapeDtypeStruct
    vm = pltpu.VMEM
    scratch = [
        vm((2, 4, 1024, 256), BF16),
        vm((8, 512, 256), BF16), vm((8, 512, 256), BF16), vm((2, 512, 256), F32),
        vm((2, 256, 1024), BF16), vm((1024, 512), BF16), vm((1024, 512), BF16),
        vm((2, 256, 1024), BF16), vm((2, 256, 1024), BF16), vm((2, 256, 1024), BF16),
        vm((2, 256, 1024), F32), vm((256, 1024), F32), vm((256, 1024), F32), vm((256, 1024), F32),
        vm((256, 1024), F32),
        vm((8, 3, 2, 128, 128), BF16), vm((8, 2, 128, 128), BF16), vm((2, 128, 1024), BF16),
        vm((2, 1024, 128), F32), vm((8, 3, 2, 128, 128), BF16), vm((8, 3, 2, 128, 128), BF16),
        vm((6, 512, 256), BF16), vm((2, 8, 128, 128), F32), vm((2, 8, 1024), F32), vm((160, 128), F32),
        vm((16, 24, 128), F32), vm((16, 24, 128), F32), vm((18, 8, 128), F32), vm((8, 18, 8, 128), F32),
        vm((16, 32, 64), F32), vm((16, 32, 64), F32), vm((1, 8, 1024), F32),
        vm((2, 64, 512), F32),
        vm((8, 128), F32), vm((22, 8, 128), F32),
    ]
    for _ in range(SLOTS):
        for p in range(3):
            scratch.append(vm((2, 4, 4, 2, PART_ROWS[p], 256), F32))
    for p in range(3):
        scratch.append(vm((JOBS, PART_ROWS[p], 256), F32))
    scratch += [vm(shape, F32) for shape in recv_shapes()]
    scratch += [
        dma((9,)), dma((2,)), dma((6,)), dma((6,)), dma((4, 2, 2)), dma((8, 2)), dma, dma((7, 2)), dma((7, 2)),
        dma((JOBS, 9, 4)), dma((JOBS, 9, 4)), dma((JOBS, 3, 5)), dma((JOBS, 3, 5)), dma((JOBS, 3)),
        pltpu.SemaphoreType.REGULAR((SLOTS,)),
        dma((15,)), dma((15,)), dma((7,)), dma((7,)), dma((15,)), dma((15,)), dma((22,)), dma((22,)),
        dma((2,)),
    ]
    return pl.pallas_call(
        backward_kernel,
        out_shape=[
            sd((4, 1024, 256), F32), sd((8, 128), F32), sd((2, 8, 128), F32),
            sd((64, 1000), F32), sd((1024, 512), F32),
        ],
        in_specs=[VM] * len(small) + [ANY] * len(kept),
        out_specs=[ANY, VM, VM, VM, ANY],
        scratch_shapes=scratch,
        compiler_params=params(1, 64 * 2**20 - 2**17),
    )(*small, *kept)


def adamw(weight, first, second, grad, factor):
    clipped = grad * factor
    first_new = BETA_ONE * first + (1.0 - BETA_ONE) * clipped
    second_new = BETA_TWO * second + (1.0 - BETA_TWO) * clipped * clipped
    first_hat = first_new / (1.0 - BETA_ONE**STEP)
    second_hat = second_new / (1.0 - BETA_TWO**STEP)
    weight_new = weight - LEARN * (first_hat / (jnp.sqrt(second_hat) + ADAM_EPS) + DECAY * weight)
    return (weight_new, first_new, second_new)


def local(
    x_in, scale_ids, pad_mask, loss_weights, targets, labels,
    cond_w, attn_w, mlp_w, head_w, class_table, biases,
    first_cond, first_attn, first_mlp, first_head, first_table, first_bias,
    second_cond, second_attn, second_mlp, second_head, second_table, second_bias,
):

    x_rows = x_in.reshape(256, 1024)
    small = (labels.reshape(1, 2), biases.reshape(10, 128), scale_ids, pad_mask, loss_weights, targets)
    (
        msg_all, slots_all, cond_all, embedded, ada, loss_tile, wb_cond,
        w, wo, h1, h2, h3, heads, o, att, x1, mlp, x2, f, u, dlogits,
    ) = forward_pass(small + (class_table.T, cond_w, x_rows), (attn_w, mlp_w, head_w))
    true_count = loss_tile[7, 0]
    summed, squares, bias_sum, grad_table, grad_cond = backward_pass(
        (msg_all, slots_all, cond_all, embedded, ada, loss_tile, wb_cond, x_rows),
        (w, wo, h1, h2, h3, heads, o, att, x1, mlp, x2, f, u, dlogits),
    )
    bias_sum = bias_sum.reshape(16, 128)
    loss_total = bias_sum[10, 0]
    grad_bias = bias_sum[:10].reshape(1280)
    grad_norm = jnp.sqrt(squares[0, 0])
    factor = jnp.minimum(1.0, CLIP / grad_norm)
    grads = (grad_cond, summed[0], summed[1:3], summed[3], grad_table, grad_bias)
    weights = (cond_w, attn_w, mlp_w, head_w, class_table.T, biases)
    firsts = (first_cond, first_attn, first_mlp, first_head, first_table.T, first_bias)
    seconds = (second_cond, second_attn, second_mlp, second_head, second_table.T, second_bias)
    results = [
        adamw(weight, first, second, grad, factor)
        for weight, first, second, grad in zip(weights, firsts, seconds, grads)
    ]
    new_weights = [entry[0] for entry in results]
    new_first = [entry[1] for entry in results]
    new_second = [entry[2] for entry in results]
    copies = [weight.astype(BF16) for weight in new_weights]
    for group in (new_weights, new_first, new_second, copies):
        group[4] = group[4].T
    return tuple(new_weights + new_first + new_second + copies + [grad_norm, loss_total, true_count])


def solution(mesh):
    split = (P(None, "dp"), P(None, "dp"), P(None, None, "dp"), P(None, "dp"), P(None, "dp"), P("dp"))
    in_specs = (P("dp", "seq", None),) + (P("dp", "seq"),) * 4 + (P("dp"),) + split * 3
    out_specs = split * 4 + (P(), P(), P())
    return jax.shard_map(local, mesh=mesh, in_specs=in_specs, out_specs=out_specs, check_vma=False)
```
